256 devices in a mesh: lon: 32 (over y_lo, z, core), lat: 8 (over x, y_hi).
Axes of the slice: x: 4, y: 4 (y_hi: 2, y_lo: 2; y = y_hi * 2 + y_lo), z: 8, core: 2. Of those that a mesh axis runs over, the one named last changes fastest.
Arguments:
- features: bfloat16 [2, 16, 4096, 256], P(None, 'lat', 'lon'), may hold values from -6 to 6
- out_grad: bfloat16 [2, 16, 4096, 256], P(None, 'lat', 'lon'), may hold values from -8 to 8
- first_kernel: bfloat16 [3, 3, 256, 256], replicated, may hold values from -0.125 to 0.125
- second_kernel: bfloat16 [3, 3, 256, 256], replicated, may hold values from -0.125 to 0.125
- strides: int32 [2, 16, 3], replicated, may hold values from 1 to 16, as said below
Outputs:
- input_grad: bfloat16 [2, 16, 4096, 256], P(None, 'lat', 'lon')
- first_grad: float32 [3, 3, 256, 256], replicated
- second_grad: float32 [3, 3, 256, 256], replicated
The draws below stay inside these ranges and needn't reach their ends.
Inputs may be any that keep to these rules, and one draw needn't show every extreme that they name: strides[s, p, k] is 16 where the source row of p and k is the polar row; with d the source row's distance from the pole it is otherwise within one of (16 + d) // (2 d + 1) and below 16.
All inputs are finite; a program needn't handle non-finite values.
Results may differ from the reference program's by a relative error of at most 0.0033.
Values may be sent and summed in bfloat16 or wider, within the bound.
No kernel may reach another device: no remote copies, remote signals or barrier semaphores. Data moves between devices by JAX's collectives and lax.ppermute only.
A program may use at most 64 MiB of HBM per device.

```python
import math
import jax
import jax.numpy as jnp
from jax import lax

CH = 256
POLE = 16
SPAN = 16
COLS = 4096
CELLS = 131072


def draw_out_grad(key, part):
    first_key, second_key = jax.random.split(key, 2)
    base_values = jax.random.normal(first_key, (2, POLE, COLS, CH), jnp.float32)
    col_scale = jnp.exp(jax.random.uniform(second_key, (1, 1, COLS, 1), jnp.float32, 0.0, 1.0) * math.log(10.0)) / 3.0
    return jnp.clip(base_values * col_scale, -8.0, 8.0).astype(jnp.bfloat16)


def draw_strides(key, part):
    row_ids = jnp.arange(POLE, dtype=jnp.int32)
    source_rows = jnp.stack([jnp.maximum(row_ids - 1, 0), row_ids, jnp.minimum(row_ids + 1, POLE - 1)], axis=1)
    distance = jnp.broadcast_to(source_rows[None], (2, POLE, 3)).astype(jnp.int32)
    base_stride = (SPAN + distance) // (2 * distance + 1)
    jitter = jax.random.randint(key, (2, POLE, 3), -1, 2, dtype=jnp.int32)
    moved = jnp.clip(base_stride + jitter, 1, SPAN - 1)
    return jnp.where(distance == 0, SPAN, moved).astype(jnp.int32)


def block_scale(stream_key, extent, shards, smallest, high):
    def one(position, blocks):
        heights = jax.random.uniform(jax.random.fold_in(jax.random.fold_in(stream_key, 6), position), (blocks,), jnp.float32, smallest / len(shards), high / len(shards))
        return jnp.repeat(jnp.exp(heights), extent[position] // blocks).reshape((-1,) + (1,) * (len(extent) - position - 1))

    factor_of = one(*shards[0])
    for cut in shards[1:]:
        factor_of = factor_of * one(*cut)
    return factor_of


def normal_values(stream_key, extent, scale, reach, cuts=(), kind=jnp.bfloat16):
    result = jax.random.normal(stream_key, extent, jnp.float32) * scale
    if len(cuts) > 0:
        result = block_scale(stream_key, extent, cuts, -0.22, 0.18) * result
    return jnp.clip(result, min=-reach, max=reach).astype(kind)


def setup_inputs(seed: int = 0) -> dict:
    key_of = jax.random.split(jax.random.key(seed), 6)
    features = normal_values(key_of[0], (2, POLE, COLS, CH), 1.0, 6.0, ((1, 8), (2, 32)))
    out_grad = draw_out_grad(jax.random.fold_in(key_of[5], 71), 0)
    first_kernel = normal_values(key_of[2], (3, 3, CH, CH), (9 * CH) ** -0.5, 0.125)
    second_kernel = normal_values(key_of[3], (3, 3, CH, CH), (9 * CH) ** -0.5, 0.125)
    strides = draw_strides(jax.random.fold_in(key_of[5], 71), 0)
    return {"features": features, "out_grad": out_grad, "first_kernel": first_kernel, "second_kernel": second_kernel, "strides": strides}


def fetch_row(field_in, row_index):
    return lax.dynamic_index_in_dim(field_in, row_index.astype(jnp.int32), 0, keepdims=False)

def source_info(out_row, kernel_row):
    if kernel_row == 0:
        return (jnp.maximum(out_row - 1, 0), out_row == 0, out_row < 0)
    if kernel_row == 1:
        return (out_row, out_row < 0, out_row < 0)
    return (jnp.minimum(out_row + 1, POLE - 1), out_row < 0, out_row == POLE - 1)

def tapped(field_in, strides, out_row, kernel_row, kernel_col):
    source_row, mirror, missing = source_info(out_row, kernel_row)
    stride_value = strides[out_row, kernel_row]
    offset = ((kernel_col - 1) * stride_value + jnp.where(mirror, COLS // 2, 0)).astype(jnp.int32)
    sliced = jnp.roll(fetch_row(field_in, source_row), -offset, axis=0)
    return jnp.where(missing, jnp.zeros_like(sliced), sliced)

def forward_row(field_in, kernel, strides, out_row):
    summed = jnp.zeros((COLS, CH), jnp.float32)
    for kernel_row in range(3):
        for kernel_col in range(3):
            sliced = tapped(field_in, strides, out_row, kernel_row, kernel_col)
            summed = summed + jnp.dot(sliced, kernel[kernel_row, kernel_col], preferred_element_type=jnp.float32)
    return summed

def slot_sum(grad_row, stride_value, mirror, missing, kernel_set):
    summed = jnp.zeros((COLS, CH), jnp.float32)
    for kernel_col in range(3):
        offset = ((kernel_col - 1) * stride_value + jnp.where(mirror, COLS // 2, 0)).astype(jnp.int32)
        sliced = jnp.roll(grad_row, offset, axis=0)
        summed = summed + jnp.dot(sliced, kernel_set[kernel_col].T, preferred_element_type=jnp.float32)
    return jnp.where(missing, jnp.zeros_like(summed), summed)

def adjoint_row(grad_in, kernel, strides, in_row):
    top_mirror = in_row == 0
    above_row = jnp.maximum(in_row - 1, 0)
    below_row = jnp.minimum(in_row + 1, POLE - 1)
    above_stride = jnp.where(top_mirror, strides[0, 0], strides[above_row, 2])
    below_stride = strides[below_row, 0]
    above_kernel = [jnp.where(top_mirror, kernel[0, kernel_col], kernel[2, kernel_col]) for kernel_col in range(3)]
    below_kernel = [kernel[0, kernel_col] for kernel_col in range(3)]
    centre_kernel = [kernel[1, kernel_col] for kernel_col in range(3)]
    centre = slot_sum(fetch_row(grad_in, in_row), strides[in_row, 1], in_row < 0, in_row < 0, centre_kernel)
    above = slot_sum(fetch_row(grad_in, above_row), above_stride, top_mirror, in_row < 0, above_kernel)
    below = slot_sum(fetch_row(grad_in, below_row), below_stride, in_row < 0, in_row == POLE - 1, below_kernel)
    return centre + above + below

def slab_grads(features, out_grad, first_kernel, second_kernel, strides):
    row_ids = jnp.arange(POLE, dtype=jnp.int32)

    def first_pass(in_row):
        pre_act = forward_row(features, first_kernel, strides, in_row)
        activated = jax.nn.gelu(pre_act).astype(jnp.bfloat16)
        act_grad = adjoint_row(out_grad, second_kernel, strides, in_row)
        _, pullback = jax.vjp(jax.nn.gelu, pre_act)
        pre_grad = pullback(act_grad)[0].astype(jnp.bfloat16)
        return (activated, pre_grad)
    activated, pre_grad = lax.map(first_pass, row_ids)

    def second_pass(in_row):
        summed = adjoint_row(pre_grad, first_kernel, strides, in_row)
        return (fetch_row(out_grad, in_row).astype(jnp.float32) + summed).astype(jnp.bfloat16)
    input_grad = lax.map(second_pass, row_ids)

    def weight_step(carry, out_row):
        first_sum, second_sum = carry
        first_terms = []
        second_terms = []
        pre_row = fetch_row(pre_grad, out_row)
        grad_row = fetch_row(out_grad, out_row)
        for kernel_row in range(3):
            for kernel_col in range(3):
                feature_tap = tapped(features, strides, out_row, kernel_row, kernel_col)
                act_tap = tapped(activated, strides, out_row, kernel_row, kernel_col)
                first_terms.append(jnp.dot(feature_tap.T, pre_row, preferred_element_type=jnp.float32))
                second_terms.append(jnp.dot(act_tap.T, grad_row, preferred_element_type=jnp.float32))
        first_sum = first_sum + jnp.stack(first_terms).reshape(3, 3, CH, CH)
        second_sum = second_sum + jnp.stack(second_terms).reshape(3, 3, CH, CH)
        return ((first_sum, second_sum), None)
    zero_grads = jnp.zeros((3, 3, CH, CH), jnp.float32)
    (first_sum, second_sum), _ = lax.scan(weight_step, (zero_grads, zero_grads), row_ids)
    return (input_grad, first_sum, second_sum)

def reference(features, out_grad, first_kernel, second_kernel, strides):
    grads_list = []
    first_total = jnp.zeros((3, 3, CH, CH), jnp.float32)
    second_total = jnp.zeros((3, 3, CH, CH), jnp.float32)
    for slab in range(2):
        input_part, first_sum, second_sum = slab_grads(features[slab], out_grad[slab], first_kernel, second_kernel, strides[slab])
        grads_list.append(input_part)
        first_total = first_total + first_sum
        second_total = second_total + second_sum
    grad_scale = 1.0 / math.sqrt(CELLS)
    return (jnp.stack(grads_list), first_total * grad_scale, second_total * grad_scale)
```

```python
import functools
import math

import jax
import jax.numpy as jnp
from jax import lax
from jax.experimental import pallas as pl
from jax.experimental.pallas import tpu as pltpu
from jax.sharding import Mesh
from jax.sharding import PartitionSpec as P

POLE = 16
SPAN = 16
ALL = ("yl", "z", "core", "x", "yh")
PLANE = ("x", "yh", "yl")
NN = (((1,), (0,)), ((), ()))
NT = (((1,), (1,)), ((), ()))
TN = (((0,), (0,)), ((), ()))
ROOT = math.sqrt(2.0 / math.pi)
CUBIC = 0.044715


def dot(a, b, dims):
    return lax.dot_general(a, b, dims, preferred_element_type=jnp.float32)


def fill(ext, field, own, down, cross, bottom, left, right, mirror):
    width = own.shape[2]
    for s in range(2):
        for row in range(4):
            place = ext.at[s * 4 + row]
            if row == 0:
                above, across = down[field, s].astype(jnp.float32), cross[field, s].astype(jnp.float32)
                middle = jnp.where(mirror, across, above)
            elif row == 3:
                middle = bottom[field, s].astype(jnp.float32)
            else:
                middle = own[s, row - 1].astype(jnp.float32)
            place[:SPAN] = left[field, s, row].astype(jnp.float32)
            place[SPAN : SPAN + width] = middle
            place[SPAN + width : 2 * SPAN + width] = right[field, s, row].astype(jnp.float32)


def tap(ext, s, row, shift, width):
    if isinstance(shift, int):
        return ext[s * 4 + row, SPAN + shift : SPAN + shift + width, :].astype(jnp.bfloat16)
    start = SPAN + shift
    rest = lax.rem(start, 8)
    span = ext[s * 4 + row, pl.ds(pl.multiple_of(start - rest, 8), width + 8), :]
    chans = span.shape[-1]
    turned = pltpu.roll(span.reshape(width // 8 + 1, 8, chans), lax.rem(8 - rest, 8), 1)
    lane = lax.broadcasted_iota(jnp.int32, (1, 8, chans), 1)
    moved = jnp.where(lane < 8 - rest, turned[:-1], turned[1:])
    return moved.reshape(width, chans).astype(jnp.bfloat16)


def adjoint_stride(strides, s, row, slot, lat):
    here = lat * 2 + row
    if slot == 0:
        if row == 1:
            return strides[s, lat * 2, 2]
        return jnp.where(lat == 0, strides[s, 0, 0], strides[s, jnp.maximum(here - 1, 0), 2])
    if slot == 1:
        return strides[s, here, 1]
    return strides[s, jnp.minimum(here + 1, POLE - 1), 0]


def adjoint_taps(ext, taps, strides, lat, width):
    for row in range(2):
        for s in range(2):
            at = (row * 2 + s) * width
            for slot in range(3):
                stride = adjoint_stride(strides, s, row, slot, lat)
                for col in range(3):
                    shift = 0 if col == 1 else -(col - 1) * stride
                    taps[slot * 3 + col, at : at + width] = tap(ext, s, row + slot, shift, width)


def adjoint_product(taps, kernel, mirror, row, half):
    total = None
    at = row * half
    for slot in range(3):
        for col in range(3):
            weight = kernel[2 - slot, col]
            if slot == 0 and row == 0:
                weight = jnp.where(mirror, kernel[0, col], weight)
            term = dot(taps[slot * 3 + col, at : at + half], weight, NT)
            total = term if total is None else total + term
    return total


def main_kernel(where, strides, feat, grad, down, cross, bottom, left, right, first_kernel, second_kernel,
                keep, send, pre_grad, ext_f, ext_g, taps_f, taps_g, act):
    lat, core = where[0], where[1]
    mirror = lat == 0
    width = feat.shape[2]
    half = 2 * width
    fill(ext_f, 0, feat, down, cross, bottom, left, right, mirror)
    for row in range(2):
        for s in range(2):
            at = (row * 2 + s) * width
            for k in range(3):
                stride = strides[s, lat * 2 + row, k]
                for col in range(3):
                    shift = 0 if col == 1 else (col - 1) * stride
                    taps_f[k * 3 + col, at : at + width] = tap(ext_f, s, row + k, shift, width)
    fill(ext_g, 1, grad, down, cross, bottom, left, right, mirror)
    adjoint_taps(ext_g, taps_g, strides, lat, width)

    for row in range(2):
        at = row * half
        pre = None
        for k in range(3):
            for col in range(3):
                term = dot(taps_f[k * 3 + col, at : at + half], first_kernel[k, col], NN)
                pre = term if pre is None else pre + term
        square = pre * pre
        bend = jnp.tanh(ROOT * (pre + CUBIC * (pre * square)))
        act[at : at + half] = (0.5 * pre * (1.0 + bend)).astype(jnp.bfloat16)
        slope = 0.5 * (1.0 + bend) + 0.5 * pre * (1.0 - bend * bend) * (ROOT * (1.0 + 3.0 * CUBIC * square))
        back = adjoint_product(taps_g, second_kernel, mirror, row, half)
        result = (back * slope).astype(jnp.bfloat16)
        for s in range(2):
            pre_grad[s, row] = result[s * width : (s + 1) * width]

    def place(value, k, col, owner):
        at = (k * 3 + col) * 256

        @pl.when(core == owner)
        def _():
            keep[at : at + 256] = value

        @pl.when(core != owner)
        def _():
            send[at : at + 256] = value.astype(jnp.bfloat16)

    activated = act[...]
    for col in range(3):
        edge = dot(activated[:half], taps_g[col, :half], TN)
        upper = dot(activated[half:], taps_g[col, half:], TN)
        lower = dot(activated, taps_g[6 + col], TN)
        place(dot(activated, taps_g[3 + col], TN), 1, col, 1)
        place(lower + jnp.where(mirror, edge, 0.0), 0, col, 1)
        place(upper + jnp.where(mirror, 0.0, edge), 2, col, 1)
    cells = [pre_grad[s, row] for row in range(2) for s in range(2)]
    pre_all = jnp.concatenate(cells, axis=0)
    for k in range(3):
        for col in range(3):
            place(dot(taps_f[k * 3 + col], pre_all, TN), k, col, 0)


def back_kernel(where, strides, grad, pre, down, cross, bottom, left, right, first_kernel, out, ext, taps):
    lat = where[0]
    mirror = lat == 0
    width = grad.shape[2]
    fill(ext, 0, pre, down, cross, bottom, left, right, mirror)
    adjoint_taps(ext, taps, strides, lat, width)
    for row in range(2):
        total = adjoint_product(taps, first_kernel, mirror, row, 2 * width)
        for s in range(2):
            own = grad[s, row].astype(jnp.float32)
            out[s, row] = (own + total[s * width : (s + 1) * width]).astype(jnp.bfloat16)


def halos(fields, lon_count, lat_count):
    n, _, _, width, _ = fields.shape
    at = lambda lon, lat: (lon % lon_count) * lat_count + lat
    lons = range(lon_count)
    down = lax.ppermute(fields[:, :, 1], ALL, [(at(i, k), at(i, k + 1)) for i in lons for k in range(lat_count - 1)])
    bottom = lax.ppermute(fields[:, :, 0], ALL, [(at(i, k + 1), at(i, k)) for i in lons for k in range(lat_count - 1)])
    cross = lax.ppermute(fields[:, :, 0], ALL, [(at(i, 0), at(i + lon_count // 2, 0)) for i in lons])
    lat = lax.axis_index(("x", "yh"))
    top = jnp.where(lat == 0, cross, down)

    def edge(cut):
        return jnp.concatenate([cut(top)[:, :, None], cut(fields), cut(bottom)[:, :, None]], axis=2)

    head = edge(lambda a: lax.slice_in_dim(a, 0, SPAN, axis=a.ndim - 2))
    tail = edge(lambda a: lax.slice_in_dim(a, width - SPAN, width, axis=a.ndim - 2))
    lats = range(lat_count)
    left = lax.ppermute(tail, ALL, [(at(i, k), at(i + 1, k)) for i in lons for k in lats])
    right = lax.ppermute(head, ALL, [(at(i + 1, k), at(i, k)) for i in lons for k in lats])
    return down, cross, bottom, left, right


def summed(keep, send):
    core = lax.axis_index("core")
    swap = [(0, 1), (1, 0)]
    total = keep + lax.ppermute(send, "core", swap).astype(jnp.float32)
    planes = lax.axis_size(PLANE)
    rows, cols = total.shape
    spread = lax.all_to_all(total.astype(jnp.bfloat16).reshape(planes, rows // planes, cols), PLANE, 0, 0, tiled=True)
    part = jnp.sum(spread.astype(jnp.float32), axis=0)
    count = lax.axis_size("z")
    reach = 1
    while reach < count:
        reach *= 2
        part = part + lax.ppermute(part, "z", [(i, i ^ (reach - 1)) for i in range(count)])
    part = part.astype(jnp.bfloat16)
    copies = jnp.broadcast_to(part[None], (planes,) + part.shape)
    mine = lax.all_to_all(copies, PLANE, 0, 0, tiled=True).reshape(rows, cols)
    other = lax.ppermute(mine, "core", swap)
    first = jnp.where(core == 0, mine, other).astype(jnp.float32)
    second = jnp.where(core == 0, other, mine).astype(jnp.float32)
    return first, second


def local(features, out_grad, first_kernel, second_kernel, strides):
    slabs, rows, width, chans = features.shape
    lat_axes, lon_axes = ("x", "yh"), ("yl", "z", "core")
    lat_count, lon_count = lax.axis_size(lat_axes), lax.axis_size(lon_axes)
    where = jnp.stack([lax.axis_index(lat_axes), lax.axis_index("core")]).astype(jnp.int32)
    smem = pl.BlockSpec(memory_space=pltpu.SMEM)
    vmem = pl.BlockSpec(memory_space=pltpu.VMEM)
    cells = slabs * rows * width
    ext = pltpu.VMEM((slabs * (rows + 2), width + 2 * SPAN + 8, chans), jnp.float32)
    taps = pltpu.VMEM((9, cells, chans), jnp.bfloat16)
    params = pltpu.CompilerParams(vmem_limit_bytes=48 * 1024 * 1024)
    grads = (9 * chans, chans)

    around = halos(jnp.stack([features, out_grad]), lon_count, lat_count)
    keep, send, pre_grad = pl.pallas_call(
        main_kernel,
        out_shape=[
            jax.ShapeDtypeStruct(grads, jnp.float32),
            jax.ShapeDtypeStruct(grads, jnp.bfloat16),
            jax.ShapeDtypeStruct(features.shape, jnp.bfloat16),
        ],
        in_specs=[smem, smem] + [vmem] * 9,
        out_specs=[vmem] * 3,
        scratch_shapes=[ext, ext, taps, taps, pltpu.VMEM((cells, chans), jnp.bfloat16)],
        compiler_params=params,
        name="main",
    )(where, strides, features, out_grad, *around, first_kernel, second_kernel)

    first, second = summed(keep, send)

    around = halos(pre_grad[None], lon_count, lat_count)
    input_grad = pl.pallas_call(
        back_kernel,
        out_shape=jax.ShapeDtypeStruct(features.shape, jnp.bfloat16),
        in_specs=[smem, smem] + [vmem] * 8,
        out_specs=vmem,
        scratch_shapes=[ext, taps],
        compiler_params=params,
        name="back",
    )(where, strides, out_grad, pre_grad, *around, first_kernel)

    scale = 1.0 / math.sqrt(cells * lat_count * lon_count)
    shape = first_kernel.shape
    return input_grad, (first * scale).reshape(shape), (second * scale).reshape(shape)


def solution(mesh):
    wide = Mesh(mesh.devices.reshape(2, 8, 2, 4, 2), ALL)
    field = P(None, ("x", "yh"), ("yl", "z", "core"), None)
    return jax.shard_map(
        local,
        mesh=wide,
        in_specs=(field, field, P(), P(), P()),
        out_specs=(field, P(), P()),
        check_vma=False,
    )
```

```python
import math

import jax
import jax.numpy as jnp
from jax import lax
from jax.experimental import pallas as pl
from jax.experimental.pallas import tpu as pltpu
from jax.sharding import Mesh
from jax.sharding import PartitionSpec as P

POLE = 16
SPAN = 16
ALL = ("yl", "z", "core", "x", "yh")
PLANE = ("x", "yh", "yl")
NN = (((1,), (0,)), ((), ()))
NT = (((1,), (1,)), ((), ()))
TN = (((0,), (0,)), ((), ()))
ROOT = math.sqrt(2.0 / math.pi)
CUBIC = 0.044715


def dot(a, b, dims):
    return lax.dot_general(a, b, dims, preferred_element_type=jnp.float32)


def fill(ext, field, own, halo, where):
    pair, next_pair, in_chip, next_chip = halo
    width = own.shape[2]
    odd, core = where[2] == 1, where[1] == 1
    for s in range(2):
        for row in range(4):
            place = ext.at[s * 4 + row]
            if row in (0, 3):
                one, other = pair[field, s].astype(jnp.float32), next_pair[field, s].astype(jnp.float32)
                middle = jnp.where(odd, one, other) if row == 0 else jnp.where(odd, other, one)
            else:
                middle = own[s, row - 1].astype(jnp.float32)
            near, far = in_chip[field, s, row].astype(jnp.float32), next_chip[field, s, row].astype(jnp.float32)
            place[:SPAN] = jnp.where(core, near, far)
            place[SPAN : SPAN + width] = middle
            place[SPAN + width : 2 * SPAN + width] = jnp.where(core, far, near)


def tap(ext, s, row, shift, width):
    if isinstance(shift, int):
        return ext[s * 4 + row, SPAN + shift : SPAN + shift + width, :].astype(jnp.bfloat16)
    start = SPAN + shift
    rest = lax.rem(start, 8)
    span = ext[s * 4 + row, pl.ds(pl.multiple_of(start - rest, 8), width + 8), :]
    chans = span.shape[-1]
    turned = pltpu.roll(span.reshape(width // 8 + 1, 8, chans), lax.rem(8 - rest, 8), 1)
    lane = lax.broadcasted_iota(jnp.int32, (1, 8, chans), 1)
    moved = jnp.where(lane < 8 - rest, turned[:-1], turned[1:])
    return moved.reshape(width, chans).astype(jnp.bfloat16)


def adjoint_stride(strides, s, row, slot, lat):
    here = lat * 2 + row
    if slot == 0:
        if row == 1:
            return strides[s, lat * 2, 2]
        return jnp.where(lat == 0, strides[s, 0, 0], strides[s, jnp.maximum(here - 1, 0), 2])
    if slot == 1:
        return strides[s, here, 1]
    return strides[s, jnp.minimum(here + 1, POLE - 1), 0]


def adjoint_taps(ext, taps, strides, lat, width):
    for row in range(2):
        for s in range(2):
            at = (row * 2 + s) * width
            for slot in range(3):
                stride = adjoint_stride(strides, s, row, slot, lat)
                for col in range(3):
                    shift = 0 if col == 1 else -(col - 1) * stride
                    taps[slot * 3 + col, at : at + width] = tap(ext, s, row + slot, shift, width)


def adjoint_product(taps, kernel, mirror, row, half):
    total = None
    at = row * half
    for slot in range(3):
        for col in range(3):
            weight = kernel[2 - slot, col]
            if slot == 0 and row == 0:
                weight = jnp.where(mirror, kernel[0, col], weight)
            term = dot(taps[slot * 3 + col, at : at + half], weight, NT)
            total = term if total is None else total + term
    return total


def main_kernel(where, strides, feat, grad, pair, next_pair, in_chip, next_chip, first_kernel, second_kernel,
                keep, send, pre_grad, ext_f, ext_g, taps_f, taps_g, act):
    lat, core = where[0], where[1]
    mirror = lat == 0
    width = feat.shape[2]
    half = 2 * width
    halo = (pair, next_pair, in_chip, next_chip)
    fill(ext_f, 0, feat, halo, where)
    for row in range(2):
        for s in range(2):
            at = (row * 2 + s) * width
            for k in range(3):
                stride = strides[s, lat * 2 + row, k]
                for col in range(3):
                    shift = 0 if col == 1 else (col - 1) * stride
                    taps_f[k * 3 + col, at : at + width] = tap(ext_f, s, row + k, shift, width)
    fill(ext_g, 1, grad, halo, where)
    adjoint_taps(ext_g, taps_g, strides, lat, width)

    for row in range(2):
        at = row * half
        pre = None
        for k in range(3):
            for col in range(3):
                term = dot(taps_f[k * 3 + col, at : at + half], first_kernel[k, col], NN)
                pre = term if pre is None else pre + term
        square = pre * pre
        bend = jnp.tanh(ROOT * (pre + CUBIC * (pre * square)))
        act[at : at + half] = (0.5 * pre * (1.0 + bend)).astype(jnp.bfloat16)
        slope = 0.5 * (1.0 + bend) + 0.5 * pre * (1.0 - bend * bend) * (ROOT * (1.0 + 3.0 * CUBIC * square))
        back = adjoint_product(taps_g, second_kernel, mirror, row, half)
        result = (back * slope).astype(jnp.bfloat16)
        for s in range(2):
            pre_grad[s, row] = result[s * width : (s + 1) * width]

    def place(value, k, col, owner):
        at = (k * 3 + col) * 256

        @pl.when(core == owner)
        def _():
            keep[at : at + 256] = value

        @pl.when(core != owner)
        def _():
            send[at : at + 256] = value.astype(jnp.bfloat16)

    activated = act[...]
    for col in range(3):
        edge = dot(activated[:half], taps_g[col, :half], TN)
        upper = dot(activated[half:], taps_g[col, half:], TN)
        lower = dot(activated, taps_g[6 + col], TN)
        place(dot(activated, taps_g[3 + col], TN), 1, col, 1)
        place(lower + jnp.where(mirror, edge, 0.0), 0, col, 1)
        place(upper + jnp.where(mirror, 0.0, edge), 2, col, 1)
    cells = [pre_grad[s, row] for row in range(2) for s in range(2)]
    pre_all = jnp.concatenate(cells, axis=0)
    for k in range(3):
        for col in range(3):
            place(dot(taps_f[k * 3 + col], pre_all, TN), k, col, 0)


def back_kernel(where, strides, grad, pre, pair, next_pair, in_chip, next_chip, first_kernel, out, ext, taps):
    lat = where[0]
    mirror = lat == 0
    width = grad.shape[2]
    fill(ext, 0, pre, (pair, next_pair, in_chip, next_chip), where)
    adjoint_taps(ext, taps, strides, lat, width)
    for row in range(2):
        total = adjoint_product(taps, first_kernel, mirror, row, 2 * width)
        for s in range(2):
            own = grad[s, row].astype(jnp.float32)
            out[s, row] = (own + total[s * width : (s + 1) * width]).astype(jnp.bfloat16)


def both_ways(pairs):
    return pairs + [(b, a) for a, b in pairs]


def row_halos(fields, lon_count, lat_count):
    at = lambda lon, lat: (lon % lon_count) * lat_count + lat
    lons = range(lon_count)
    odd = lax.rem(lax.axis_index(("x", "yh")), 2)
    row = lambda i: lax.dynamic_index_in_dim(fields, i, 2, keepdims=False)
    pair = lax.ppermute(row(1 - odd), ALL, both_ways([(at(i, k), at(i, k + 1)) for i in lons for k in range(0, lat_count, 2)]))
    between = both_ways([(at(i, k), at(i, k + 1)) for i in lons for k in range(1, lat_count - 1, 2)])
    across = [(at(i, 0), at(i + lon_count // 2, 0)) for i in lons]
    return pair, lax.ppermute(row(odd), ALL, between + across)


def column_halos(fields, pair, next_pair, lon_count, lat_count):
    width = fields.shape[3]
    at = lambda lon, lat: (lon % lon_count) * lat_count + lat
    odd, core = lax.rem(lax.axis_index(("x", "yh")), 2) == 1, lax.axis_index("core")

    def edge(start):
        cut = lambda a: lax.dynamic_slice_in_dim(a, start, SPAN, a.ndim - 2)
        one, other = cut(pair), cut(next_pair)
        top, bottom = jnp.where(odd, one, other), jnp.where(odd, other, one)
        return jnp.concatenate([top[:, :, None], cut(fields), bottom[:, :, None]], axis=2)

    reach = width - SPAN
    places = [(i, k) for i in range(0, lon_count, 2) for k in range(lat_count)]
    next_chip = lax.ppermute(edge(core * reach), ALL, both_ways([(at(i + 1, k), at(i + 2, k)) for i, k in places]))
    in_chip = lax.ppermute(edge((1 - core) * reach), "core", [(0, 1), (1, 0)])
    return in_chip, next_chip


def folded(count, cores, reach):
    pairs = []
    for i in range(count):
        for core in range(cores):
            turn = 2 * core
            base = (i + turn) % count
            partner = base ^ (reach - 1 if reach == count else reach // 2)
            pairs.append((i * cores + core, (partner - turn) % count * cores + core))
    return pairs


def local(features, out_grad, first_kernel, second_kernel, strides):
    slabs, rows, width, chans = features.shape
    lat_axes, lon_axes = ("x", "yh"), ("yl", "z", "core")
    lat_count, lon_count = lax.axis_size(lat_axes), lax.axis_size(lon_axes)
    lat, core = lax.axis_index(lat_axes), lax.axis_index("core")
    where = jnp.stack([lat, core, lax.rem(lat, 2)]).astype(jnp.int32)
    smem = pl.BlockSpec(memory_space=pltpu.SMEM)
    vmem = pl.BlockSpec(memory_space=pltpu.VMEM)
    cells = slabs * rows * width
    ext = pltpu.VMEM((slabs * (rows + 2), width + 2 * SPAN + 8, chans), jnp.float32)
    taps = pltpu.VMEM((9, cells, chans), jnp.bfloat16)
    params = pltpu.CompilerParams(vmem_limit_bytes=48 * 1024 * 1024)
    grads = (9 * chans, chans)
    swap = [(0, 1), (1, 0)]

    fields = jnp.stack([features, out_grad])
    around = row_halos(fields, lon_count, lat_count)
    around += column_halos(fields, *around, lon_count, lat_count)
    keep, send, pre_grad = pl.pallas_call(
        main_kernel,
        out_shape=[
            jax.ShapeDtypeStruct(grads, jnp.float32),
            jax.ShapeDtypeStruct(grads, jnp.bfloat16),
            jax.ShapeDtypeStruct(features.shape, jnp.bfloat16),
        ],
        in_specs=[smem, smem] + [vmem] * 8,
        out_specs=[vmem] * 3,
        scratch_shapes=[ext, ext, taps, taps, pltpu.VMEM((cells, chans), jnp.bfloat16)],
        compiler_params=params,
        name="main",
    )(where, strides, features, out_grad, *around, first_kernel, second_kernel)

    total = keep + lax.ppermute(send, "core", swap).astype(jnp.float32)
    planes, height, cores = lax.axis_size(PLANE), lax.axis_size("z"), lax.axis_size("core")
    total = total.astype(jnp.bfloat16).reshape(planes, 9 * chans // planes, chans)
    spread = lax.all_to_all(total, PLANE, 0, 0, tiled=True)

    pre_field = pre_grad[None]
    around = row_halos(pre_field, lon_count, lat_count)
    spread, around = lax.optimization_barrier((spread, around))
    around += column_halos(pre_field, *around, lon_count, lat_count)

    part = jnp.sum(spread.astype(jnp.float32), axis=0)
    reach = 2
    while reach <= height:
        part = part + lax.ppermute(part, ("z", "core"), folded(height, cores, reach))
        if reach == 2:
            part, around = lax.optimization_barrier((part, around))
            input_grad = pl.pallas_call(
                back_kernel,
                out_shape=jax.ShapeDtypeStruct(features.shape, jnp.bfloat16),
                in_specs=[smem, smem] + [vmem] * 7,
                out_specs=vmem,
                scratch_shapes=[ext, taps],
                compiler_params=params,
                name="back",
            )(where, strides, out_grad, pre_grad, *around, first_kernel)
        reach *= 2
    part, input_grad = lax.optimization_barrier((part.astype(jnp.bfloat16), input_grad))

    copies = jnp.broadcast_to(part[None], (planes,) + part.shape)
    mine = lax.all_to_all(copies, PLANE, 0, 0, tiled=True).reshape(grads)
    other = lax.ppermute(mine, "core", swap)
    scale = 1.0 / math.sqrt(cells * lat_count * lon_count)
    first = jnp.where(core == 0, mine, other).astype(jnp.float32) * scale
    second = jnp.where(core == 0, other, mine).astype(jnp.float32) * scale
    return input_grad, first.reshape(first_kernel.shape), second.reshape(first_kernel.shape)


def solution(mesh):
    wide = Mesh(mesh.devices.reshape(2, 8, 2, 4, 2), ALL)
    field = P(None, ("x", "yh"), ("yl", "z", "core"), None)
    return jax.shard_map(
        local,
        mesh=wide,
        in_specs=(field, field, P(), P(), P()),
        out_specs=(field, P(), P()),
        check_vma=False,
    )
```

```python
import math

import jax
import jax.numpy as jnp
from jax import lax
from jax.experimental import pallas as pl
from jax.experimental.pallas import tpu as pltpu
from jax.sharding import Mesh
from jax.sharding import PartitionSpec as P

POLE = 16
SPAN = 16
ALL = ("yl", "z", "core", "x", "yh")
PLANE = ("x", "yh", "yl")
NN = (((1,), (0,)), ((), ()))
NT = (((1,), (1,)), ((), ()))
TN = (((0,), (0,)), ((), ()))
ROOT = math.sqrt(2.0 / math.pi)
CUBIC = 0.044715


def dot(a, b, dims):
    return lax.dot_general(a, b, dims, preferred_element_type=jnp.float32)


def fill(ext, field, own, halo, where):
    pair, next_pair, in_chip, next_chip = halo
    width = own.shape[2]
    odd, core = where[2] == 1, where[1] == 1
    for s in range(2):
        for row in range(4):
            place = ext.at[s * 4 + row]
            if row in (0, 3):
                one, other = pair[field, s].astype(jnp.float32), next_pair[field, s].astype(jnp.float32)
                middle = jnp.where(odd, one, other) if row == 0 else jnp.where(odd, other, one)
            else:
                middle = own[s, row - 1].astype(jnp.float32)
            near, far = in_chip[field, s, row].astype(jnp.float32), next_chip[field, s, row].astype(jnp.float32)
            place[:SPAN] = jnp.where(core, near, far)
            place[SPAN : SPAN + width] = middle
            place[SPAN + width : 2 * SPAN + width] = jnp.where(core, far, near)


def tap(ext, s, row, shift, width):
    if isinstance(shift, int):
        return ext[s * 4 + row, SPAN + shift : SPAN + shift + width, :].astype(jnp.bfloat16)
    start = SPAN + shift
    rest = lax.rem(start, 8)
    span = ext[s * 4 + row, pl.ds(pl.multiple_of(start - rest, 8), width + 8), :]
    chans = span.shape[-1]
    turned = pltpu.roll(span.reshape(width // 8 + 1, 8, chans), lax.rem(8 - rest, 8), 1)
    lane = lax.broadcasted_iota(jnp.int32, (1, 8, chans), 1)
    moved = jnp.where(lane < 8 - rest, turned[:-1], turned[1:])
    return moved.reshape(width, chans).astype(jnp.bfloat16)


def adjoint_stride(strides, s, row, slot, lat):
    here = lat * 2 + row
    if slot == 0:
        if row == 1:
            return strides[s, lat * 2, 2]
        return jnp.where(lat == 0, strides[s, 0, 0], strides[s, jnp.maximum(here - 1, 0), 2])
    if slot == 1:
        return strides[s, here, 1]
    return strides[s, jnp.minimum(here + 1, POLE - 1), 0]


def adjoint_taps(ext, taps, strides, lat, width):
    for row in range(2):
        for s in range(2):
            at = (row * 2 + s) * width
            for slot in range(3):
                stride = adjoint_stride(strides, s, row, slot, lat)
                for col in range(3):
                    shift = 0 if col == 1 else -(col - 1) * stride
                    taps[slot * 3 + col, at : at + width] = tap(ext, s, row + slot, shift, width)


def adjoint_product(taps, kernel, mirror, row, half):
    total = None
    at = row * half
    for slot in range(3):
        for col in range(3):
            weight = kernel[2 - slot, col]
            if slot == 0 and row == 0:
                weight = jnp.where(mirror, kernel[0, col], weight)
            term = dot(taps[slot * 3 + col, at : at + half], weight, NT)
            total = term if total is None else total + term
    return total


def main_kernel(where, strides, feat, grad, pair, next_pair, in_chip, next_chip, first_kernel, second_kernel,
                keep, send, pre_grad, ext_f, ext_g, taps_f, taps_g, act, sums):
    lat, core = where[0], where[1]
    mirror = lat == 0
    width = feat.shape[2]
    half = 2 * width
    halo = (pair, next_pair, in_chip, next_chip)
    fill(ext_f, 0, feat, halo, where)
    for row in range(2):
        for s in range(2):
            at = (row * 2 + s) * width
            for k in range(3):
                stride = strides[s, lat * 2 + row, k]
                for col in range(3):
                    shift = 0 if col == 1 else (col - 1) * stride
                    taps_f[k * 3 + col, at : at + width] = tap(ext_f, s, row + k, shift, width)
    fill(ext_g, 1, grad, halo, where)
    adjoint_taps(ext_g, taps_g, strides, lat, width)

    for row in range(2):
        at = row * half
        pre = None
        for k in range(3):
            for col in range(3):
                term = dot(taps_f[k * 3 + col, at : at + half], first_kernel[k, col], NN)
                pre = term if pre is None else pre + term
        square = pre * pre
        bend = jnp.tanh(ROOT * (pre + CUBIC * (pre * square)))
        act[at : at + half] = (0.5 * pre * (1.0 + bend)).astype(jnp.bfloat16)
        slope = 0.5 * (1.0 + bend) + 0.5 * pre * (1.0 - bend * bend) * (ROOT * (1.0 + 3.0 * CUBIC * square))
        back = adjoint_product(taps_g, second_kernel, mirror, row, half)
        result = (back * slope).astype(jnp.bfloat16)
        for s in range(2):
            pre_grad[s, row] = result[s * width : (s + 1) * width]

    def place(value, k, col, owner):
        at = (k * 3 + col) * 256
        sums[jnp.where(core == owner, 0, 1), at : at + 256] = value

    turned = act[...].T
    for col in range(3):
        edge = dot(turned[:, :half], taps_g[col, :half], NN)
        upper = dot(turned[:, half:], taps_g[col, half:], NN)
        lower = dot(turned, taps_g[6 + col], NN)
        place(dot(turned, taps_g[3 + col], NN), 1, col, 1)
        place(lower + jnp.where(mirror, edge, 0.0), 0, col, 1)
        place(upper + jnp.where(mirror, 0.0, edge), 2, col, 1)
    pre_all = jnp.concatenate([pre_grad[s, row] for row in range(2) for s in range(2)], axis=0)
    for k in range(3):
        for col in range(3):
            place(dot(taps_f[k * 3 + col], pre_all, TN), k, col, 0)
    keep[...] = sums[0]
    send[...] = sums[1].astype(jnp.bfloat16)


def back_kernel(where, strides, grad, pre, pair, next_pair, in_chip, next_chip, first_kernel, out, ext, taps):
    lat = where[0]
    mirror = lat == 0
    width = grad.shape[2]
    fill(ext, 0, pre, (pair, next_pair, in_chip, next_chip), where)
    adjoint_taps(ext, taps, strides, lat, width)
    for row in range(2):
        total = adjoint_product(taps, first_kernel, mirror, row, 2 * width)
        for s in range(2):
            own = grad[s, row].astype(jnp.float32)
            out[s, row] = (own + total[s * width : (s + 1) * width]).astype(jnp.bfloat16)


def both_ways(pairs):
    return pairs + [(b, a) for a, b in pairs]


def row_halos(fields, lon_count, lat_count):
    at = lambda lon, lat: (lon % lon_count) * lat_count + lat
    lons = range(lon_count)
    odd = lax.rem(lax.axis_index(("x", "yh")), 2)
    row = lambda i: lax.dynamic_index_in_dim(fields, i, 2, keepdims=False)
    pair = lax.ppermute(row(1 - odd), ALL, both_ways([(at(i, k), at(i, k + 1)) for i in lons for k in range(0, lat_count, 2)]))
    between = both_ways([(at(i, k), at(i, k + 1)) for i in lons for k in range(1, lat_count - 1, 2)])
    across = [(at(i, 0), at(i + lon_count // 2, 0)) for i in lons]
    return pair, lax.ppermute(row(odd), ALL, between + across)


def column_halos(fields, pair, next_pair, lon_count, lat_count):
    width = fields.shape[3]
    at = lambda lon, lat: (lon % lon_count) * lat_count + lat
    odd, core = lax.rem(lax.axis_index(("x", "yh")), 2) == 1, lax.axis_index("core")

    def edge(start):
        cut = lambda a: lax.dynamic_slice_in_dim(a, start, SPAN, a.ndim - 2)
        one, other = cut(pair), cut(next_pair)
        top, bottom = jnp.where(odd, one, other), jnp.where(odd, other, one)
        return jnp.concatenate([top[:, :, None], cut(fields), bottom[:, :, None]], axis=2)

    reach = width - SPAN
    places = [(i, k) for i in range(0, lon_count, 2) for k in range(lat_count)]
    next_chip = lax.ppermute(edge(core * reach), ALL, both_ways([(at(i + 1, k), at(i + 2, k)) for i, k in places]))
    in_chip = lax.ppermute(edge((1 - core) * reach), "core", [(0, 1), (1, 0)])
    return in_chip, next_chip


def folded(count, cores, reach):
    pairs = []
    for i in range(count):
        for core in range(cores):
            turn = 2 * core
            base = (i + turn) % count
            partner = base ^ (reach - 1 if reach == count else reach // 2)
            pairs.append((i * cores + core, (partner - turn) % count * cores + core))
    return pairs


def local(features, out_grad, first_kernel, second_kernel, strides):
    slabs, rows, width, chans = features.shape
    lat_axes, lon_axes = ("x", "yh"), ("yl", "z", "core")
    lat_count, lon_count = lax.axis_size(lat_axes), lax.axis_size(lon_axes)
    lat, core = lax.axis_index(lat_axes), lax.axis_index("core")
    where = jnp.stack([lat, core, lax.rem(lat, 2)]).astype(jnp.int32)
    smem = pl.BlockSpec(memory_space=pltpu.SMEM)
    vmem = pl.BlockSpec(memory_space=pltpu.VMEM)
    cells = slabs * rows * width
    ext = pltpu.VMEM((slabs * (rows + 2), width + 2 * SPAN + 8, chans), jnp.float32)
    taps = pltpu.VMEM((9, cells, chans), jnp.bfloat16)
    params = pltpu.CompilerParams(vmem_limit_bytes=48 * 1024 * 1024)
    grads = (9 * chans, chans)
    swap = [(0, 1), (1, 0)]

    fields = jnp.stack([features, out_grad])
    around = row_halos(fields, lon_count, lat_count)
    around += column_halos(fields, *around, lon_count, lat_count)
    keep, send, pre_grad = pl.pallas_call(
        main_kernel,
        out_shape=[
            jax.ShapeDtypeStruct(grads, jnp.float32),
            jax.ShapeDtypeStruct(grads, jnp.bfloat16),
            jax.ShapeDtypeStruct(features.shape, jnp.bfloat16),
        ],
        in_specs=[smem, smem] + [vmem] * 8,
        out_specs=[vmem] * 3,
        scratch_shapes=[ext, ext, taps, taps, pltpu.VMEM((cells, chans), jnp.bfloat16), pltpu.VMEM((2,) + grads, jnp.float32)],
        compiler_params=params,
        name="main",
    )(where, strides, features, out_grad, *around, first_kernel, second_kernel)

    total = keep + lax.ppermute(send, "core", swap).astype(jnp.float32)
    planes, height, cores = lax.axis_size(PLANE), lax.axis_size("z"), lax.axis_size("core")
    total = total.astype(jnp.bfloat16).reshape(planes, 9 * chans // planes, chans)
    spread = lax.all_to_all(total, PLANE, 0, 0, tiled=True)

    spread, pre_grad = lax.optimization_barrier((spread, pre_grad))
    pre_field = pre_grad[None]
    pair, next_pair = row_halos(pre_field, lon_count, lat_count)
    part = jnp.sum(spread.astype(jnp.float32), axis=0)
    reach = 2
    while reach <= height:
        part = part + lax.ppermute(part, ("z", "core"), folded(height, cores, reach))
        reach *= 2
        if reach == height:
            part, pair = lax.optimization_barrier((part, pair))
    part, next_pair = lax.optimization_barrier((part.astype(jnp.bfloat16), next_pair))
    around = (pair, next_pair) + column_halos(pre_field, pair, next_pair, lon_count, lat_count)
    input_grad = pl.pallas_call(
        back_kernel,
        out_shape=jax.ShapeDtypeStruct(features.shape, jnp.bfloat16),
        in_specs=[smem, smem] + [vmem] * 7,
        out_specs=vmem,
        scratch_shapes=[ext, taps],
        compiler_params=params,
        name="back",
    )(where, strides, out_grad, pre_grad, *around, first_kernel)

    copies = jnp.broadcast_to(part[None], (planes,) + part.shape)
    mine = lax.all_to_all(copies, PLANE, 0, 0, tiled=True).reshape(grads)
    mine, input_grad = lax.optimization_barrier((mine, input_grad))
    other = lax.ppermute(mine, "core", swap)
    scale = 1.0 / math.sqrt(cells * lat_count * lon_count)
    first = jnp.where(core == 0, mine, other).astype(jnp.float32) * scale
    second = jnp.where(core == 0, other, mine).astype(jnp.float32) * scale
    return input_grad, first.reshape(first_kernel.shape), second.reshape(first_kernel.shape)


def solution(mesh):
    wide = Mesh(mesh.devices.reshape(2, 8, 2, 4, 2), ALL)
    field = P(None, ("x", "yh"), ("yl", "z", "core"), None)
    return jax.shard_map(
        local,
        mesh=wide,
        in_specs=(field, field, P(), P(), P()),
        out_specs=(field, P(), P()),
        check_vma=False,
    )
```

```python
import math

import jax
import jax.numpy as jnp
from jax import lax
from jax.experimental import pallas as pl
from jax.experimental.pallas import tpu as pltpu
from jax.sharding import Mesh
from jax.sharding import PartitionSpec as P

POLE = 16
SPAN = 16
ALL = ("yl", "z", "core", "x", "yh")
PLANE = ("x", "yh", "yl")
NN = (((1,), (0,)), ((), ()))
NT = (((1,), (1,)), ((), ()))
TN = (((0,), (0,)), ((), ()))
ROOT = math.sqrt(2.0 / math.pi)
CUBIC = 0.044715


def dot(a, b, dims):
    return lax.dot_general(a, b, dims, preferred_element_type=jnp.float32)


def fill(ext, field, own, halo, where):
    pair, next_pair, in_chip, next_chip = halo
    width = own.shape[2]
    odd, core = where[2] == 1, where[1] == 1
    for s in range(2):
        for row in range(4):
            place = ext.at[s * 4 + row]
            if row in (0, 3):
                one, other = pair[field, s].astype(jnp.float32), next_pair[field, s].astype(jnp.float32)
                middle = jnp.where(odd, one, other) if row == 0 else jnp.where(odd, other, one)
            else:
                middle = own[s, row - 1].astype(jnp.float32)
            near, far = in_chip[field, s, row].astype(jnp.float32), next_chip[field, s, row].astype(jnp.float32)
            place[:SPAN] = jnp.where(core, near, far)
            place[SPAN : SPAN + width] = middle
            place[SPAN + width : 2 * SPAN + width] = jnp.where(core, far, near)


def tap(ext, s, row, shift, width):
    if isinstance(shift, int):
        return ext[s * 4 + row, SPAN + shift : SPAN + shift + width, :].astype(jnp.bfloat16)
    start = SPAN + shift
    rest = lax.rem(start, 8)
    span = ext[s * 4 + row, pl.ds(pl.multiple_of(start - rest, 8), width + 8), :]
    chans = span.shape[-1]
    turned = pltpu.roll(span.reshape(width // 8 + 1, 8, chans), lax.rem(8 - rest, 8), 1)
    lane = lax.broadcasted_iota(jnp.int32, (1, 8, chans), 1)
    moved = jnp.where(lane < 8 - rest, turned[:-1], turned[1:])
    return moved.reshape(width, chans).astype(jnp.bfloat16)


def adjoint_stride(strides, s, row, slot, lat):
    here = lat * 2 + row
    if slot == 0:
        if row == 1:
            return strides[s, lat * 2, 2]
        return jnp.where(lat == 0, strides[s, 0, 0], strides[s, jnp.maximum(here - 1, 0), 2])
    if slot == 1:
        return strides[s, here, 1]
    return strides[s, jnp.minimum(here + 1, POLE - 1), 0]


def adjoint_taps(ext, taps, strides, lat, width):
    for row in range(2):
        for s in range(2):
            at = (row * 2 + s) * width
            for slot in range(3):
                stride = adjoint_stride(strides, s, row, slot, lat)
                for col in range(3):
                    shift = 0 if col == 1 else -(col - 1) * stride
                    taps[slot * 3 + col, at : at + width] = tap(ext, s, row + slot, shift, width)


def adjoint_product(taps, kernel, mirror, row, half):
    total = None
    at = row * half
    for slot in range(3):
        for col in range(3):
            weight = kernel[2 - slot, col]
            if slot == 0 and row == 0:
                weight = jnp.where(mirror, kernel[0, col], weight)
            term = dot(taps[slot * 3 + col, at : at + half], weight, NT)
            total = term if total is None else total + term
    return total


def main_kernel(where, strides, feat, grad, pair, next_pair, in_chip, next_chip, first_kernel, second_kernel,
                keep, send, pre_grad, ext_f, ext_g, taps_f, taps_g, act, sums, first_held, second_held, sems):
    lat, core = where[0], where[1]
    mirror = lat == 0
    width = feat.shape[2]
    half = 2 * width
    fetch_first = pltpu.make_async_copy(first_kernel, first_held, sems.at[0])
    fetch_second = pltpu.make_async_copy(second_kernel, second_held, sems.at[1])
    fetch_first.start()
    fetch_second.start()
    halo = (pair, next_pair, in_chip, next_chip)
    fill(ext_f, 0, feat, halo, where)
    for row in range(2):
        for s in range(2):
            at = (row * 2 + s) * width
            for k in range(3):
                stride = strides[s, lat * 2 + row, k]
                for col in range(3):
                    shift = 0 if col == 1 else (col - 1) * stride
                    taps_f[k * 3 + col, at : at + width] = tap(ext_f, s, row + k, shift, width)
    fill(ext_g, 1, grad, halo, where)
    adjoint_taps(ext_g, taps_g, strides, lat, width)
    fetch_first.wait()
    fetch_second.wait()

    for row in range(2):
        at = row * half
        pre = None
        for k in range(3):
            for col in range(3):
                term = dot(taps_f[k * 3 + col, at : at + half], first_held[k, col], NN)
                pre = term if pre is None else pre + term
        square = pre * pre
        bend = jnp.tanh(ROOT * (pre + CUBIC * (pre * square)))
        act[at : at + half] = (0.5 * pre * (1.0 + bend)).astype(jnp.bfloat16)
        slope = 0.5 * (1.0 + bend) + 0.5 * pre * (1.0 - bend * bend) * (ROOT * (1.0 + 3.0 * CUBIC * square))
        back = adjoint_product(taps_g, second_held, mirror, row, half)
        result = (back * slope).astype(jnp.bfloat16)
        for s in range(2):
            pre_grad[s, row] = result[s * width : (s + 1) * width]

    def place(value, k, col, owner):
        at = (k * 3 + col) * 256
        sums[jnp.where(core == owner, 0, 1), at : at + 256] = value

    turned = act[...].T
    for col in range(3):
        edge = dot(turned[:, :half], taps_g[col, :half], NN)
        upper = dot(turned[:, half:], taps_g[col, half:], NN)
        lower = dot(turned, taps_g[6 + col], NN)
        place(dot(turned, taps_g[3 + col], NN), 1, col, 1)
        place(lower + jnp.where(mirror, edge, 0.0), 0, col, 1)
        place(upper + jnp.where(mirror, 0.0, edge), 2, col, 1)
    pre_all = jnp.concatenate([pre_grad[s, row] for row in range(2) for s in range(2)], axis=0)
    for k in range(3):
        for col in range(3):
            place(dot(taps_f[k * 3 + col], pre_all, TN), k, col, 0)
    store = pltpu.make_async_copy(sums.at[0], keep, sems.at[2])
    store.start()
    send[...] = sums[1].astype(jnp.bfloat16)
    store.wait()


def back_kernel(where, strides, grad, pre, pair, next_pair, in_chip, next_chip, first_kernel, out, ext, taps):
    lat = where[0]
    mirror = lat == 0
    width = grad.shape[2]
    fill(ext, 0, pre, (pair, next_pair, in_chip, next_chip), where)
    adjoint_taps(ext, taps, strides, lat, width)
    for row in range(2):
        total = adjoint_product(taps, first_kernel, mirror, row, 2 * width)
        for s in range(2):
            own = grad[s, row].astype(jnp.float32)
            out[s, row] = (own + total[s * width : (s + 1) * width]).astype(jnp.bfloat16)


def part_kernel(scale, where, mine, other, first, second):
    own, swapped = mine[...].astype(jnp.float32) * scale, other[...].astype(jnp.float32) * scale
    keeps = where[1] == 0
    first[...] = jnp.where(keeps, own, swapped)
    second[...] = jnp.where(keeps, swapped, own)


def both_ways(pairs):
    return pairs + [(b, a) for a, b in pairs]


def row_halos(fields, lon_count, lat_count):
    at = lambda lon, lat: (lon % lon_count) * lat_count + lat
    lons = range(lon_count)
    odd = lax.rem(lax.axis_index(("x", "yh")), 2)
    row = lambda i: lax.dynamic_index_in_dim(fields, i, 2, keepdims=False)
    pair = lax.ppermute(row(1 - odd), ALL, both_ways([(at(i, k), at(i, k + 1)) for i in lons for k in range(0, lat_count, 2)]))
    between = both_ways([(at(i, k), at(i, k + 1)) for i in lons for k in range(1, lat_count - 1, 2)])
    across = [(at(i, 0), at(i + lon_count // 2, 0)) for i in lons]
    return pair, lax.ppermute(row(odd), ALL, between + across)


def column_halos(fields, pair, next_pair, lon_count, lat_count):
    width = fields.shape[3]
    at = lambda lon, lat: (lon % lon_count) * lat_count + lat
    odd, core = lax.rem(lax.axis_index(("x", "yh")), 2) == 1, lax.axis_index("core")

    def edge(start):
        cut = lambda a: lax.dynamic_slice_in_dim(a, start, SPAN, a.ndim - 2)
        one, other = cut(pair), cut(next_pair)
        top, bottom = jnp.where(odd, one, other), jnp.where(odd, other, one)
        return jnp.concatenate([top[:, :, None], cut(fields), bottom[:, :, None]], axis=2)

    reach = width - SPAN
    places = [(i, k) for i in range(0, lon_count, 2) for k in range(lat_count)]
    next_chip = lax.ppermute(edge(core * reach), ALL, both_ways([(at(i + 1, k), at(i + 2, k)) for i, k in places]))
    in_chip = lax.ppermute(edge((1 - core) * reach), "core", [(0, 1), (1, 0)])
    return in_chip, next_chip


def folded(count, cores, reach):
    pairs = []
    for i in range(count):
        for core in range(cores):
            turn = 2 * core
            base = (i + turn) % count
            partner = base ^ (reach - 1 if reach == count else reach // 2)
            pairs.append((i * cores + core, (partner - turn) % count * cores + core))
    return pairs


def local(features, out_grad, first_kernel, second_kernel, strides):
    slabs, rows, width, chans = features.shape
    lat_axes, lon_axes = ("x", "yh"), ("yl", "z", "core")
    lat_count, lon_count = lax.axis_size(lat_axes), lax.axis_size(lon_axes)
    lat, core = lax.axis_index(lat_axes), lax.axis_index("core")
    where = jnp.stack([lat, core, lax.rem(lat, 2)]).astype(jnp.int32)
    smem = pl.BlockSpec(memory_space=pltpu.SMEM)
    vmem = pl.BlockSpec(memory_space=pltpu.VMEM)
    anywhere = pl.BlockSpec(memory_space=pl.ANY)
    cells = slabs * rows * width
    ext = pltpu.VMEM((slabs * (rows + 2), width + 2 * SPAN + 8, chans), jnp.float32)
    taps = pltpu.VMEM((9, cells, chans), jnp.bfloat16)
    params = pltpu.CompilerParams(vmem_limit_bytes=48 * 1024 * 1024)
    grads = (9 * chans, chans)
    swap = [(0, 1), (1, 0)]

    fields = jnp.stack([features, out_grad])
    around = row_halos(fields, lon_count, lat_count)
    around += column_halos(fields, *around, lon_count, lat_count)
    keep, send, pre_grad = pl.pallas_call(
        main_kernel,
        out_shape=[
            jax.ShapeDtypeStruct(grads, jnp.float32),
            jax.ShapeDtypeStruct(grads, jnp.bfloat16),
            jax.ShapeDtypeStruct(features.shape, jnp.bfloat16),
        ],
        in_specs=[smem, smem] + [vmem] * 6 + [anywhere] * 2,
        out_specs=[anywhere, vmem, vmem],
        scratch_shapes=[
            ext,
            ext,
            taps,
            taps,
            pltpu.VMEM((cells, chans), jnp.bfloat16),
            pltpu.VMEM((2,) + grads, jnp.float32),
            pltpu.VMEM(first_kernel.shape, jnp.bfloat16),
            pltpu.VMEM(first_kernel.shape, jnp.bfloat16),
            pltpu.SemaphoreType.DMA((3,)),
        ],
        compiler_params=params,
        name="main",
    )(where, strides, features, out_grad, *around, first_kernel, second_kernel)

    total = keep + lax.ppermute(send, "core", swap).astype(jnp.float32)
    planes, height, cores = lax.axis_size(PLANE), lax.axis_size("z"), lax.axis_size("core")
    total = total.astype(jnp.bfloat16).reshape(planes, 9 * chans // planes, chans)
    spread = lax.all_to_all(total, PLANE, 0, 0, tiled=True)

    pre_field = pre_grad[None]
    around = row_halos(pre_field, lon_count, lat_count)
    spread, around = lax.optimization_barrier((spread, around))
    part = jnp.sum(spread.astype(jnp.float32), axis=0)
    reach = 2
    while reach <= height:
        part = part + lax.ppermute(part, ("z", "core"), folded(height, cores, reach))
        if reach == height // 2:
            part, pre_field = lax.optimization_barrier((part, pre_field))
        reach *= 2
    around += column_halos(pre_field, *around, lon_count, lat_count)
    input_grad = pl.pallas_call(
        back_kernel,
        out_shape=jax.ShapeDtypeStruct(features.shape, jnp.bfloat16),
        in_specs=[smem, smem] + [vmem] * 7,
        out_specs=vmem,
        scratch_shapes=[ext, taps],
        compiler_params=params,
        name="back",
    )(where, strides, out_grad, pre_grad, *around, first_kernel)

    copies = jnp.broadcast_to(part.astype(jnp.bfloat16)[None], (planes,) + part.shape)
    mine = lax.all_to_all(copies, PLANE, 0, 0, tiled=True).reshape(grads)
    mine, input_grad = lax.optimization_barrier((mine, input_grad))
    other = lax.ppermute(mine, "core", swap)
    scale = 1.0 / math.sqrt(cells * lat_count * lon_count)
    block = pl.BlockSpec((9 * chans // 4, chans), lambda i: (i, 0))
    first, second = pl.pallas_call(
        lambda *refs: part_kernel(scale, *refs),
        grid=(4,),
        out_shape=[jax.ShapeDtypeStruct(grads, jnp.float32)] * 2,
        in_specs=[smem, block, block],
        out_specs=[block, block],
        compiler_params=params,
        name="part",
    )(where, mine, other)
    return input_grad, first.reshape(first_kernel.shape), second.reshape(first_kernel.shape)


def solution(mesh):
    wide = Mesh(mesh.devices.reshape(2, 8, 2, 4, 2), ALL)
    field = P(None, ("x", "yh"), ("yl", "z", "core"), None)
    return jax.shard_map(
        local,
        mesh=wide,
        in_specs=(field, field, P(), P(), P()),
        out_specs=(field, P(), P()),
        check_vma=False,
    )
```

```python
import math

import jax
import jax.numpy as jnp
from jax import lax
from jax.experimental import pallas as pl
from jax.experimental.pallas import tpu as pltpu
from jax.sharding import Mesh
from jax.sharding import PartitionSpec as P

POLE = 16
SPAN = 16
ALL = ("yl", "z", "core", "x", "yh")
PLANE = ("x", "yh", "yl")
NN = (((1,), (0,)), ((), ()))
NT = (((1,), (1,)), ((), ()))
TN = (((0,), (0,)), ((), ()))
ROOT = math.sqrt(2.0 / math.pi)
CUBIC = 0.044715


def dot(a, b, dims):
    return lax.dot_general(a, b, dims, preferred_element_type=jnp.float32)


def fill(ext, field, own, halo, where):
    pair, next_pair, in_chip, next_chip = halo
    width = own.shape[2]
    odd, core = where[2] == 1, where[1] == 1
    for s in range(2):
        for row in range(4):
            place = ext.at[s * 4 + row]
            if row in (0, 3):
                one, other = pair[field, s].astype(jnp.float32), next_pair[field, s].astype(jnp.float32)
                middle = jnp.where(odd, one, other) if row == 0 else jnp.where(odd, other, one)
            else:
                middle = own[s, row - 1].astype(jnp.float32)
            near, far = in_chip[field, s, row].astype(jnp.float32), next_chip[field, s, row].astype(jnp.float32)
            place[:SPAN] = jnp.where(core, near, far)
            place[SPAN : SPAN + width] = middle
            place[SPAN + width : 2 * SPAN + width] = jnp.where(core, far, near)


def tap(ext, s, row, shift, width):
    if isinstance(shift, int):
        return ext[s * 4 + row, SPAN + shift : SPAN + shift + width, :].astype(jnp.bfloat16)
    start = SPAN + shift
    rest = lax.rem(start, 8)
    span = ext[s * 4 + row, pl.ds(pl.multiple_of(start - rest, 8), width + 8), :]
    chans = span.shape[-1]
    turned = pltpu.roll(span.reshape(width // 8 + 1, 8, chans), lax.rem(8 - rest, 8), 1)
    lane = lax.broadcasted_iota(jnp.int32, (1, 8, chans), 1)
    moved = jnp.where(lane < 8 - rest, turned[:-1], turned[1:])
    return moved.reshape(width, chans).astype(jnp.bfloat16)


def adjoint_stride(strides, s, row, slot, lat):
    here = lat * 2 + row
    if slot == 0:
        if row == 1:
            return strides[s, lat * 2, 2]
        return jnp.where(lat == 0, strides[s, 0, 0], strides[s, jnp.maximum(here - 1, 0), 2])
    if slot == 1:
        return strides[s, here, 1]
    return strides[s, jnp.minimum(here + 1, POLE - 1), 0]


def adjoint_taps(ext, taps, strides, lat, width):
    for row in range(2):
        for s in range(2):
            at = (row * 2 + s) * width
            for slot in range(3):
                stride = adjoint_stride(strides, s, row, slot, lat)
                for col in range(3):
                    shift = 0 if col == 1 else -(col - 1) * stride
                    taps[slot * 3 + col, at : at + width] = tap(ext, s, row + slot, shift, width)


def adjoint_product(taps, kernel, mirror, row, half):
    total = None
    at = row * half
    for slot in range(3):
        for col in range(3):
            weight = kernel[2 - slot, col]
            if slot == 0 and row == 0:
                weight = jnp.where(mirror, kernel[0, col], weight)
            term = dot(taps[slot * 3 + col, at : at + half], weight, NT)
            total = term if total is None else total + term
    return total


OWN = ((0, 1), (0, 2), (1, 0), (1, 1))


def stretch(place, middle, near, far, core):
    width = middle.shape[0]
    near, far = near.astype(jnp.float32), far.astype(jnp.float32)
    place[:SPAN] = jnp.where(core, near, far)
    place[SPAN : SPAN + width] = middle.astype(jnp.float32)
    place[SPAN + width : 2 * SPAN + width] = jnp.where(core, far, near)


def moved(ext, at, shift, width):
    return tap(ext, at // 4, at % 4, shift, width)


def early_kernel(where, strides, feat, grad, in_chip, next_chip, first_kernel, second_kernel,
                 taps_f, taps_g, pre_part, back_part, ext_f, ext_g):
    lat, core = where[0], where[1] == 1
    width = feat.shape[2]
    half = 2 * width
    for field, own, ext in ((0, feat, ext_f), (1, grad, ext_g)):
        for s in range(2):
            for row in range(2):
                stretch(ext.at[s * 2 + row], own[s, row], in_chip[field, s, row], next_chip[field, s, row], core)
    for i, (row, k) in enumerate(OWN):
        for s in range(2):
            ahead, behind = strides[s, lat * 2 + row, k], adjoint_stride(strides, s, row, k, lat)
            at, cells = s * 2 + row + k - 1, slice(s * width, (s + 1) * width)
            for col in range(3):
                taps_f[i * 3 + col, cells] = moved(ext_f, at, 0 if col == 1 else (col - 1) * ahead, width)
                taps_g[i * 3 + col, cells] = moved(ext_g, at, 0 if col == 1 else (1 - col) * behind, width)
    for row in range(2):
        pre, back = None, None
        for i, (at, k) in enumerate(OWN):
            if at != row:
                continue
            for col in range(3):
                term = dot(taps_f[i * 3 + col], first_kernel[k, col], NN)
                pre = term if pre is None else pre + term
                term = dot(taps_g[i * 3 + col], second_kernel[2 - k, col], NT)
                back = term if back is None else back + term
        pre_part[row * half : (row + 1) * half] = pre
        back_part[row * half : (row + 1) * half] = back


def main_kernel(where, strides, own_f, own_g, pre_part, back_part, pair, next_pair, in_chip, next_chip,
                first_kernel, second_kernel, keep, send, pre_grad, ext_f, ext_g, edge_f, edge_g, act, sums):
    lat, core = where[0], where[1]
    odd, second_core = where[2] == 1, core == 1
    mirror = lat == 0
    width = pair.shape[2]
    half = 2 * width
    for field, ext in ((0, ext_f), (1, ext_g)):
        for s in range(2):
            one, other = pair[field, s], next_pair[field, s]
            for row in range(2):
                middle = jnp.where(odd, one, other) if row == 0 else jnp.where(odd, other, one)
                stretch(ext.at[s * 2 + row], middle, in_chip[field, s, row], next_chip[field, s, row], second_core)
    for row in range(2):
        for s in range(2):
            ahead, behind = strides[s, lat * 2 + row, 2 * row], adjoint_stride(strides, s, row, 2 * row, lat)
            cells = slice(s * width, (s + 1) * width)
            for col in range(3):
                edge_f[row * 3 + col, cells] = moved(ext_f, s * 2 + row, 0 if col == 1 else (col - 1) * ahead, width)
                edge_g[row * 3 + col, cells] = moved(ext_g, s * 2 + row, 0 if col == 1 else (1 - col) * behind, width)

    for row in range(2):
        at = slice(row * half, (row + 1) * half)
        pre, back = pre_part[at], back_part[at]
        for col in range(3):
            pre += dot(edge_f[row * 3 + col], first_kernel[2 * row, col], NN)
            weight = second_kernel[2 - 2 * row, col]
            if row == 0:
                weight = jnp.where(mirror, second_kernel[0, col], weight)
            back += dot(edge_g[row * 3 + col], weight, NT)
        square = pre * pre
        bend = jnp.tanh(ROOT * (pre + CUBIC * (pre * square)))
        act[at] = (0.5 * pre * (1.0 + bend)).astype(jnp.bfloat16)
        slope = 0.5 * (1.0 + bend) + 0.5 * pre * (1.0 - bend * bend) * (ROOT * (1.0 + 3.0 * CUBIC * square))
        result = (back * slope).astype(jnp.bfloat16)
        for s in range(2):
            pre_grad[s, row] = result[s * width : (s + 1) * width]

    def place(value, k, col, owner):
        at = (k * 3 + col) * 256
        sums[jnp.where(core == owner, 0, 1), at : at + 256] = value

    def taps_of(own, edge, row, k, col):
        return own[OWN.index((row, k)) * 3 + col] if (row, k) in OWN else edge[row * 3 + col]

    turned = act[...].T
    above, below = turned[:, :half], turned[:, half:]
    for col in range(3):
        edge, upper = (dot(a, taps_of(own_g, edge_g, r, 0, col), NN) for r, a in enumerate((above, below)))
        centre, lower = (
            sum(dot(a, taps_of(own_g, edge_g, r, slot, col), NN) for r, a in enumerate((above, below))) for slot in (1, 2)
        )
        place(centre, 1, col, 1)
        place(lower + jnp.where(mirror, edge, 0.0), 0, col, 1)
        place(upper + jnp.where(mirror, 0.0, edge), 2, col, 1)
    rows = [jnp.concatenate([pre_grad[s, row] for s in range(2)], axis=0) for row in range(2)]
    for k in range(3):
        for col in range(3):
            place(sum(dot(taps_of(own_f, edge_f, r, k, col), rows[r], TN) for r in range(2)), k, col, 0)
    keep[...] = sums[0]
    send[...] = sums[1].astype(jnp.bfloat16)


def back_kernel(where, strides, grad, pre, pair, next_pair, in_chip, next_chip, first_kernel, out, ext, taps):
    lat = where[0]
    mirror = lat == 0
    width = grad.shape[2]
    fill(ext, 0, pre, (pair, next_pair, in_chip, next_chip), where)
    adjoint_taps(ext, taps, strides, lat, width)
    for row in range(2):
        total = adjoint_product(taps, first_kernel, mirror, row, 2 * width)
        for s in range(2):
            own = grad[s, row].astype(jnp.float32)
            out[s, row] = (own + total[s * width : (s + 1) * width]).astype(jnp.bfloat16)


def part_kernel(scale, where, mine, other, first, second):
    own, swapped = mine[...].astype(jnp.float32) * scale, other[...].astype(jnp.float32) * scale
    keeps = where[1] == 0
    first[...] = jnp.where(keeps, own, swapped)
    second[...] = jnp.where(keeps, swapped, own)


def both_ways(pairs):
    return pairs + [(b, a) for a, b in pairs]


def row_halos(fields, lon_count, lat_count):
    at = lambda lon, lat: (lon % lon_count) * lat_count + lat
    lons = range(lon_count)
    odd = lax.rem(lax.axis_index(("x", "yh")), 2)
    row = lambda i: lax.dynamic_index_in_dim(fields, i, 2, keepdims=False)
    pair = lax.ppermute(row(1 - odd), ALL, both_ways([(at(i, k), at(i, k + 1)) for i in lons for k in range(0, lat_count, 2)]))
    between = both_ways([(at(i, k), at(i, k + 1)) for i in lons for k in range(1, lat_count - 1, 2)])
    across = [(at(i, 0), at(i + lon_count // 2, 0)) for i in lons]
    return pair, lax.ppermute(row(odd), ALL, between + across)


def column_halos(parts, width, lon_count, lat_count):
    at = lambda lon, lat: (lon % lon_count) * lat_count + lat
    core = lax.axis_index("core")

    def edge(start):
        return jnp.concatenate([lax.dynamic_slice_in_dim(a, start, SPAN, 3) for a in parts], axis=2)

    reach = width - SPAN
    places = [(i, k) for i in range(0, lon_count, 2) for k in range(lat_count)]
    next_chip = lax.ppermute(edge(core * reach), ALL, both_ways([(at(i + 1, k), at(i + 2, k)) for i, k in places]))
    in_chip = lax.ppermute(edge((1 - core) * reach), "core", [(0, 1), (1, 0)])
    return in_chip, next_chip


def ordered(pair, next_pair):
    odd = lax.rem(lax.axis_index(("x", "yh")), 2) == 1
    return jnp.where(odd, pair, next_pair)[:, :, None], jnp.where(odd, next_pair, pair)[:, :, None]


def folded(count, cores, reach):
    pairs = []
    for i in range(count):
        for core in range(cores):
            turn = 2 * core
            base = (i + turn) % count
            partner = base ^ (reach - 1 if reach == count else reach // 2)
            pairs.append((i * cores + core, (partner - turn) % count * cores + core))
    return pairs


def local(features, out_grad, first_kernel, second_kernel, strides):
    slabs, rows, width, chans = features.shape
    lat_axes, lon_axes = ("x", "yh"), ("yl", "z", "core")
    lat_count, lon_count = lax.axis_size(lat_axes), lax.axis_size(lon_axes)
    lat, core = lax.axis_index(lat_axes), lax.axis_index("core")
    where = jnp.stack([lat, core, lax.rem(lat, 2)]).astype(jnp.int32)
    smem = pl.BlockSpec(memory_space=pltpu.SMEM)
    vmem = pl.BlockSpec(memory_space=pltpu.VMEM)
    cells = slabs * rows * width
    ext = pltpu.VMEM((slabs * (rows + 2), width + 2 * SPAN + 8, chans), jnp.float32)
    taps = pltpu.VMEM((9, cells, chans), jnp.bfloat16)
    params = pltpu.CompilerParams(vmem_limit_bytes=48 * 1024 * 1024)
    grads = (9 * chans, chans)
    swap = [(0, 1), (1, 0)]

    fields = jnp.stack([features, out_grad])
    rows_around = row_halos(fields, lon_count, lat_count)
    own_columns = column_halos([fields], width, lon_count, lat_count)
    ext_rows = pltpu.VMEM((2 * slabs, width + 2 * SPAN + 8, chans), jnp.float32)
    half = slabs * width
    early = pl.pallas_call(
        early_kernel,
        out_shape=[jax.ShapeDtypeStruct((3 * len(OWN), half, chans), jnp.bfloat16)] * 2
        + [jax.ShapeDtypeStruct((cells, chans), jnp.float32)] * 2,
        in_specs=[smem, smem] + [vmem] * 6,
        out_specs=[vmem] * 4,
        scratch_shapes=[ext_rows, ext_rows],
        compiler_params=params,
        name="early",
    )(where, strides, features, out_grad, *own_columns, first_kernel, second_kernel)
    early, rows_around = lax.optimization_barrier((early, rows_around))
    corners = column_halos(ordered(*rows_around), width, lon_count, lat_count)
    edge = pltpu.VMEM((6, half, chans), jnp.bfloat16)
    keep, send, pre_grad = pl.pallas_call(
        main_kernel,
        out_shape=[
            jax.ShapeDtypeStruct(grads, jnp.float32),
            jax.ShapeDtypeStruct(grads, jnp.bfloat16),
            jax.ShapeDtypeStruct(features.shape, jnp.bfloat16),
        ],
        in_specs=[smem, smem] + [vmem] * 10,
        out_specs=[vmem] * 3,
        scratch_shapes=[
            ext_rows,
            ext_rows,
            edge,
            edge,
            pltpu.VMEM((cells, chans), jnp.bfloat16),
            pltpu.VMEM((2,) + grads, jnp.float32),
        ],
        compiler_params=params,
        name="main",
    )(where, strides, *early, *rows_around, *corners, first_kernel, second_kernel)

    total = keep + lax.ppermute(send, "core", swap).astype(jnp.float32)
    planes, height, cores = lax.axis_size(PLANE), lax.axis_size("z"), lax.axis_size("core")
    total = total.astype(jnp.bfloat16).reshape(planes, 9 * chans // planes, chans)
    spread = lax.all_to_all(total, PLANE, 0, 0, tiled=True)

    spread, pre_grad = lax.optimization_barrier((spread, pre_grad))
    pre_field = pre_grad[None]
    pair, next_pair = row_halos(pre_field, lon_count, lat_count)
    part = jnp.sum(spread.astype(jnp.float32), axis=0)
    reach = 2
    while reach <= height:
        part = part + lax.ppermute(part, ("z", "core"), folded(height, cores, reach))
        reach *= 2
        if reach == height:
            part, pair = lax.optimization_barrier((part, pair))
    part, next_pair = lax.optimization_barrier((part.astype(jnp.bfloat16), next_pair))
    above, below = ordered(pair, next_pair)
    around = (pair, next_pair) + column_halos([above, pre_field, below], width, lon_count, lat_count)
    input_grad = pl.pallas_call(
        back_kernel,
        out_shape=jax.ShapeDtypeStruct(features.shape, jnp.bfloat16),
        in_specs=[smem, smem] + [vmem] * 7,
        out_specs=vmem,
        scratch_shapes=[ext, taps],
        compiler_params=params,
        name="back",
    )(where, strides, out_grad, pre_grad, *around, first_kernel)

    copies = jnp.broadcast_to(part[None], (planes,) + part.shape)
    mine = lax.all_to_all(copies, PLANE, 0, 0, tiled=True).reshape(grads)
    mine, input_grad = lax.optimization_barrier((mine, input_grad))
    other = lax.ppermute(mine, "core", swap)
    scale = 1.0 / math.sqrt(cells * lat_count * lon_count)
    block = pl.BlockSpec((9 * chans // 4, chans), lambda i: (i, 0))
    first, second = pl.pallas_call(
        lambda *refs: part_kernel(scale, *refs),
        grid=(4,),
        out_shape=[jax.ShapeDtypeStruct(grads, jnp.float32)] * 2,
        in_specs=[smem, block, block],
        out_specs=[block, block],
        compiler_params=params,
        name="part",
    )(where, mine, other)
    return input_grad, first.reshape(first_kernel.shape), second.reshape(first_kernel.shape)


def solution(mesh):
    wide = Mesh(mesh.devices.reshape(2, 8, 2, 4, 2), ALL)
    field = P(None, ("x", "yh"), ("yl", "z", "core"), None)
    return jax.shard_map(
        local,
        mesh=wide,
        in_specs=(field, field, P(), P(), P()),
        out_specs=(field, P(), P()),
        check_vma=False,
    )
```

```python
import math

import jax
import jax.numpy as jnp
from jax import lax
from jax.experimental import pallas as pl
from jax.experimental.pallas import tpu as pltpu
from jax.sharding import Mesh
from jax.sharding import PartitionSpec as P

POLE = 16
SPAN = 16
ALL = ("yl", "z", "core", "x", "yh")
PLANE = ("x", "yh", "yl")
NN = (((1,), (0,)), ((), ()))
NT = (((1,), (1,)), ((), ()))
TN = (((0,), (0,)), ((), ()))
ROOT = math.sqrt(2.0 / math.pi)
CUBIC = 0.044715


def dot(a, b, dims):
    return lax.dot_general(a, b, dims, preferred_element_type=jnp.float32)


def fill(ext, field, own, halo, where):
    pair, next_pair, in_chip, next_chip = halo
    width = own.shape[2]
    odd, core = where[2] == 1, where[1] == 1
    for s in range(2):
        for row in range(4):
            place = ext.at[s * 4 + row]
            if row in (0, 3):
                one, other = pair[field, s].astype(jnp.float32), next_pair[field, s].astype(jnp.float32)
                middle = jnp.where(odd, one, other) if row == 0 else jnp.where(odd, other, one)
            else:
                middle = own[s, row - 1].astype(jnp.float32)
            near, far = in_chip[field, s, row].astype(jnp.float32), next_chip[field, s, row].astype(jnp.float32)
            place[:SPAN] = jnp.where(core, near, far)
            place[SPAN : SPAN + width] = middle
            place[SPAN + width : 2 * SPAN + width] = jnp.where(core, far, near)


def tap(ext, s, row, shift, width):
    if isinstance(shift, int):
        return ext[s * 4 + row, SPAN + shift : SPAN + shift + width, :].astype(jnp.bfloat16)
    start = SPAN + shift
    rest = lax.rem(start, 8)
    span = ext[s * 4 + row, pl.ds(pl.multiple_of(start - rest, 8), width + 8), :]
    chans = span.shape[-1]
    turned = pltpu.roll(span.reshape(width // 8 + 1, 8, chans), lax.rem(8 - rest, 8), 1)
    lane = lax.broadcasted_iota(jnp.int32, (1, 8, chans), 1)
    moved = jnp.where(lane < 8 - rest, turned[:-1], turned[1:])
    return moved.reshape(width, chans).astype(jnp.bfloat16)


def adjoint_stride(strides, s, row, slot, lat):
    here = lat * 2 + row
    if slot == 0:
        if row == 1:
            return strides[s, lat * 2, 2]
        return jnp.where(lat == 0, strides[s, 0, 0], strides[s, jnp.maximum(here - 1, 0), 2])
    if slot == 1:
        return strides[s, here, 1]
    return strides[s, jnp.minimum(here + 1, POLE - 1), 0]


def adjoint_taps(ext, taps, strides, lat, width):
    for row in range(2):
        for s in range(2):
            at = (row * 2 + s) * width
            for slot in range(3):
                stride = adjoint_stride(strides, s, row, slot, lat)
                for col in range(3):
                    shift = 0 if col == 1 else -(col - 1) * stride
                    taps[slot * 3 + col, at : at + width] = tap(ext, s, row + slot, shift, width)


def adjoint_product(taps, kernel, mirror, row, half):
    total = None
    at = row * half
    for slot in range(3):
        for col in range(3):
            weight = kernel[2 - slot, col]
            if slot == 0 and row == 0:
                weight = jnp.where(mirror, kernel[0, col], weight)
            term = dot(taps[slot * 3 + col, at : at + half], weight, NT)
            total = term if total is None else total + term
    return total


OWN = ((0, 1), (0, 2), (1, 0), (1, 1))


def stretch(place, middle, near, far, core):
    width = middle.shape[0]
    near, far = near.astype(jnp.float32), far.astype(jnp.float32)
    place[:SPAN] = jnp.where(core, near, far)
    place[SPAN : SPAN + width] = middle.astype(jnp.float32)
    place[SPAN + width : 2 * SPAN + width] = jnp.where(core, far, near)


def moved(ext, at, shift, width):
    return tap(ext, at // 4, at % 4, shift, width)


def early_kernel(where, strides, feat, grad, in_chip, next_chip, first_kernel, second_kernel,
                 taps_f, taps_g, pre_part, back_part, ext_f, ext_g):
    lat, core = where[0], where[1] == 1
    width = feat.shape[2]
    half = 2 * width
    for field, own, ext in ((0, feat, ext_f), (1, grad, ext_g)):
        for s in range(2):
            for row in range(2):
                stretch(ext.at[s * 2 + row], own[s, row], in_chip[field, s, row], next_chip[field, s, row], core)
    for i, (row, k) in enumerate(OWN):
        for s in range(2):
            ahead, behind = strides[s, lat * 2 + row, k], adjoint_stride(strides, s, row, k, lat)
            at, cells = s * 2 + row + k - 1, slice(s * width, (s + 1) * width)
            for col in range(3):
                taps_f[i * 3 + col, cells] = moved(ext_f, at, 0 if col == 1 else (col - 1) * ahead, width)
                taps_g[i * 3 + col, cells] = moved(ext_g, at, 0 if col == 1 else (1 - col) * behind, width)
    for row in range(2):
        pre, back = None, None
        for i, (at, k) in enumerate(OWN):
            if at != row:
                continue
            for col in range(3):
                term = dot(taps_f[i * 3 + col], first_kernel[k, col], NN)
                pre = term if pre is None else pre + term
                term = dot(taps_g[i * 3 + col], second_kernel[2 - k, col], NT)
                back = term if back is None else back + term
        pre_part[row * half : (row + 1) * half] = pre
        back_part[row * half : (row + 1) * half] = back


def main_kernel(where, strides, own_f, own_g, pre_part, back_part, pair, next_pair, in_chip, next_chip,
                first_kernel, second_kernel, keep, send, pre_grad, ext_f, ext_g, edge_f, edge_g, act, sums):
    lat, core = where[0], where[1]
    odd, second_core = where[2] == 1, core == 1
    mirror = lat == 0
    width = pair.shape[2]
    half = 2 * width
    for field, ext in ((0, ext_f), (1, ext_g)):
        for s in range(2):
            one, other = pair[field, s], next_pair[field, s]
            for row in range(2):
                middle = jnp.where(odd, one, other) if row == 0 else jnp.where(odd, other, one)
                stretch(ext.at[s * 2 + row], middle, in_chip[field, s, row], next_chip[field, s, row], second_core)
    for row in range(2):
        for s in range(2):
            ahead, behind = strides[s, lat * 2 + row, 2 * row], adjoint_stride(strides, s, row, 2 * row, lat)
            cells = slice(s * width, (s + 1) * width)
            for col in range(3):
                edge_f[row * 3 + col, cells] = moved(ext_f, s * 2 + row, 0 if col == 1 else (col - 1) * ahead, width)
                edge_g[row * 3 + col, cells] = moved(ext_g, s * 2 + row, 0 if col == 1 else (1 - col) * behind, width)

    for row in range(2):
        at = slice(row * half, (row + 1) * half)
        pre, back = pre_part[at], back_part[at]
        for col in range(3):
            pre += dot(edge_f[row * 3 + col], first_kernel[2 * row, col], NN)
            weight = second_kernel[2 - 2 * row, col]
            if row == 0:
                weight = jnp.where(mirror, second_kernel[0, col], weight)
            back += dot(edge_g[row * 3 + col], weight, NT)
        square = pre * pre
        bend = jnp.tanh(ROOT * (pre + CUBIC * (pre * square)))
        act[at] = (0.5 * pre * (1.0 + bend)).astype(jnp.bfloat16)
        slope = 0.5 * (1.0 + bend) + 0.5 * pre * (1.0 - bend * bend) * (ROOT * (1.0 + 3.0 * CUBIC * square))
        result = (back * slope).astype(jnp.bfloat16)
        for s in range(2):
            pre_grad[s, row] = result[s * width : (s + 1) * width]

    def place(value, k, col, owner):
        at = (k * 3 + col) * 256
        sums[jnp.where(core == owner, 0, 1), at : at + 256] = value

    def taps_of(own, edge, row, k, col):
        return own[OWN.index((row, k)) * 3 + col] if (row, k) in OWN else edge[row * 3 + col]

    turned = act[...].T
    above, below = turned[:, :half], turned[:, half:]
    for col in range(3):
        edge, upper = (dot(a, taps_of(own_g, edge_g, r, 0, col), NN) for r, a in enumerate((above, below)))
        centre, lower = (
            sum(dot(a, taps_of(own_g, edge_g, r, slot, col), NN) for r, a in enumerate((above, below))) for slot in (1, 2)
        )
        place(centre, 1, col, 1)
        place(lower + jnp.where(mirror, edge, 0.0), 0, col, 1)
        place(upper + jnp.where(mirror, 0.0, edge), 2, col, 1)
    rows = [jnp.concatenate([pre_grad[s, row] for s in range(2)], axis=0) for row in range(2)]
    for k in range(3):
        for col in range(3):
            place(sum(dot(taps_of(own_f, edge_f, r, k, col), rows[r], TN) for r in range(2)), k, col, 0)
    keep[...] = sums[0]
    send[...] = sums[1].astype(jnp.bfloat16)


def back_kernel(where, strides, grad, pre, pair, next_pair, in_chip, next_chip, first_kernel, out, ext, taps):
    lat = where[0]
    mirror = lat == 0
    width = grad.shape[2]
    fill(ext, 0, pre, (pair, next_pair, in_chip, next_chip), where)
    adjoint_taps(ext, taps, strides, lat, width)
    for row in range(2):
        total = adjoint_product(taps, first_kernel, mirror, row, 2 * width)
        for s in range(2):
            own = grad[s, row].astype(jnp.float32)
            out[s, row] = (own + total[s * width : (s + 1) * width]).astype(jnp.bfloat16)


def part_kernel(scale, where, mine, other, first, second, held, sems):
    keeps = where[1] == 0
    count = sems.shape[1]
    step = mine.shape[0] // count
    stores = []
    for i in range(count):
        rows = pl.ds(i * step, step)
        own, swapped = mine[rows].astype(jnp.float32) * scale, other[rows].astype(jnp.float32) * scale
        held[0, rows] = jnp.where(keeps, own, swapped)
        held[1, rows] = jnp.where(keeps, swapped, own)
        for j, out in enumerate((first, second)):
            stores.append(pltpu.make_async_copy(held.at[j, rows], out.at[rows], sems.at[j, i]))
            stores[-1].start()
    for store in stores:
        store.wait()


def both_ways(pairs):
    return pairs + [(b, a) for a, b in pairs]


def row_halos(fields, lon_count, lat_count):
    at = lambda lon, lat: (lon % lon_count) * lat_count + lat
    lons = range(lon_count)
    odd = lax.rem(lax.axis_index(("x", "yh")), 2)
    row = lambda i: lax.dynamic_index_in_dim(fields, i, 2, keepdims=False)
    pair = lax.ppermute(row(1 - odd), ALL, both_ways([(at(i, k), at(i, k + 1)) for i in lons for k in range(0, lat_count, 2)]))
    between = both_ways([(at(i, k), at(i, k + 1)) for i in lons for k in range(1, lat_count - 1, 2)])
    across = [(at(i, 0), at(i + lon_count // 2, 0)) for i in lons]
    return pair, lax.ppermute(row(odd), ALL, between + across)


def column_halos(parts, width, lon_count, lat_count):
    at = lambda lon, lat: (lon % lon_count) * lat_count + lat
    core = lax.axis_index("core")

    def edge(start):
        return jnp.concatenate([lax.dynamic_slice_in_dim(a, start, SPAN, 3) for a in parts], axis=2)

    reach = width - SPAN
    places = [(i, k) for i in range(0, lon_count, 2) for k in range(lat_count)]
    next_chip = lax.ppermute(edge(core * reach), ALL, both_ways([(at(i + 1, k), at(i + 2, k)) for i, k in places]))
    in_chip = lax.ppermute(edge((1 - core) * reach), "core", [(0, 1), (1, 0)])
    return in_chip, next_chip


def ordered(pair, next_pair):
    odd = lax.rem(lax.axis_index(("x", "yh")), 2) == 1
    return jnp.where(odd, pair, next_pair)[:, :, None], jnp.where(odd, next_pair, pair)[:, :, None]


def folded(count, cores, reach):
    pairs = []
    for i in range(count):
        for core in range(cores):
            turn = 2 * core
            base = (i + turn) % count
            partner = base ^ (reach - 1 if reach == count else reach // 2)
            pairs.append((i * cores + core, (partner - turn) % count * cores + core))
    return pairs


def local(features, out_grad, first_kernel, second_kernel, strides):
    slabs, rows, width, chans = features.shape
    lat_axes, lon_axes = ("x", "yh"), ("yl", "z", "core")
    lat_count, lon_count = lax.axis_size(lat_axes), lax.axis_size(lon_axes)
    lat, core = lax.axis_index(lat_axes), lax.axis_index("core")
    where = jnp.stack([lat, core, lax.rem(lat, 2)]).astype(jnp.int32)
    smem = pl.BlockSpec(memory_space=pltpu.SMEM)
    vmem = pl.BlockSpec(memory_space=pltpu.VMEM)
    anywhere = pl.BlockSpec(memory_space=pl.ANY)
    cells = slabs * rows * width
    ext = pltpu.VMEM((slabs * (rows + 2), width + 2 * SPAN + 8, chans), jnp.float32)
    taps = pltpu.VMEM((9, cells, chans), jnp.bfloat16)
    params = pltpu.CompilerParams(vmem_limit_bytes=24 * 1024 * 1024)
    grads = (9 * chans, chans)
    swap = [(0, 1), (1, 0)]

    fields = jnp.stack([features, out_grad])
    rows_around = row_halos(fields, lon_count, lat_count)
    own_columns = column_halos([fields], width, lon_count, lat_count)
    ext_rows = pltpu.VMEM((2 * slabs, width + 2 * SPAN + 8, chans), jnp.float32)
    half = slabs * width
    early = pl.pallas_call(
        early_kernel,
        out_shape=[jax.ShapeDtypeStruct((3 * len(OWN), half, chans), jnp.bfloat16)] * 2
        + [jax.ShapeDtypeStruct((cells, chans), jnp.float32)] * 2,
        in_specs=[smem, smem] + [vmem] * 6,
        out_specs=[vmem] * 4,
        scratch_shapes=[ext_rows, ext_rows],
        compiler_params=params,
        name="early",
    )(where, strides, features, out_grad, *own_columns, first_kernel, second_kernel)
    early, rows_around = lax.optimization_barrier((early, rows_around))
    corners = column_halos(ordered(*rows_around), width, lon_count, lat_count)
    edge = pltpu.VMEM((6, half, chans), jnp.bfloat16)
    keep, send, pre_grad = pl.pallas_call(
        main_kernel,
        out_shape=[
            jax.ShapeDtypeStruct(grads, jnp.float32),
            jax.ShapeDtypeStruct(grads, jnp.bfloat16),
            jax.ShapeDtypeStruct(features.shape, jnp.bfloat16),
        ],
        in_specs=[smem, smem] + [vmem] * 10,
        out_specs=[vmem] * 3,
        scratch_shapes=[
            ext_rows,
            ext_rows,
            edge,
            edge,
            pltpu.VMEM((cells, chans), jnp.bfloat16),
            pltpu.VMEM((2,) + grads, jnp.float32),
        ],
        compiler_params=params,
        name="main",
    )(where, strides, *early, *rows_around, *corners, first_kernel, second_kernel)

    total = keep + lax.ppermute(send, "core", swap).astype(jnp.float32)
    planes, height, cores = lax.axis_size(PLANE), lax.axis_size("z"), lax.axis_size("core")
    total = total.astype(jnp.bfloat16).reshape(planes, 9 * chans // planes, chans)
    spread = lax.all_to_all(total, PLANE, 0, 0, tiled=True)

    spread, pre_grad = lax.optimization_barrier((spread, pre_grad))
    pre_field = pre_grad[None]
    pair, next_pair = row_halos(pre_field, lon_count, lat_count)
    part = jnp.sum(spread.astype(jnp.float32), axis=0)
    reach = 2
    while reach <= height:
        part = part + lax.ppermute(part, ("z", "core"), folded(height, cores, reach))
        reach *= 2
        if reach == height:
            part, pair = lax.optimization_barrier((part, pair))
    part, next_pair = lax.optimization_barrier((part.astype(jnp.bfloat16), next_pair))
    above, below = ordered(pair, next_pair)
    around = (pair, next_pair) + column_halos([above, pre_field, below], width, lon_count, lat_count)
    input_grad = pl.pallas_call(
        back_kernel,
        out_shape=jax.ShapeDtypeStruct(features.shape, jnp.bfloat16),
        in_specs=[smem, smem] + [vmem] * 7,
        out_specs=vmem,
        scratch_shapes=[ext, taps],
        compiler_params=params,
        name="back",
    )(where, strides, out_grad, pre_grad, *around, first_kernel)

    copies = jnp.broadcast_to(part[None], (planes,) + part.shape)
    mine = lax.all_to_all(copies, PLANE, 0, 0, tiled=True).reshape(grads)
    mine, input_grad = lax.optimization_barrier((mine, input_grad))
    other = lax.ppermute(mine, "core", swap)
    scale = 1.0 / math.sqrt(cells * lat_count * lon_count)
    first, second = pl.pallas_call(
        lambda *refs: part_kernel(scale, *refs),
        out_shape=[jax.ShapeDtypeStruct(grads, jnp.float32)] * 2,
        in_specs=[smem, vmem, vmem],
        out_specs=[anywhere] * 2,
        scratch_shapes=[pltpu.VMEM((2,) + grads, jnp.float32), pltpu.SemaphoreType.DMA((2, 9))],
        compiler_params=params,
        name="part",
    )(where, mine, other)
    return input_grad, first.reshape(first_kernel.shape), second.reshape(first_kernel.shape)


def solution(mesh):
    wide = Mesh(mesh.devices.reshape(2, 8, 2, 4, 2), ALL)
    field = P(None, ("x", "yh"), ("yl", "z", "core"), None)
    return jax.shard_map(
        local,
        mesh=wide,
        in_specs=(field, field, P(), P(), P()),
        out_specs=(field, P(), P()),
        check_vma=False,
    )
```

```python
import math

import jax
import jax.numpy as jnp
from jax import lax
from jax.experimental import pallas as pl
from jax.experimental.pallas import tpu as pltpu
from jax.sharding import Mesh
from jax.sharding import PartitionSpec as P

POLE = 16
SPAN = 16
ALL = ("yl", "z", "core", "x", "yh")
PLANE = ("x", "yh", "yl")
NN = (((1,), (0,)), ((), ()))
NT = (((1,), (1,)), ((), ()))
TN = (((0,), (0,)), ((), ()))
ROOT = math.sqrt(2.0 / math.pi)
CUBIC = 0.044715


def dot(a, b, dims):
    return lax.dot_general(a, b, dims, preferred_element_type=jnp.float32)


def fill(ext, field, own, halo, where):
    pair, next_pair, in_chip, next_chip = halo
    width = own.shape[2]
    odd, core = where[2] == 1, where[1] == 1
    for s in range(2):
        for row in range(4):
            place = ext.at[s * 4 + row]
            if row in (0, 3):
                one, other = pair[field, s].astype(jnp.float32), next_pair[field, s].astype(jnp.float32)
                middle = jnp.where(odd, one, other) if row == 0 else jnp.where(odd, other, one)
            else:
                middle = own[s, row - 1].astype(jnp.float32)
            near, far = in_chip[field, s, row].astype(jnp.float32), next_chip[field, s, row].astype(jnp.float32)
            place[:SPAN] = jnp.where(core, near, far)
            place[SPAN : SPAN + width] = middle
            place[SPAN + width : 2 * SPAN + width] = jnp.where(core, far, near)


def tap(ext, s, row, shift, width):
    if isinstance(shift, int):
        return ext[s * 4 + row, SPAN + shift : SPAN + shift + width, :].astype(jnp.bfloat16)
    start = SPAN + shift
    rest = lax.rem(start, 8)
    span = ext[s * 4 + row, pl.ds(pl.multiple_of(start - rest, 8), width + 8), :]
    chans = span.shape[-1]
    turned = pltpu.roll(span.reshape(width // 8 + 1, 8, chans), lax.rem(8 - rest, 8), 1)
    lane = lax.broadcasted_iota(jnp.int32, (1, 8, chans), 1)
    moved = jnp.where(lane < 8 - rest, turned[:-1], turned[1:])
    return moved.reshape(width, chans).astype(jnp.bfloat16)


def adjoint_stride(strides, s, row, slot, lat):
    here = lat * 2 + row
    if slot == 0:
        if row == 1:
            return strides[s, lat * 2, 2]
        return jnp.where(lat == 0, strides[s, 0, 0], strides[s, jnp.maximum(here - 1, 0), 2])
    if slot == 1:
        return strides[s, here, 1]
    return strides[s, jnp.minimum(here + 1, POLE - 1), 0]


def adjoint_taps(ext, taps, strides, lat, width):
    for row in range(2):
        for s in range(2):
            at = (row * 2 + s) * width
            for slot in range(3):
                stride = adjoint_stride(strides, s, row, slot, lat)
                for col in range(3):
                    shift = 0 if col == 1 else -(col - 1) * stride
                    taps[slot * 3 + col, at : at + width] = tap(ext, s, row + slot, shift, width)


def adjoint_product(taps, kernel, mirror, row, half):
    total = None
    at = row * half
    for slot in range(3):
        for col in range(3):
            weight = kernel[2 - slot, col]
            if slot == 0 and row == 0:
                weight = jnp.where(mirror, kernel[0, col], weight)
            term = dot(taps[slot * 3 + col, at : at + half], weight, NT)
            total = term if total is None else total + term
    return total


OWN = ((0, 1), (0, 2), (1, 0), (1, 1))


def stretch(place, middle, near, far, core):
    width = middle.shape[0]
    near, far = near.astype(jnp.float32), far.astype(jnp.float32)
    place[:SPAN] = jnp.where(core, near, far)
    place[SPAN : SPAN + width] = middle.astype(jnp.float32)
    place[SPAN + width : 2 * SPAN + width] = jnp.where(core, far, near)


def moved(ext, at, shift, width):
    return tap(ext, at // 4, at % 4, shift, width)


def early_kernel(where, strides, feat, grad, in_chip, next_chip, first_kernel, second_kernel,
                 taps_f, taps_g, pre_part, back_part, ext_f, ext_g):
    lat, core = where[0], where[1] == 1
    width = feat.shape[2]
    half = 2 * width
    for field, own, ext in ((0, feat, ext_f), (1, grad, ext_g)):
        for s in range(2):
            for row in range(2):
                stretch(ext.at[s * 2 + row], own[s, row], in_chip[field, s, row], next_chip[field, s, row], core)
    for i, (row, k) in enumerate(OWN):
        for s in range(2):
            ahead, behind = strides[s, lat * 2 + row, k], adjoint_stride(strides, s, row, k, lat)
            at, cells = s * 2 + row + k - 1, slice(s * width, (s + 1) * width)
            for col in range(3):
                taps_f[i * 3 + col, cells] = moved(ext_f, at, 0 if col == 1 else (col - 1) * ahead, width)
                taps_g[i * 3 + col, cells] = moved(ext_g, at, 0 if col == 1 else (1 - col) * behind, width)
    for row in range(2):
        pre, back = None, None
        for i, (at, k) in enumerate(OWN):
            if at != row:
                continue
            for col in range(3):
                term = dot(taps_f[i * 3 + col], first_kernel[k, col], NN)
                pre = term if pre is None else pre + term
                term = dot(taps_g[i * 3 + col], second_kernel[2 - k, col], NT)
                back = term if back is None else back + term
        pre_part[row * half : (row + 1) * half] = pre
        back_part[row * half : (row + 1) * half] = back


def main_kernel(where, strides, own_f, own_g, pre_part, back_part, pair, next_pair, in_chip, next_chip,
                first_kernel, second_kernel, keep, send, pre_grad, ext_f, ext_g, edge_f, edge_g, act, sums):
    lat, core = where[0], where[1]
    odd, second_core = where[2] == 1, core == 1
    mirror = lat == 0
    width = pair.shape[2]
    half = 2 * width
    for field, ext in ((0, ext_f), (1, ext_g)):
        for s in range(2):
            one, other = pair[field, s], next_pair[field, s]
            for row in range(2):
                middle = jnp.where(odd, one, other) if row == 0 else jnp.where(odd, other, one)
                stretch(ext.at[s * 2 + row], middle, in_chip[field, s, row], next_chip[field, s, row], second_core)
    for row in range(2):
        for s in range(2):
            ahead, behind = strides[s, lat * 2 + row, 2 * row], adjoint_stride(strides, s, row, 2 * row, lat)
            cells = slice(s * width, (s + 1) * width)
            for col in range(3):
                edge_f[row * 3 + col, cells] = moved(ext_f, s * 2 + row, 0 if col == 1 else (col - 1) * ahead, width)
                edge_g[row * 3 + col, cells] = moved(ext_g, s * 2 + row, 0 if col == 1 else (1 - col) * behind, width)

    for row in range(2):
        at = slice(row * half, (row + 1) * half)
        pre, back = pre_part[at], back_part[at]
        for col in range(3):
            pre += dot(edge_f[row * 3 + col], first_kernel[2 * row, col], NN)
            weight = second_kernel[2 - 2 * row, col]
            if row == 0:
                weight = jnp.where(mirror, second_kernel[0, col], weight)
            back += dot(edge_g[row * 3 + col], weight, NT)
        square = pre * pre
        bend = jnp.tanh(ROOT * (pre + CUBIC * (pre * square)))
        act[at] = (0.5 * pre * (1.0 + bend)).astype(jnp.bfloat16)
        slope = 0.5 * (1.0 + bend) + 0.5 * pre * (1.0 - bend * bend) * (ROOT * (1.0 + 3.0 * CUBIC * square))
        result = (back * slope).astype(jnp.bfloat16)
        for s in range(2):
            pre_grad[s, row] = result[s * width : (s + 1) * width]

    def place(value, k, col, owner):
        at = (k * 3 + col) * 256
        sums[jnp.where(core == owner, 0, 1), at : at + 256] = value

    def taps_of(own, edge, row, k, col):
        return own[OWN.index((row, k)) * 3 + col] if (row, k) in OWN else edge[row * 3 + col]

    turned = act[...].T
    above, below = turned[:, :half], turned[:, half:]
    for col in range(3):
        edge, upper = (dot(a, taps_of(own_g, edge_g, r, 0, col), NN) for r, a in enumerate((above, below)))
        centre, lower = (
            sum(dot(a, taps_of(own_g, edge_g, r, slot, col), NN) for r, a in enumerate((above, below))) for slot in (1, 2)
        )
        place(centre, 1, col, 1)
        place(lower + jnp.where(mirror, edge, 0.0), 0, col, 1)
        place(upper + jnp.where(mirror, 0.0, edge), 2, col, 1)
    rows = [jnp.concatenate([pre_grad[s, row] for s in range(2)], axis=0) for row in range(2)]
    for k in range(3):
        for col in range(3):
            place(sum(dot(taps_of(own_f, edge_f, r, k, col), rows[r], TN) for r in range(2)), k, col, 0)
    keep[...] = sums[0]
    send[...] = sums[1].astype(jnp.bfloat16)


def back_kernel(where, strides, grad, pre, pair, next_pair, in_chip, next_chip, first_kernel, out, ext, taps):
    lat = where[0]
    mirror = lat == 0
    width = grad.shape[2]
    fill(ext, 0, pre, (pair, next_pair, in_chip, next_chip), where)
    adjoint_taps(ext, taps, strides, lat, width)
    for row in range(2):
        total = adjoint_product(taps, first_kernel, mirror, row, 2 * width)
        for s in range(2):
            own = grad[s, row].astype(jnp.float32)
            out[s, row] = (own + total[s * width : (s + 1) * width]).astype(jnp.bfloat16)


def part_kernel(scale, owner, where, given, *refs):
    first, second, held, sems = refs[-4:]
    count = sems.shape[0]
    step = given.shape[0] // count
    rows = [pl.ds(i * step, step) for i in range(count)]
    to_first = where[1] == owner

    def every(act_on):
        for i, at in enumerate(rows):
            act_on(i, at)

    def write(out):
        def one(i, at):
            held[at] = given[at].astype(jnp.float32) * scale
            pltpu.make_async_copy(held.at[at], out.at[at], sems.at[i]).start()

        every(one)
        every(lambda i, at: pltpu.make_async_copy(held.at[at], out.at[at], sems.at[i]).wait())

    pl.when(to_first)(lambda: write(first))
    pl.when(jnp.logical_not(to_first))(lambda: write(second))


def copies_kernel(part, got, out):
    value = (part[...] + got[...]).astype(jnp.bfloat16)
    for i in range(out.shape[0]):
        out[i] = value


def both_ways(pairs):
    return pairs + [(b, a) for a, b in pairs]


def row_halos(fields, lon_count, lat_count):
    at = lambda lon, lat: (lon % lon_count) * lat_count + lat
    lons = range(lon_count)
    odd = lax.rem(lax.axis_index(("x", "yh")), 2)
    row = lambda i: lax.dynamic_index_in_dim(fields, i, 2, keepdims=False)
    pair = lax.ppermute(row(1 - odd), ALL, both_ways([(at(i, k), at(i, k + 1)) for i in lons for k in range(0, lat_count, 2)]))
    between = both_ways([(at(i, k), at(i, k + 1)) for i in lons for k in range(1, lat_count - 1, 2)])
    across = [(at(i, 0), at(i + lon_count // 2, 0)) for i in lons]
    return pair, lax.ppermute(row(odd), ALL, between + across)


def column_halos(parts, width, lon_count, lat_count):
    at = lambda lon, lat: (lon % lon_count) * lat_count + lat
    core = lax.axis_index("core")

    def edge(start):
        return jnp.concatenate([lax.dynamic_slice_in_dim(a, start, SPAN, 3) for a in parts], axis=2)

    reach = width - SPAN
    places = [(i, k) for i in range(0, lon_count, 2) for k in range(lat_count)]
    next_chip = lax.ppermute(edge(core * reach), ALL, both_ways([(at(i + 1, k), at(i + 2, k)) for i, k in places]))
    in_chip = lax.ppermute(edge((1 - core) * reach), "core", [(0, 1), (1, 0)])
    return in_chip, next_chip


def ordered(pair, next_pair):
    odd = lax.rem(lax.axis_index(("x", "yh")), 2) == 1
    return jnp.where(odd, pair, next_pair)[:, :, None], jnp.where(odd, next_pair, pair)[:, :, None]


def folded(count, cores, reach):
    pairs = []
    for i in range(count):
        for core in range(cores):
            turn = 2 * core
            base = (i + turn) % count
            partner = base ^ (reach - 1 if reach == count else reach // 2)
            pairs.append((i * cores + core, (partner - turn) % count * cores + core))
    return pairs


def local(features, out_grad, first_kernel, second_kernel, strides):
    slabs, rows, width, chans = features.shape
    lat_axes, lon_axes = ("x", "yh"), ("yl", "z", "core")
    lat_count, lon_count = lax.axis_size(lat_axes), lax.axis_size(lon_axes)
    lat, core = lax.axis_index(lat_axes), lax.axis_index("core")
    where = jnp.stack([lat, core, lax.rem(lat, 2)]).astype(jnp.int32)
    smem = pl.BlockSpec(memory_space=pltpu.SMEM)
    vmem = pl.BlockSpec(memory_space=pltpu.VMEM)
    anywhere = pl.BlockSpec(memory_space=pl.ANY)
    cells = slabs * rows * width
    ext = pltpu.VMEM((slabs * (rows + 2), width + 2 * SPAN + 8, chans), jnp.float32)
    taps = pltpu.VMEM((9, cells, chans), jnp.bfloat16)
    params = pltpu.CompilerParams(vmem_limit_bytes=24 * 1024 * 1024)
    grads = (9 * chans, chans)
    swap = [(0, 1), (1, 0)]

    fields = jnp.stack([features, out_grad])
    rows_around = row_halos(fields, lon_count, lat_count)
    own_columns = column_halos([fields], width, lon_count, lat_count)
    ext_rows = pltpu.VMEM((2 * slabs, width + 2 * SPAN + 8, chans), jnp.float32)
    half = slabs * width
    early = pl.pallas_call(
        early_kernel,
        out_shape=[jax.ShapeDtypeStruct((3 * len(OWN), half, chans), jnp.bfloat16)] * 2
        + [jax.ShapeDtypeStruct((cells, chans), jnp.float32)] * 2,
        in_specs=[smem, smem] + [vmem] * 6,
        out_specs=[vmem] * 4,
        scratch_shapes=[ext_rows, ext_rows],
        compiler_params=params,
        name="early",
    )(where, strides, features, out_grad, *own_columns, first_kernel, second_kernel)
    early, rows_around = lax.optimization_barrier((early, rows_around))
    corners = column_halos(ordered(*rows_around), width, lon_count, lat_count)
    edge = pltpu.VMEM((6, half, chans), jnp.bfloat16)
    keep, send, pre_grad = pl.pallas_call(
        main_kernel,
        out_shape=[
            jax.ShapeDtypeStruct(grads, jnp.float32),
            jax.ShapeDtypeStruct(grads, jnp.bfloat16),
            jax.ShapeDtypeStruct(features.shape, jnp.bfloat16),
        ],
        in_specs=[smem, smem] + [vmem] * 10,
        out_specs=[vmem] * 3,
        scratch_shapes=[
            ext_rows,
            ext_rows,
            edge,
            edge,
            pltpu.VMEM((cells, chans), jnp.bfloat16),
            pltpu.VMEM((2,) + grads, jnp.float32),
        ],
        compiler_params=params,
        name="main",
    )(where, strides, *early, *rows_around, *corners, first_kernel, second_kernel)

    total = keep + lax.ppermute(send, "core", swap).astype(jnp.float32)
    planes, height, cores = lax.axis_size(PLANE), lax.axis_size("z"), lax.axis_size("core")
    total = total.astype(jnp.bfloat16).reshape(planes, 9 * chans // planes, chans)
    spread = lax.all_to_all(total, PLANE, 0, 0, tiled=True)

    spread, pre_grad = lax.optimization_barrier((spread, pre_grad))
    pre_field = pre_grad[None]
    pair, next_pair = row_halos(pre_field, lon_count, lat_count)
    part = jnp.sum(spread.astype(jnp.float32), axis=0)
    reach = 2
    while reach <= height:
        got = lax.ppermute(part, ("z", "core"), folded(height, cores, reach))
        if reach < height:
            part = part + got
        reach *= 2
        if reach == height:
            part, pair = lax.optimization_barrier((part, pair))
    got, next_pair = lax.optimization_barrier((got, next_pair))
    above, below = ordered(pair, next_pair)
    around = (pair, next_pair) + column_halos([above, pre_field, below], width, lon_count, lat_count)
    input_grad = pl.pallas_call(
        back_kernel,
        out_shape=jax.ShapeDtypeStruct(features.shape, jnp.bfloat16),
        in_specs=[smem, smem] + [vmem] * 7,
        out_specs=vmem,
        scratch_shapes=[ext, taps],
        compiler_params=params,
        name="back",
    )(where, strides, out_grad, pre_grad, *around, first_kernel)

    copies = pl.pallas_call(
        copies_kernel,
        out_shape=jax.ShapeDtypeStruct((planes,) + part.shape, jnp.bfloat16),
        in_specs=[vmem] * 2,
        out_specs=vmem,
        compiler_params=params,
        name="copies",
    )(part, got)
    mine = lax.all_to_all(copies, PLANE, 0, 0, tiled=True).reshape(grads)
    mine, input_grad = lax.optimization_barrier((mine, input_grad))
    other = lax.ppermute(mine, "core", swap)
    scale = 1.0 / math.sqrt(cells * lat_count * lon_count)
    wide = [jax.ShapeDtypeStruct(grads, jnp.float32)] * 2
    scratch = [pltpu.VMEM(grads, jnp.float32), pltpu.SemaphoreType.DMA((6,))]
    sides = pl.pallas_call(
        lambda *refs: part_kernel(scale, 0, *refs),
        out_shape=wide,
        in_specs=[smem, vmem],
        out_specs=[anywhere] * 2,
        scratch_shapes=scratch,
        compiler_params=params,
        name="own_part",
    )(where, mine)
    first, second = pl.pallas_call(
        lambda *refs: part_kernel(scale, 1, *refs),
        out_shape=wide,
        in_specs=[smem, vmem, anywhere, anywhere],
        out_specs=[anywhere] * 2,
        scratch_shapes=scratch,
        input_output_aliases={2: 0, 3: 1},
        compiler_params=params,
        name="other_part",
    )(where, other, *sides)
    return input_grad, first.reshape(first_kernel.shape), second.reshape(first_kernel.shape)


def solution(mesh):
    wide = Mesh(mesh.devices.reshape(2, 8, 2, 4, 2), ALL)
    field = P(None, ("x", "yh"), ("yl", "z", "core"), None)
    return jax.shard_map(
        local,
        mesh=wide,
        in_specs=(field, field, P(), P(), P()),
        out_specs=(field, P(), P()),
        check_vma=False,
    )
```

```python
import math

import jax
import jax.numpy as jnp
from jax import lax
from jax.experimental import pallas as pl
from jax.experimental.pallas import tpu as pltpu
from jax.sharding import Mesh
from jax.sharding import PartitionSpec as P

POLE = 16
SPAN = 16
ALL = ("yl", "z", "core", "x", "yh")
PLANE = ("x", "yh", "yl")
NN = (((1,), (0,)), ((), ()))
NT = (((1,), (1,)), ((), ()))
TN = (((0,), (0,)), ((), ()))
ROOT = math.sqrt(2.0 / math.pi)
CUBIC = 0.044715


def dot(a, b, dims):
    return lax.dot_general(a, b, dims, preferred_element_type=jnp.float32)


def fill(ext, field, own, halo, where):
    pair, next_pair, in_chip, next_chip = halo
    width = own.shape[2]
    odd, core = where[2] == 1, where[1] == 1
    for s in range(2):
        for row in range(4):
            place = ext.at[s * 4 + row]
            if row in (0, 3):
                one, other = pair[field, s].astype(jnp.float32), next_pair[field, s].astype(jnp.float32)
                middle = jnp.where(odd, one, other) if row == 0 else jnp.where(odd, other, one)
            else:
                middle = own[s, row - 1].astype(jnp.float32)
            near, far = in_chip[field, s, row].astype(jnp.float32), next_chip[field, s, row].astype(jnp.float32)
            place[:SPAN] = jnp.where(core, near, far)
            place[SPAN : SPAN + width] = middle
            place[SPAN + width : 2 * SPAN + width] = jnp.where(core, far, near)


def tap(ext, s, row, shift, width):
    if isinstance(shift, int):
        return ext[s * 4 + row, SPAN + shift : SPAN + shift + width, :].astype(jnp.bfloat16)
    start = SPAN + shift
    rest = lax.rem(start, 8)
    span = ext[s * 4 + row, pl.ds(pl.multiple_of(start - rest, 8), width + 8), :]
    chans = span.shape[-1]
    turned = pltpu.roll(span.reshape(width // 8 + 1, 8, chans), lax.rem(8 - rest, 8), 1)
    lane = lax.broadcasted_iota(jnp.int32, (1, 8, chans), 1)
    moved = jnp.where(lane < 8 - rest, turned[:-1], turned[1:])
    return moved.reshape(width, chans).astype(jnp.bfloat16)


def adjoint_stride(strides, s, row, slot, lat):
    here = lat * 2 + row
    if slot == 0:
        if row == 1:
            return strides[s, lat * 2, 2]
        return jnp.where(lat == 0, strides[s, 0, 0], strides[s, jnp.maximum(here - 1, 0), 2])
    if slot == 1:
        return strides[s, here, 1]
    return strides[s, jnp.minimum(here + 1, POLE - 1), 0]


def adjoint_taps(ext, taps, strides, lat, width):
    for row in range(2):
        for s in range(2):
            at = (row * 2 + s) * width
            for slot in range(3):
                stride = adjoint_stride(strides, s, row, slot, lat)
                for col in range(3):
                    shift = 0 if col == 1 else -(col - 1) * stride
                    taps[slot * 3 + col, at : at + width] = tap(ext, s, row + slot, shift, width)


def adjoint_product(taps, kernel, mirror, row, half):
    total = None
    at = row * half
    for slot in range(3):
        for col in range(3):
            weight = kernel[2 - slot, col]
            if slot == 0 and row == 0:
                weight = jnp.where(mirror, kernel[0, col], weight)
            term = dot(taps[slot * 3 + col, at : at + half], weight, NT)
            total = term if total is None else total + term
    return total


OWN = ((0, 1), (0, 2), (1, 0), (1, 1))


def stretch(place, middle, near, far, core):
    width = middle.shape[0]
    near, far = near.astype(jnp.float32), far.astype(jnp.float32)
    place[:SPAN] = jnp.where(core, near, far)
    place[SPAN : SPAN + width] = middle.astype(jnp.float32)
    place[SPAN + width : 2 * SPAN + width] = jnp.where(core, far, near)


def moved(ext, at, shift, width):
    return tap(ext, at // 4, at % 4, shift, width)


def early_kernel(where, strides, feat, grad, in_chip, next_chip, first_kernel, second_kernel,
                 taps_f, taps_g, pre_part, back_part, ext_f, ext_g):
    lat, core = where[0], where[1] == 1
    width = feat.shape[2]
    half = 2 * width
    for field, own, ext in ((0, feat, ext_f), (1, grad, ext_g)):
        for s in range(2):
            for row in range(2):
                stretch(ext.at[s * 2 + row], own[s, row], in_chip[field, s, row], next_chip[field, s, row], core)
    for i, (row, k) in enumerate(OWN):
        for s in range(2):
            ahead, behind = strides[s, lat * 2 + row, k], adjoint_stride(strides, s, row, k, lat)
            at, cells = s * 2 + row + k - 1, slice(s * width, (s + 1) * width)
            for col in range(3):
                taps_f[i * 3 + col, cells] = moved(ext_f, at, 0 if col == 1 else (col - 1) * ahead, width)
                taps_g[i * 3 + col, cells] = moved(ext_g, at, 0 if col == 1 else (1 - col) * behind, width)
    for row in range(2):
        pre, back = None, None
        for i, (at, k) in enumerate(OWN):
            if at != row:
                continue
            for col in range(3):
                term = dot(taps_f[i * 3 + col], first_kernel[k, col], NN)
                pre = term if pre is None else pre + term
                term = dot(taps_g[i * 3 + col], second_kernel[2 - k, col], NT)
                back = term if back is None else back + term
        pre_part[row * half : (row + 1) * half] = pre
        back_part[row * half : (row + 1) * half] = back


def main_kernel(where, strides, own_f, own_g, pre_part, back_part, pair, next_pair, in_chip, next_chip,
                first_kernel, second_kernel, keep, send, pre_grad, ext_f, ext_g, edge_f, edge_g, act, sums):
    lat, core = where[0], where[1]
    odd, second_core = where[2] == 1, core == 1
    mirror = lat == 0
    width = pair.shape[2]
    half = 2 * width
    for field, ext in ((0, ext_f), (1, ext_g)):
        for s in range(2):
            one, other = pair[field, s], next_pair[field, s]
            for row in range(2):
                middle = jnp.where(odd, one, other) if row == 0 else jnp.where(odd, other, one)
                stretch(ext.at[s * 2 + row], middle, in_chip[field, s, row], next_chip[field, s, row], second_core)
    for row in range(2):
        for s in range(2):
            ahead, behind = strides[s, lat * 2 + row, 2 * row], adjoint_stride(strides, s, row, 2 * row, lat)
            cells = slice(s * width, (s + 1) * width)
            for col in range(3):
                edge_f[row * 3 + col, cells] = moved(ext_f, s * 2 + row, 0 if col == 1 else (col - 1) * ahead, width)
                edge_g[row * 3 + col, cells] = moved(ext_g, s * 2 + row, 0 if col == 1 else (1 - col) * behind, width)

    for row in range(2):
        at = slice(row * half, (row + 1) * half)
        pre, back = pre_part[at], back_part[at]
        for col in range(3):
            pre += dot(edge_f[row * 3 + col], first_kernel[2 * row, col], NN)
            weight = second_kernel[2 - 2 * row, col]
            if row == 0:
                weight = jnp.where(mirror, second_kernel[0, col], weight)
            back += dot(edge_g[row * 3 + col], weight, NT)
        square = pre * pre
        bend = jnp.tanh(ROOT * (pre + CUBIC * (pre * square)))
        act[at] = (0.5 * pre * (1.0 + bend)).astype(jnp.bfloat16)
        slope = 0.5 * (1.0 + bend) + 0.5 * pre * (1.0 - bend * bend) * (ROOT * (1.0 + 3.0 * CUBIC * square))
        result = (back * slope).astype(jnp.bfloat16)
        for s in range(2):
            pre_grad[s, row] = result[s * width : (s + 1) * width]

    def place(value, k, col, owner):
        at = (k * 3 + col) * 256
        sums[jnp.where(core == owner, 0, 1), at : at + 256] = value

    def taps_of(own, edge, row, k, col):
        return own[OWN.index((row, k)) * 3 + col] if (row, k) in OWN else edge[row * 3 + col]

    turned = act[...].T
    above, below = turned[:, :half], turned[:, half:]
    for col in range(3):
        edge, upper = (dot(a, taps_of(own_g, edge_g, r, 0, col), NN) for r, a in enumerate((above, below)))
        centre, lower = (
            sum(dot(a, taps_of(own_g, edge_g, r, slot, col), NN) for r, a in enumerate((above, below))) for slot in (1, 2)
        )
        place(centre, 1, col, 1)
        place(lower + jnp.where(mirror, edge, 0.0), 0, col, 1)
        place(upper + jnp.where(mirror, 0.0, edge), 2, col, 1)
    rows = [jnp.concatenate([pre_grad[s, row] for s in range(2)], axis=0) for row in range(2)]
    for k in range(3):
        for col in range(3):
            place(sum(dot(taps_of(own_f, edge_f, r, k, col), rows[r], TN) for r in range(2)), k, col, 0)
    keep[...] = sums[0]
    send[...] = sums[1].astype(jnp.bfloat16)


def back_kernel(where, strides, grad, pre, pair, next_pair, in_chip, next_chip, first_kernel, out, ext, taps):
    lat = where[0]
    mirror = lat == 0
    width = grad.shape[2]
    fill(ext, 0, pre, (pair, next_pair, in_chip, next_chip), where)
    adjoint_taps(ext, taps, strides, lat, width)
    for row in range(2):
        total = adjoint_product(taps, first_kernel, mirror, row, 2 * width)
        for s in range(2):
            own = grad[s, row].astype(jnp.float32)
            out[s, row] = (own + total[s * width : (s + 1) * width]).astype(jnp.bfloat16)


def part_kernel(scale, owner, where, given, *refs):
    first, second, held, sems = refs[-4:]
    count = sems.shape[0]
    step = given.shape[0] // count
    rows = [pl.ds(i * step, step) for i in range(count)]
    to_first = where[1] == owner

    def every(act_on):
        for i, at in enumerate(rows):
            act_on(i, at)

    def write(out):
        def one(i, at):
            held[at] = given[at].astype(jnp.float32) * scale
            pltpu.make_async_copy(held.at[at], out.at[at], sems.at[i]).start()

        every(one)
        every(lambda i, at: pltpu.make_async_copy(held.at[at], out.at[at], sems.at[i]).wait())

    pl.when(to_first)(lambda: write(first))
    pl.when(jnp.logical_not(to_first))(lambda: write(second))


def copies_kernel(part, got, out):
    value = (part[...] + got[...]).astype(jnp.bfloat16)
    for i in range(out.shape[0]):
        out[i] = value


def both_ways(pairs):
    return pairs + [(b, a) for a, b in pairs]


def row_halos(fields, lon_count, lat_count):
    at = lambda lon, lat: (lon % lon_count) * lat_count + lat
    lons = range(lon_count)
    odd = lax.rem(lax.axis_index(("x", "yh")), 2)
    row = lambda i: lax.dynamic_index_in_dim(fields, i, 2, keepdims=False)
    pair = lax.ppermute(row(1 - odd), ALL, both_ways([(at(i, k), at(i, k + 1)) for i in lons for k in range(0, lat_count, 2)]))
    between = both_ways([(at(i, k), at(i, k + 1)) for i in lons for k in range(1, lat_count - 1, 2)])
    across = [(at(i, 0), at(i + lon_count // 2, 0)) for i in lons]
    return pair, lax.ppermute(row(odd), ALL, between + across)


def column_halos(parts, width, lon_count, lat_count):
    at = lambda lon, lat: (lon % lon_count) * lat_count + lat
    core = lax.axis_index("core")

    def edge(start):
        return jnp.concatenate([lax.dynamic_slice_in_dim(a, start, SPAN, 3) for a in parts], axis=2)

    reach = width - SPAN
    places = [(i, k) for i in range(0, lon_count, 2) for k in range(lat_count)]
    next_chip = lax.ppermute(edge(core * reach), ALL, both_ways([(at(i + 1, k), at(i + 2, k)) for i, k in places]))
    in_chip = lax.ppermute(edge((1 - core) * reach), "core", [(0, 1), (1, 0)])
    return in_chip, next_chip


def ordered(pair, next_pair):
    odd = lax.rem(lax.axis_index(("x", "yh")), 2) == 1
    return jnp.where(odd, pair, next_pair)[:, :, None], jnp.where(odd, next_pair, pair)[:, :, None]


def folded(count, cores, reach):
    pairs = []
    for i in range(count):
        for core in range(cores):
            turn = 2 * core
            base = (i + turn) % count
            partner = base ^ (reach - 1 if reach == count else reach // 2)
            pairs.append((i * cores + core, (partner - turn) % count * cores + core))
    return pairs


def local(features, out_grad, first_kernel, second_kernel, strides):
    slabs, rows, width, chans = features.shape
    lat_axes, lon_axes = ("x", "yh"), ("yl", "z", "core")
    lat_count, lon_count = lax.axis_size(lat_axes), lax.axis_size(lon_axes)
    lat, core = lax.axis_index(lat_axes), lax.axis_index("core")
    where = jnp.stack([lat, core, lax.rem(lat, 2)]).astype(jnp.int32)
    smem = pl.BlockSpec(memory_space=pltpu.SMEM)
    vmem = pl.BlockSpec(memory_space=pltpu.VMEM)
    anywhere = pl.BlockSpec(memory_space=pl.ANY)
    cells = slabs * rows * width
    ext = pltpu.VMEM((slabs * (rows + 2), width + 2 * SPAN + 8, chans), jnp.float32)
    taps = pltpu.VMEM((9, cells, chans), jnp.bfloat16)
    params = pltpu.CompilerParams(vmem_limit_bytes=24 * 1024 * 1024)
    grads = (9 * chans, chans)
    swap = [(0, 1), (1, 0)]

    fields = jnp.stack([features, out_grad])
    rows_around = row_halos(fields, lon_count, lat_count)
    own_columns = column_halos([fields], width, lon_count, lat_count)
    ext_rows = pltpu.VMEM((2 * slabs, width + 2 * SPAN + 8, chans), jnp.float32)
    half = slabs * width
    early = pl.pallas_call(
        early_kernel,
        out_shape=[jax.ShapeDtypeStruct((3 * len(OWN), half, chans), jnp.bfloat16)] * 2
        + [jax.ShapeDtypeStruct((cells, chans), jnp.float32)] * 2,
        in_specs=[smem, smem] + [vmem] * 6,
        out_specs=[vmem] * 4,
        scratch_shapes=[ext_rows, ext_rows],
        compiler_params=params,
        name="early",
    )(where, strides, features, out_grad, *own_columns, first_kernel, second_kernel)
    early, rows_around = lax.optimization_barrier((early, rows_around))
    corners = column_halos(ordered(*rows_around), width, lon_count, lat_count)
    edge = pltpu.VMEM((6, half, chans), jnp.bfloat16)
    keep, send, pre_grad = pl.pallas_call(
        main_kernel,
        out_shape=[
            jax.ShapeDtypeStruct(grads, jnp.float32),
            jax.ShapeDtypeStruct(grads, jnp.bfloat16),
            jax.ShapeDtypeStruct(features.shape, jnp.bfloat16),
        ],
        in_specs=[smem, smem] + [vmem] * 10,
        out_specs=[vmem] * 3,
        scratch_shapes=[
            ext_rows,
            ext_rows,
            edge,
            edge,
            pltpu.VMEM((cells, chans), jnp.bfloat16),
            pltpu.VMEM((2,) + grads, jnp.float32),
        ],
        compiler_params=params,
        name="main",
    )(where, strides, *early, *rows_around, *corners, first_kernel, second_kernel)

    total = keep + lax.ppermute(send, "core", swap).astype(jnp.float32)
    planes, height, cores = lax.axis_size(PLANE), lax.axis_size("z"), lax.axis_size("core")
    total = total.astype(jnp.bfloat16).reshape(planes, 9 * chans // planes, chans)
    pre_field = pre_grad[None]
    pair, next_pair = row_halos(pre_field, lon_count, lat_count)
    total, pair = lax.optimization_barrier((total, pair))
    spread = lax.all_to_all(total, PLANE, 0, 0, tiled=True)

    spread, next_pair = lax.optimization_barrier((spread, next_pair))
    part = jnp.sum(spread.astype(jnp.float32), axis=0)
    reach = 2
    while reach <= height:
        got = lax.ppermute(part, ("z", "core"), folded(height, cores, reach))
        if reach < height:
            part = part + got
        reach *= 2
    got, pair, pre_field = lax.optimization_barrier((got, pair, pre_field))
    above, below = ordered(pair, next_pair)
    around = (pair, next_pair) + column_halos([above, pre_field, below], width, lon_count, lat_count)
    input_grad = pl.pallas_call(
        back_kernel,
        out_shape=jax.ShapeDtypeStruct(features.shape, jnp.bfloat16),
        in_specs=[smem, smem] + [vmem] * 7,
        out_specs=vmem,
        scratch_shapes=[ext, taps],
        compiler_params=params,
        name="back",
    )(where, strides, out_grad, pre_grad, *around, first_kernel)

    copies = pl.pallas_call(
        copies_kernel,
        out_shape=jax.ShapeDtypeStruct((planes,) + part.shape, jnp.bfloat16),
        in_specs=[vmem] * 2,
        out_specs=vmem,
        compiler_params=params,
        name="copies",
    )(part, got)
    mine = lax.all_to_all(copies, PLANE, 0, 0, tiled=True).reshape(grads)
    mine, input_grad = lax.optimization_barrier((mine, input_grad))
    other = lax.ppermute(mine, "core", swap)
    scale = 1.0 / math.sqrt(cells * lat_count * lon_count)
    wide = [jax.ShapeDtypeStruct(grads, jnp.float32)] * 2
    scratch = [pltpu.VMEM(grads, jnp.float32), pltpu.SemaphoreType.DMA((6,))]
    sides = pl.pallas_call(
        lambda *refs: part_kernel(scale, 0, *refs),
        out_shape=wide,
        in_specs=[smem, vmem],
        out_specs=[anywhere] * 2,
        scratch_shapes=scratch,
        compiler_params=params,
        name="own_part",
    )(where, mine)
    first, second = pl.pallas_call(
        lambda *refs: part_kernel(scale, 1, *refs),
        out_shape=wide,
        in_specs=[smem, vmem, anywhere, anywhere],
        out_specs=[anywhere] * 2,
        scratch_shapes=scratch,
        input_output_aliases={2: 0, 3: 1},
        compiler_params=params,
        name="other_part",
    )(where, other, *sides)
    return input_grad, first.reshape(first_kernel.shape), second.reshape(first_kernel.shape)


def solution(mesh):
    wide = Mesh(mesh.devices.reshape(2, 8, 2, 4, 2), ALL)
    field = P(None, ("x", "yh"), ("yl", "z", "core"), None)
    return jax.shard_map(
        local,
        mesh=wide,
        in_specs=(field, field, P(), P(), P()),
        out_specs=(field, P(), P()),
        check_vma=False,
    )
```

```python
import math

import jax
import jax.numpy as jnp
from jax import lax
from jax.experimental import pallas as pl
from jax.experimental.pallas import tpu as pltpu
from jax.sharding import Mesh
from jax.sharding import PartitionSpec as P

POLE = 16
SPAN = 16
ALL = ("yl", "z", "core", "x", "yh")
PLANE = ("x", "yh", "yl")
NN = (((1,), (0,)), ((), ()))
NT = (((1,), (1,)), ((), ()))
TN = (((0,), (0,)), ((), ()))
ROOT = math.sqrt(2.0 / math.pi)
CUBIC = 0.044715


def dot(a, b, dims):
    return lax.dot_general(a, b, dims, preferred_element_type=jnp.float32)


def fill(ext, field, own, halo, where):
    pair, next_pair, in_chip, next_chip = halo
    width = own.shape[2]
    odd, core = where[2] == 1, where[1] == 1
    for s in range(2):
        for row in range(4):
            place = ext.at[s * 4 + row]
            if row in (0, 3):
                one, other = pair[field, s].astype(jnp.float32), next_pair[field, s].astype(jnp.float32)
                middle = jnp.where(odd, one, other) if row == 0 else jnp.where(odd, other, one)
            else:
                middle = own[s, row - 1].astype(jnp.float32)
            near, far = in_chip[field, s, row].astype(jnp.float32), next_chip[field, s, row].astype(jnp.float32)
            place[:SPAN] = jnp.where(core, near, far)
            place[SPAN : SPAN + width] = middle
            place[SPAN + width : 2 * SPAN + width] = jnp.where(core, far, near)


def tap(ext, s, row, shift, width):
    if isinstance(shift, int):
        return ext[s * 4 + row, SPAN + shift : SPAN + shift + width, :].astype(jnp.bfloat16)
    start = SPAN + shift
    rest = lax.rem(start, 8)
    span = ext[s * 4 + row, pl.ds(pl.multiple_of(start - rest, 8), width + 8), :]
    chans = span.shape[-1]
    turned = pltpu.roll(span.reshape(width // 8 + 1, 8, chans), lax.rem(8 - rest, 8), 1)
    lane = lax.broadcasted_iota(jnp.int32, (1, 8, chans), 1)
    moved = jnp.where(lane < 8 - rest, turned[:-1], turned[1:])
    return moved.reshape(width, chans).astype(jnp.bfloat16)


def adjoint_stride(strides, s, row, slot, lat):
    here = lat * 2 + row
    if slot == 0:
        if row == 1:
            return strides[s, lat * 2, 2]
        return jnp.where(lat == 0, strides[s, 0, 0], strides[s, jnp.maximum(here - 1, 0), 2])
    if slot == 1:
        return strides[s, here, 1]
    return strides[s, jnp.minimum(here + 1, POLE - 1), 0]


def adjoint_taps(ext, taps, strides, lat, width):
    for row in range(2):
        for s in range(2):
            at = (row * 2 + s) * width
            for slot in range(3):
                stride = adjoint_stride(strides, s, row, slot, lat)
                for col in range(3):
                    shift = 0 if col == 1 else -(col - 1) * stride
                    taps[slot * 3 + col, at : at + width] = tap(ext, s, row + slot, shift, width)


def adjoint_product(taps, kernel, mirror, row, half):
    total = None
    at = row * half
    for slot in range(3):
        for col in range(3):
            weight = kernel[2 - slot, col]
            if slot == 0 and row == 0:
                weight = jnp.where(mirror, kernel[0, col], weight)
            term = dot(taps[slot * 3 + col, at : at + half], weight, NT)
            total = term if total is None else total + term
    return total


OWN = ((0, 1), (0, 2), (1, 0), (1, 1))


def stretch(place, middle, near, far, core):
    width = middle.shape[0]
    near, far = near.astype(jnp.float32), far.astype(jnp.float32)
    place[:SPAN] = jnp.where(core, near, far)
    place[SPAN : SPAN + width] = middle.astype(jnp.float32)
    place[SPAN + width : 2 * SPAN + width] = jnp.where(core, far, near)


def moved(ext, at, shift, width):
    return tap(ext, at // 4, at % 4, shift, width)


def early_kernel(where, strides, feat, grad, in_chip, next_chip, first_kernel, second_kernel,
                 taps_f, taps_g, pre_part, back_part, ext_f, ext_g):
    lat, core = where[0], where[1] == 1
    width = feat.shape[2]
    half = 2 * width
    for field, own, ext in ((0, feat, ext_f), (1, grad, ext_g)):
        for s in range(2):
            for row in range(2):
                stretch(ext.at[s * 2 + row], own[s, row], in_chip[field, s, row], next_chip[field, s, row], core)
    for i, (row, k) in enumerate(OWN):
        for s in range(2):
            ahead, behind = strides[s, lat * 2 + row, k], adjoint_stride(strides, s, row, k, lat)
            at, cells = s * 2 + row + k - 1, slice(s * width, (s + 1) * width)
            for col in range(3):
                taps_f[i * 3 + col, cells] = moved(ext_f, at, 0 if col == 1 else (col - 1) * ahead, width)
                taps_g[i * 3 + col, cells] = moved(ext_g, at, 0 if col == 1 else (1 - col) * behind, width)
    for row in range(2):
        pre, back = None, None
        for i, (at, k) in enumerate(OWN):
            if at != row:
                continue
            for col in range(3):
                term = dot(taps_f[i * 3 + col], first_kernel[k, col], NN)
                pre = term if pre is None else pre + term
                term = dot(taps_g[i * 3 + col], second_kernel[2 - k, col], NT)
                back = term if back is None else back + term
        pre_part[row * half : (row + 1) * half] = pre
        back_part[row * half : (row + 1) * half] = back


def main_kernel(where, strides, own_f, own_g, pre_part, back_part, pair, next_pair, in_chip, next_chip,
                first_kernel, second_kernel, keep, send, pre_grad, ext_f, ext_g, edge_f, edge_g, act):
    lat, core = where[0], where[1]
    odd, second_core = where[2] == 1, core == 1
    mirror = lat == 0
    width = pair.shape[2]
    half = 2 * width
    for field, ext in ((0, ext_f), (1, ext_g)):
        for s in range(2):
            one, other = pair[field, s], next_pair[field, s]
            for row in range(2):
                middle = jnp.where(odd, one, other) if row == 0 else jnp.where(odd, other, one)
                stretch(ext.at[s * 2 + row], middle, in_chip[field, s, row], next_chip[field, s, row], second_core)
    for row in range(2):
        for s in range(2):
            ahead, behind = strides[s, lat * 2 + row, 2 * row], adjoint_stride(strides, s, row, 2 * row, lat)
            cells = slice(s * width, (s + 1) * width)
            for col in range(3):
                edge_f[row * 3 + col, cells] = moved(ext_f, s * 2 + row, 0 if col == 1 else (col - 1) * ahead, width)
                edge_g[row * 3 + col, cells] = moved(ext_g, s * 2 + row, 0 if col == 1 else (1 - col) * behind, width)

    for row in range(2):
        at = slice(row * half, (row + 1) * half)
        pre, back = pre_part[at], back_part[at]
        for col in range(3):
            pre += dot(edge_f[row * 3 + col], first_kernel[2 * row, col], NN)
            weight = second_kernel[2 - 2 * row, col]
            if row == 0:
                weight = jnp.where(mirror, second_kernel[0, col], weight)
            back += dot(edge_g[row * 3 + col], weight, NT)
        square = pre * pre
        bend = jnp.tanh(ROOT * (pre + CUBIC * (pre * square)))
        act[at] = (0.5 * pre * (1.0 + bend)).astype(jnp.bfloat16)
        slope = 0.5 * (1.0 + bend) + 0.5 * pre * (1.0 - bend * bend) * (ROOT * (1.0 + 3.0 * CUBIC * square))
        result = (back * slope).astype(jnp.bfloat16)
        for s in range(2):
            pre_grad[s, row] = result[s * width : (s + 1) * width]

    def taps_of(own, edge, row, k, col):
        return own[OWN.index((row, k)) * 3 + col] if (row, k) in OWN else edge[row * 3 + col]

    rows = [jnp.concatenate([pre_grad[s, row] for s in range(2)], axis=0) for row in range(2)]

    def products(first, second):
        def place(out, value, k, col):
            at = (k * 3 + col) * 256
            out[at : at + 256] = value.astype(out.dtype)

        turned = act[...].T
        above, below = turned[:, :half], turned[:, half:]
        for col in range(3):
            edge, upper = (dot(a, taps_of(own_g, edge_g, r, 0, col), NN) for r, a in enumerate((above, below)))
            centre, lower = (
                sum(dot(a, taps_of(own_g, edge_g, r, slot, col), NN) for r, a in enumerate((above, below))) for slot in (1, 2)
            )
            place(second, centre, 1, col)
            place(second, lower + jnp.where(mirror, edge, 0.0), 0, col)
            place(second, upper + jnp.where(mirror, 0.0, edge), 2, col)
        for k in range(3):
            for col in range(3):
                place(first, sum(dot(taps_of(own_f, edge_f, r, k, col), rows[r], TN) for r in range(2)), k, col)

    pl.when(core == 0)(lambda: products(keep, send))
    pl.when(core != 0)(lambda: products(send, keep))


def back_kernel(where, strides, grad, pre, pair, next_pair, in_chip, next_chip, first_kernel, out, ext, taps):
    lat = where[0]
    mirror = lat == 0
    width = grad.shape[2]
    fill(ext, 0, pre, (pair, next_pair, in_chip, next_chip), where)
    adjoint_taps(ext, taps, strides, lat, width)
    for row in range(2):
        total = adjoint_product(taps, first_kernel, mirror, row, 2 * width)
        for s in range(2):
            own = grad[s, row].astype(jnp.float32)
            out[s, row] = (own + total[s * width : (s + 1) * width]).astype(jnp.bfloat16)


def part_kernel(scale, owner, where, given, *refs):
    first, second, held, sems = refs[-4:]
    count = sems.shape[0]
    step = given.shape[0] // count
    rows = [pl.ds(i * step, step) for i in range(count)]
    to_first = where[1] == owner

    def every(act_on):
        for i, at in enumerate(rows):
            act_on(i, at)

    def write(out):
        def one(i, at):
            held[at] = given[at].astype(jnp.float32) * scale
            pltpu.make_async_copy(held.at[at], out.at[at], sems.at[i]).start()

        every(one)
        every(lambda i, at: pltpu.make_async_copy(held.at[at], out.at[at], sems.at[i]).wait())

    pl.when(to_first)(lambda: write(first))
    pl.when(jnp.logical_not(to_first))(lambda: write(second))


def copies_kernel(part, got, out):
    value = (part[...] + got[...]).astype(jnp.bfloat16)
    for i in range(out.shape[0]):
        out[i] = value


def both_ways(pairs):
    return pairs + [(b, a) for a, b in pairs]


def row_halos(fields, lon_count, lat_count):
    at = lambda lon, lat: (lon % lon_count) * lat_count + lat
    lons = range(lon_count)
    odd = lax.rem(lax.axis_index(("x", "yh")), 2)
    row = lambda i: lax.dynamic_index_in_dim(fields, i, 2, keepdims=False)
    pair = lax.ppermute(row(1 - odd), ALL, both_ways([(at(i, k), at(i, k + 1)) for i in lons for k in range(0, lat_count, 2)]))
    between = both_ways([(at(i, k), at(i, k + 1)) for i in lons for k in range(1, lat_count - 1, 2)])
    across = [(at(i, 0), at(i + lon_count // 2, 0)) for i in lons]
    return pair, lax.ppermute(row(odd), ALL, between + across)


def column_halos(parts, width, lon_count, lat_count):
    at = lambda lon, lat: (lon % lon_count) * lat_count + lat
    core = lax.axis_index("core")

    def edge(start):
        return jnp.concatenate([lax.dynamic_slice_in_dim(a, start, SPAN, 3) for a in parts], axis=2)

    reach = width - SPAN
    places = [(i, k) for i in range(0, lon_count, 2) for k in range(lat_count)]
    next_chip = lax.ppermute(edge(core * reach), ALL, both_ways([(at(i + 1, k), at(i + 2, k)) for i, k in places]))
    in_chip = lax.ppermute(edge((1 - core) * reach), "core", [(0, 1), (1, 0)])
    return in_chip, next_chip


def ordered(pair, next_pair):
    odd = lax.rem(lax.axis_index(("x", "yh")), 2) == 1
    return jnp.where(odd, pair, next_pair)[:, :, None], jnp.where(odd, next_pair, pair)[:, :, None]


def folded(count, cores, reach):
    pairs = []
    for i in range(count):
        for core in range(cores):
            turn = 2 * core
            base = (i + turn) % count
            partner = base ^ (reach - 1 if reach == count else reach // 2)
            pairs.append((i * cores + core, (partner - turn) % count * cores + core))
    return pairs


def local(features, out_grad, first_kernel, second_kernel, strides):
    slabs, rows, width, chans = features.shape
    lat_axes, lon_axes = ("x", "yh"), ("yl", "z", "core")
    lat_count, lon_count = lax.axis_size(lat_axes), lax.axis_size(lon_axes)
    lat, core = lax.axis_index(lat_axes), lax.axis_index("core")
    where = jnp.stack([lat, core, lax.rem(lat, 2)]).astype(jnp.int32)
    smem = pl.BlockSpec(memory_space=pltpu.SMEM)
    vmem = pl.BlockSpec(memory_space=pltpu.VMEM)
    anywhere = pl.BlockSpec(memory_space=pl.ANY)
    cells = slabs * rows * width
    ext = pltpu.VMEM((slabs * (rows + 2), width + 2 * SPAN + 8, chans), jnp.float32)
    taps = pltpu.VMEM((9, cells, chans), jnp.bfloat16)
    params = pltpu.CompilerParams(vmem_limit_bytes=24 * 1024 * 1024)
    grads = (9 * chans, chans)
    swap = [(0, 1), (1, 0)]

    fields = jnp.stack([features, out_grad])
    rows_around = row_halos(fields, lon_count, lat_count)
    own_columns = column_halos([fields], width, lon_count, lat_count)
    ext_rows = pltpu.VMEM((2 * slabs, width + 2 * SPAN + 8, chans), jnp.float32)
    half = slabs * width
    early = pl.pallas_call(
        early_kernel,
        out_shape=[jax.ShapeDtypeStruct((3 * len(OWN), half, chans), jnp.bfloat16)] * 2
        + [jax.ShapeDtypeStruct((cells, chans), jnp.float32)] * 2,
        in_specs=[smem, smem] + [vmem] * 6,
        out_specs=[vmem] * 4,
        scratch_shapes=[ext_rows, ext_rows],
        compiler_params=params,
        name="early",
    )(where, strides, features, out_grad, *own_columns, first_kernel, second_kernel)
    early, rows_around = lax.optimization_barrier((early, rows_around))
    corners = column_halos(ordered(*rows_around), width, lon_count, lat_count)
    edge = pltpu.VMEM((6, half, chans), jnp.bfloat16)
    keep, send, pre_grad = pl.pallas_call(
        main_kernel,
        out_shape=[
            jax.ShapeDtypeStruct(grads, jnp.float32),
            jax.ShapeDtypeStruct(grads, jnp.bfloat16),
            jax.ShapeDtypeStruct(features.shape, jnp.bfloat16),
        ],
        in_specs=[smem, smem] + [vmem] * 10,
        out_specs=[vmem] * 3,
        scratch_shapes=[
            ext_rows,
            ext_rows,
            edge,
            edge,
            pltpu.VMEM((cells, chans), jnp.bfloat16),
        ],
        compiler_params=params,
        name="main",
    )(where, strides, *early, *rows_around, *corners, first_kernel, second_kernel)

    total = keep + lax.ppermute(send, "core", swap).astype(jnp.float32)
    planes, height, cores = lax.axis_size(PLANE), lax.axis_size("z"), lax.axis_size("core")
    total = total.astype(jnp.bfloat16).reshape(planes, 9 * chans // planes, chans)
    spread = lax.all_to_all(total, PLANE, 0, 0, tiled=True)

    spread, pre_grad = lax.optimization_barrier((spread, pre_grad))
    pre_field = pre_grad[None]
    pair, next_pair = row_halos(pre_field, lon_count, lat_count)
    part = jnp.sum(spread.astype(jnp.float32), axis=0)
    reach = 2
    while reach <= height:
        got = lax.ppermute(part, ("z", "core"), folded(height, cores, reach))
        if reach < height:
            part = part + got
        reach *= 2
        if reach == height:
            part, pair = lax.optimization_barrier((part, pair))
    got, next_pair = lax.optimization_barrier((got, next_pair))
    above, below = ordered(pair, next_pair)
    around = (pair, next_pair) + column_halos([above, pre_field, below], width, lon_count, lat_count)
    input_grad = pl.pallas_call(
        back_kernel,
        out_shape=jax.ShapeDtypeStruct(features.shape, jnp.bfloat16),
        in_specs=[smem, smem] + [vmem] * 7,
        out_specs=vmem,
        scratch_shapes=[ext, taps],
        compiler_params=params,
        name="back",
    )(where, strides, out_grad, pre_grad, *around, first_kernel)

    copies = pl.pallas_call(
        copies_kernel,
        out_shape=jax.ShapeDtypeStruct((planes,) + part.shape, jnp.bfloat16),
        in_specs=[vmem] * 2,
        out_specs=vmem,
        compiler_params=params,
        name="copies",
    )(part, got)
    mine = lax.all_to_all(copies, PLANE, 0, 0, tiled=True).reshape(grads)
    mine, input_grad = lax.optimization_barrier((mine, input_grad))
    other = lax.ppermute(mine, "core", swap)
    scale = 1.0 / math.sqrt(cells * lat_count * lon_count)
    wide = [jax.ShapeDtypeStruct(grads, jnp.float32)] * 2
    scratch = [pltpu.VMEM(grads, jnp.float32), pltpu.SemaphoreType.DMA((6,))]
    sides = pl.pallas_call(
        lambda *refs: part_kernel(scale, 0, *refs),
        out_shape=wide,
        in_specs=[smem, vmem],
        out_specs=[anywhere] * 2,
        scratch_shapes=scratch,
        compiler_params=params,
        name="own_part",
    )(where, mine)
    first, second = pl.pallas_call(
        lambda *refs: part_kernel(scale, 1, *refs),
        out_shape=wide,
        in_specs=[smem, vmem, anywhere, anywhere],
        out_specs=[anywhere] * 2,
        scratch_shapes=scratch,
        input_output_aliases={2: 0, 3: 1},
        compiler_params=params,
        name="other_part",
    )(where, other, *sides)
    return input_grad, first.reshape(first_kernel.shape), second.reshape(first_kernel.shape)


def solution(mesh):
    wide = Mesh(mesh.devices.reshape(2, 8, 2, 4, 2), ALL)
    field = P(None, ("x", "yh"), ("yl", "z", "core"), None)
    return jax.shard_map(
        local,
        mesh=wide,
        in_specs=(field, field, P(), P(), P()),
        out_specs=(field, P(), P()),
        check_vma=False,
    )
```

```python
import math

import jax
import jax.numpy as jnp
from jax import lax
from jax.experimental import pallas as pl
from jax.experimental.pallas import tpu as pltpu
from jax.sharding import Mesh
from jax.sharding import PartitionSpec as P

POLE = 16
SPAN = 16
ALL = ("yl", "z", "core", "x", "yh")
PLANE = ("x", "yh", "yl")
NN = (((1,), (0,)), ((), ()))
NT = (((1,), (1,)), ((), ()))
TN = (((0,), (0,)), ((), ()))
ROOT = math.sqrt(2.0 / math.pi)
CUBIC = 0.044715


def dot(a, b, dims):
    return lax.dot_general(a, b, dims, preferred_element_type=jnp.float32)


def fill(ext, field, own, halo, where):
    pair, next_pair, in_chip, next_chip = halo
    width = own.shape[2]
    odd, core = where[2] == 1, where[1] == 1
    for s in range(2):
        for row in range(4):
            place = ext.at[s * 4 + row]
            if row in (0, 3):
                one, other = pair[field, s].astype(jnp.float32), next_pair[field, s].astype(jnp.float32)
                middle = jnp.where(odd, one, other) if row == 0 else jnp.where(odd, other, one)
            else:
                middle = own[s, row - 1].astype(jnp.float32)
            near, far = in_chip[field, s, row].astype(jnp.float32), next_chip[field, s, row].astype(jnp.float32)
            place[:SPAN] = jnp.where(core, near, far)
            place[SPAN : SPAN + width] = middle
            place[SPAN + width : 2 * SPAN + width] = jnp.where(core, far, near)


def tap(ext, s, row, shift, width):
    if isinstance(shift, int):
        return ext[s * 4 + row, SPAN + shift : SPAN + shift + width, :].astype(jnp.bfloat16)
    start = SPAN + shift
    rest = lax.rem(start, 8)
    span = ext[s * 4 + row, pl.ds(pl.multiple_of(start - rest, 8), width + 8), :]
    chans = span.shape[-1]
    turned = pltpu.roll(span.reshape(width // 8 + 1, 8, chans), lax.rem(8 - rest, 8), 1)
    lane = lax.broadcasted_iota(jnp.int32, (1, 8, chans), 1)
    moved = jnp.where(lane < 8 - rest, turned[:-1], turned[1:])
    return moved.reshape(width, chans).astype(jnp.bfloat16)


def adjoint_stride(strides, s, row, slot, lat):
    here = lat * 2 + row
    if slot == 0:
        if row == 1:
            return strides[s, lat * 2, 2]
        return jnp.where(lat == 0, strides[s, 0, 0], strides[s, jnp.maximum(here - 1, 0), 2])
    if slot == 1:
        return strides[s, here, 1]
    return strides[s, jnp.minimum(here + 1, POLE - 1), 0]


def adjoint_taps(ext, taps, strides, lat, width):
    for row in range(2):
        for s in range(2):
            at = (row * 2 + s) * width
            for slot in range(3):
                stride = adjoint_stride(strides, s, row, slot, lat)
                for col in range(3):
                    shift = 0 if col == 1 else -(col - 1) * stride
                    taps[slot * 3 + col, at : at + width] = tap(ext, s, row + slot, shift, width)


def adjoint_product(taps, kernel, mirror, row, half):
    total = None
    at = row * half
    for slot in range(3):
        for col in range(3):
            weight = kernel[2 - slot, col]
            if slot == 0 and row == 0:
                weight = jnp.where(mirror, kernel[0, col], weight)
            term = dot(taps[slot * 3 + col, at : at + half], weight, NT)
            total = term if total is None else total + term
    return total


OWN = ((0, 1), (0, 2), (1, 0), (1, 1))


def stretch(place, middle, near, far, core):
    width = middle.shape[0]
    near, far = near.astype(jnp.float32), far.astype(jnp.float32)
    place[:SPAN] = jnp.where(core, near, far)
    place[SPAN : SPAN + width] = middle.astype(jnp.float32)
    place[SPAN + width : 2 * SPAN + width] = jnp.where(core, far, near)


def moved(ext, at, shift, width):
    return tap(ext, at // 4, at % 4, shift, width)


def early_kernel(where, strides, feat, grad, in_chip, next_chip, first_kernel, second_kernel,
                 taps_f, taps_g, pre_part, back_part, ext_f, ext_g):
    lat, core = where[0], where[1] == 1
    width = feat.shape[2]
    half = 2 * width
    for field, own, ext in ((0, feat, ext_f), (1, grad, ext_g)):
        for s in range(2):
            for row in range(2):
                stretch(ext.at[s * 2 + row], own[s, row], in_chip[field, s, row], next_chip[field, s, row], core)
    for i, (row, k) in enumerate(OWN):
        for s in range(2):
            ahead, behind = strides[s, lat * 2 + row, k], adjoint_stride(strides, s, row, k, lat)
            at, cells = s * 2 + row + k - 1, slice(s * width, (s + 1) * width)
            for col in range(3):
                taps_f[i * 3 + col, cells] = moved(ext_f, at, 0 if col == 1 else (col - 1) * ahead, width)
                taps_g[i * 3 + col, cells] = moved(ext_g, at, 0 if col == 1 else (1 - col) * behind, width)
    for row in range(2):
        pre, back = None, None
        for i, (at, k) in enumerate(OWN):
            if at != row:
                continue
            for col in range(3):
                term = dot(taps_f[i * 3 + col], first_kernel[k, col], NN)
                pre = term if pre is None else pre + term
                term = dot(taps_g[i * 3 + col], second_kernel[2 - k, col], NT)
                back = term if back is None else back + term
        pre_part[row * half : (row + 1) * half] = pre
        back_part[row * half : (row + 1) * half] = back


def main_kernel(where, strides, own_f, own_g, pre_part, back_part, pair, next_pair, in_chip, next_chip,
                first_kernel, second_kernel, keep, send, pre_grad, ext_f, ext_g, edge_f, edge_g, act):
    lat, core = where[0], where[1]
    odd, second_core = where[2] == 1, core == 1
    mirror = lat == 0
    width = pair.shape[2]
    half = 2 * width
    for field, ext in ((0, ext_f), (1, ext_g)):
        for s in range(2):
            one, other = pair[field, s], next_pair[field, s]
            for row in range(2):
                middle = jnp.where(odd, one, other) if row == 0 else jnp.where(odd, other, one)
                stretch(ext.at[s * 2 + row], middle, in_chip[field, s, row], next_chip[field, s, row], second_core)
    for row in range(2):
        for s in range(2):
            ahead, behind = strides[s, lat * 2 + row, 2 * row], adjoint_stride(strides, s, row, 2 * row, lat)
            cells = slice(s * width, (s + 1) * width)
            for col in range(3):
                edge_f[row * 3 + col, cells] = moved(ext_f, s * 2 + row, 0 if col == 1 else (col - 1) * ahead, width)
                edge_g[row * 3 + col, cells] = moved(ext_g, s * 2 + row, 0 if col == 1 else (1 - col) * behind, width)

    for row in range(2):
        at = slice(row * half, (row + 1) * half)
        pre, back = pre_part[at], back_part[at]
        for col in range(3):
            pre += dot(edge_f[row * 3 + col], first_kernel[2 * row, col], NN)
            weight = second_kernel[2 - 2 * row, col]
            if row == 0:
                weight = jnp.where(mirror, second_kernel[0, col], weight)
            back += dot(edge_g[row * 3 + col], weight, NT)
        square = pre * pre
        bend = jnp.tanh(ROOT * (pre + CUBIC * (pre * square)))
        act[at] = (0.5 * pre * (1.0 + bend)).astype(jnp.bfloat16)
        slope = 0.5 * (1.0 + bend) + 0.5 * pre * (1.0 - bend * bend) * (ROOT * (1.0 + 3.0 * CUBIC * square))
        result = (back * slope).astype(jnp.bfloat16)
        for s in range(2):
            pre_grad[s, row] = result[s * width : (s + 1) * width]

    def taps_of(own, edge, row, k, col):
        return own[OWN.index((row, k)) * 3 + col] if (row, k) in OWN else edge[row * 3 + col]

    rows = [jnp.concatenate([pre_grad[s, row] for s in range(2)], axis=0) for row in range(2)]

    def products(first, second):
        def place(out, value, k, col):
            at = (k * 3 + col) * 256
            out[at : at + 256] = value.astype(out.dtype)

        turned = act[...].T
        above, below = turned[:, :half], turned[:, half:]
        for col in range(3):
            edge, upper = (dot(a, taps_of(own_g, edge_g, r, 0, col), NN) for r, a in enumerate((above, below)))
            centre, lower = (
                sum(dot(a, taps_of(own_g, edge_g, r, slot, col), NN) for r, a in enumerate((above, below))) for slot in (1, 2)
            )
            place(second, centre, 1, col)
            place(second, lower + jnp.where(mirror, edge, 0.0), 0, col)
            place(second, upper + jnp.where(mirror, 0.0, edge), 2, col)
        for k in range(3):
            for col in range(3):
                place(first, sum(dot(taps_of(own_f, edge_f, r, k, col), rows[r], TN) for r in range(2)), k, col)

    pl.when(core == 0)(lambda: products(keep, send))
    pl.when(core != 0)(lambda: products(send, keep))


def back_kernel(where, strides, grad, pre, pair, next_pair, in_chip, next_chip, first_kernel, out, ext, taps):
    lat = where[0]
    mirror = lat == 0
    width = grad.shape[2]
    fill(ext, 0, pre, (pair, next_pair, in_chip, next_chip), where)
    adjoint_taps(ext, taps, strides, lat, width)
    for row in range(2):
        total = adjoint_product(taps, first_kernel, mirror, row, 2 * width)
        for s in range(2):
            own = grad[s, row].astype(jnp.float32)
            out[s, row] = (own + total[s * width : (s + 1) * width]).astype(jnp.bfloat16)


def part_kernel(scale, owner, where, given, *refs):
    first, second, held, sems = refs[-4:]
    count = sems.shape[0]
    step = given.shape[0] // count
    rows = [pl.ds(i * step, step) for i in range(count)]
    to_first = where[1] == owner

    def every(act_on):
        for i, at in enumerate(rows):
            act_on(i, at)

    def write(out):
        def one(i, at):
            held[at] = given[at].astype(jnp.float32) * scale
            pltpu.make_async_copy(held.at[at], out.at[at], sems.at[i]).start()

        every(one)
        every(lambda i, at: pltpu.make_async_copy(held.at[at], out.at[at], sems.at[i]).wait())

    pl.when(to_first)(lambda: write(first))
    pl.when(jnp.logical_not(to_first))(lambda: write(second))


def copies_kernel(part, got, out):
    value = (part[...] + got[...]).astype(jnp.bfloat16)
    for i in range(out.shape[0]):
        out[i] = value


def both_ways(pairs):
    return pairs + [(b, a) for a, b in pairs]


def row_halos(fields, lon_count, lat_count):
    at = lambda lon, lat: (lon % lon_count) * lat_count + lat
    lons = range(lon_count)
    odd = lax.rem(lax.axis_index(("x", "yh")), 2)
    row = lambda i: lax.dynamic_index_in_dim(fields, i, 2, keepdims=False)
    pair = lax.ppermute(row(1 - odd), ALL, both_ways([(at(i, k), at(i, k + 1)) for i in lons for k in range(0, lat_count, 2)]))
    between = both_ways([(at(i, k), at(i, k + 1)) for i in lons for k in range(1, lat_count - 1, 2)])
    across = [(at(i, 0), at(i + lon_count // 2, 0)) for i in lons]
    return pair, lax.ppermute(row(odd), ALL, between + across)


def column_halos(parts, width, lon_count, lat_count):
    at = lambda lon, lat: (lon % lon_count) * lat_count + lat
    core = lax.axis_index("core")

    def edge(start):
        return jnp.concatenate([lax.dynamic_slice_in_dim(a, start, SPAN, 3) for a in parts], axis=2)

    reach = width - SPAN
    places = [(i, k) for i in range(0, lon_count, 2) for k in range(lat_count)]
    next_chip = lax.ppermute(edge(core * reach), ALL, both_ways([(at(i + 1, k), at(i + 2, k)) for i, k in places]))
    in_chip = lax.ppermute(edge((1 - core) * reach), "core", [(0, 1), (1, 0)])
    return in_chip, next_chip


def ordered(pair, next_pair):
    odd = lax.rem(lax.axis_index(("x", "yh")), 2) == 1
    return jnp.where(odd, pair, next_pair)[:, :, None], jnp.where(odd, next_pair, pair)[:, :, None]


def folded(count, cores, reach):
    pairs = []
    for i in range(count):
        for core in range(cores):
            turn = 2 * core
            base = (i + turn) % count
            partner = base ^ (reach - 1 if reach == count else reach // 2)
            pairs.append((i * cores + core, (partner - turn) % count * cores + core))
    return pairs


def local(features, out_grad, first_kernel, second_kernel, strides):
    slabs, rows, width, chans = features.shape
    lat_axes, lon_axes = ("x", "yh"), ("yl", "z", "core")
    lat_count, lon_count = lax.axis_size(lat_axes), lax.axis_size(lon_axes)
    lat, core = lax.axis_index(lat_axes), lax.axis_index("core")
    where = jnp.stack([lat, core, lax.rem(lat, 2)]).astype(jnp.int32)
    smem = pl.BlockSpec(memory_space=pltpu.SMEM)
    vmem = pl.BlockSpec(memory_space=pltpu.VMEM)
    anywhere = pl.BlockSpec(memory_space=pl.ANY)
    cells = slabs * rows * width
    ext = pltpu.VMEM((slabs * (rows + 2), width + 2 * SPAN + 8, chans), jnp.float32)
    taps = pltpu.VMEM((9, cells, chans), jnp.bfloat16)
    params = pltpu.CompilerParams(vmem_limit_bytes=24 * 1024 * 1024)
    grads = (9 * chans, chans)
    swap = [(0, 1), (1, 0)]

    fields = jnp.stack([features, out_grad])
    rows_around = row_halos(fields, lon_count, lat_count)
    own_columns = column_halos([fields], width, lon_count, lat_count)
    ext_rows = pltpu.VMEM((2 * slabs, width + 2 * SPAN + 8, chans), jnp.float32)
    half = slabs * width
    early = pl.pallas_call(
        early_kernel,
        out_shape=[jax.ShapeDtypeStruct((3 * len(OWN), half, chans), jnp.bfloat16)] * 2
        + [jax.ShapeDtypeStruct((cells, chans), jnp.float32)] * 2,
        in_specs=[smem, smem] + [vmem] * 6,
        out_specs=[vmem] * 4,
        scratch_shapes=[ext_rows, ext_rows],
        compiler_params=params,
        name="early",
    )(where, strides, features, out_grad, *own_columns, first_kernel, second_kernel)
    early, rows_around = lax.optimization_barrier((early, rows_around))
    corners = column_halos(ordered(*rows_around), width, lon_count, lat_count)
    edge = pltpu.VMEM((6, half, chans), jnp.bfloat16)
    keep, send, pre_grad = pl.pallas_call(
        main_kernel,
        out_shape=[
            jax.ShapeDtypeStruct(grads, jnp.float32),
            jax.ShapeDtypeStruct(grads, jnp.bfloat16),
            jax.ShapeDtypeStruct(features.shape, jnp.bfloat16),
        ],
        in_specs=[smem, smem] + [vmem] * 10,
        out_specs=[vmem] * 3,
        scratch_shapes=[
            ext_rows,
            ext_rows,
            edge,
            edge,
            pltpu.VMEM((cells, chans), jnp.bfloat16),
        ],
        compiler_params=params,
        name="main",
    )(where, strides, *early, *rows_around, *corners, first_kernel, second_kernel)

    total = keep + lax.ppermute(send, "core", swap).astype(jnp.float32)
    planes, height, cores = lax.axis_size(PLANE), lax.axis_size("z"), lax.axis_size("core")
    total = total.astype(jnp.bfloat16).reshape(planes, 9 * chans // planes, chans)
    spread = lax.all_to_all(total, PLANE, 0, 0, tiled=True)

    spread, pre_grad = lax.optimization_barrier((spread, pre_grad))
    pre_field = pre_grad[None]
    pair, next_pair = row_halos(pre_field, lon_count, lat_count)
    part = jnp.sum(spread.astype(jnp.float32), axis=0)
    reach = 2
    while reach <= height:
        got = lax.ppermute(part, ("z", "core"), folded(height, cores, reach))
        if reach < height:
            part = part + got
        reach *= 2
        if reach == height:
            part, next_pair = lax.optimization_barrier((part, next_pair))
    got, pair = lax.optimization_barrier((got, pair))
    above, below = ordered(pair, next_pair)
    around = (pair, next_pair) + column_halos([above, pre_field, below], width, lon_count, lat_count)
    input_grad = pl.pallas_call(
        back_kernel,
        out_shape=jax.ShapeDtypeStruct(features.shape, jnp.bfloat16),
        in_specs=[smem, smem] + [vmem] * 7,
        out_specs=vmem,
        scratch_shapes=[ext, taps],
        compiler_params=params,
        name="back",
    )(where, strides, out_grad, pre_grad, *around, first_kernel)

    copies = pl.pallas_call(
        copies_kernel,
        out_shape=jax.ShapeDtypeStruct((planes,) + part.shape, jnp.bfloat16),
        in_specs=[vmem] * 2,
        out_specs=vmem,
        compiler_params=params,
        name="copies",
    )(part, got)
    mine = lax.all_to_all(copies, PLANE, 0, 0, tiled=True).reshape(grads)
    mine, input_grad = lax.optimization_barrier((mine, input_grad))
    other = lax.ppermute(mine, "core", swap)
    scale = 1.0 / math.sqrt(cells * lat_count * lon_count)
    wide = [jax.ShapeDtypeStruct(grads, jnp.float32)] * 2
    scratch = [pltpu.VMEM(grads, jnp.float32), pltpu.SemaphoreType.DMA((6,))]
    sides = pl.pallas_call(
        lambda *refs: part_kernel(scale, 0, *refs),
        out_shape=wide,
        in_specs=[smem, vmem],
        out_specs=[anywhere] * 2,
        scratch_shapes=scratch,
        compiler_params=params,
        name="own_part",
    )(where, mine)
    first, second = pl.pallas_call(
        lambda *refs: part_kernel(scale, 1, *refs),
        out_shape=wide,
        in_specs=[smem, vmem, anywhere, anywhere],
        out_specs=[anywhere] * 2,
        scratch_shapes=scratch,
        input_output_aliases={2: 0, 3: 1},
        compiler_params=params,
        name="other_part",
    )(where, other, *sides)
    return input_grad, first.reshape(first_kernel.shape), second.reshape(first_kernel.shape)


def solution(mesh):
    wide = Mesh(mesh.devices.reshape(2, 8, 2, 4, 2), ALL)
    field = P(None, ("x", "yh"), ("yl", "z", "core"), None)
    return jax.shard_map(
        local,
        mesh=wide,
        in_specs=(field, field, P(), P(), P()),
        out_specs=(field, P(), P()),
        check_vma=False,
    )
```

```python
import math

import jax
import jax.numpy as jnp
from jax import lax
from jax.experimental import pallas as pl
from jax.experimental.pallas import tpu as pltpu
from jax.sharding import Mesh
from jax.sharding import PartitionSpec as P

POLE = 16
SPAN = 16
ALL = ("yl", "z", "core", "x", "yh")
PLANE = ("x", "yh", "yl")
NN = (((1,), (0,)), ((), ()))
NT = (((1,), (1,)), ((), ()))
TN = (((0,), (0,)), ((), ()))
ROOT = math.sqrt(2.0 / math.pi)
CUBIC = 0.044715


def dot(a, b, dims):
    return lax.dot_general(a, b, dims, preferred_element_type=jnp.float32)


def fill(ext, field, own, halo, where):
    pair, next_pair, in_chip, next_chip = halo
    width = own.shape[2]
    odd, core = where[2] == 1, where[1] == 1
    for s in range(2):
        for row in range(4):
            place = ext.at[s * 4 + row]
            if row in (0, 3):
                one, other = pair[field, s].astype(jnp.float32), next_pair[field, s].astype(jnp.float32)
                middle = jnp.where(odd, one, other) if row == 0 else jnp.where(odd, other, one)
            else:
                middle = own[s, row - 1].astype(jnp.float32)
            near, far = in_chip[field, s, row].astype(jnp.float32), next_chip[field, s, row].astype(jnp.float32)
            place[:SPAN] = jnp.where(core, near, far)
            place[SPAN : SPAN + width] = middle
            place[SPAN + width : 2 * SPAN + width] = jnp.where(core, far, near)


def tap(ext, s, row, shift, width):
    if isinstance(shift, int):
        return ext[s * 4 + row, SPAN + shift : SPAN + shift + width, :].astype(jnp.bfloat16)
    start = SPAN + shift
    rest = lax.rem(start, 8)
    span = ext[s * 4 + row, pl.ds(pl.multiple_of(start - rest, 8), width + 8), :]
    chans = span.shape[-1]
    turned = pltpu.roll(span.reshape(width // 8 + 1, 8, chans), lax.rem(8 - rest, 8), 1)
    lane = lax.broadcasted_iota(jnp.int32, (1, 8, chans), 1)
    moved = jnp.where(lane < 8 - rest, turned[:-1], turned[1:])
    return moved.reshape(width, chans).astype(jnp.bfloat16)


def adjoint_stride(strides, s, row, slot, lat):
    here = lat * 2 + row
    if slot == 0:
        if row == 1:
            return strides[s, lat * 2, 2]
        return jnp.where(lat == 0, strides[s, 0, 0], strides[s, jnp.maximum(here - 1, 0), 2])
    if slot == 1:
        return strides[s, here, 1]
    return strides[s, jnp.minimum(here + 1, POLE - 1), 0]


def adjoint_taps(ext, taps, strides, lat, width):
    for row in range(2):
        for s in range(2):
            at = (row * 2 + s) * width
            for slot in range(3):
                stride = adjoint_stride(strides, s, row, slot, lat)
                for col in range(3):
                    shift = 0 if col == 1 else -(col - 1) * stride
                    taps[slot * 3 + col, at : at + width] = tap(ext, s, row + slot, shift, width)


def adjoint_product(taps, kernel, mirror, row, half):
    total = None
    at = row * half
    for slot in range(3):
        for col in range(3):
            weight = kernel[2 - slot, col]
            if slot == 0 and row == 0:
                weight = jnp.where(mirror, kernel[0, col], weight)
            term = dot(taps[slot * 3 + col, at : at + half], weight, NT)
            total = term if total is None else total + term
    return total


OWN = ((0, 1), (0, 2), (1, 0), (1, 1))


def stretch(place, middle, near, far, core):
    width = middle.shape[0]
    near, far = near.astype(jnp.float32), far.astype(jnp.float32)
    place[:SPAN] = jnp.where(core, near, far)
    place[SPAN : SPAN + width] = middle.astype(jnp.float32)
    place[SPAN + width : 2 * SPAN + width] = jnp.where(core, far, near)


def moved(ext, at, shift, width):
    return tap(ext, at // 4, at % 4, shift, width)


def early_kernel(where, strides, feat, grad, in_chip, next_chip, first_kernel, second_kernel,
                 taps_f, taps_g, pre_part, back_part, ext_f, ext_g):
    lat, core = where[0], where[1] == 1
    width = feat.shape[2]
    half = 2 * width
    for field, own, ext in ((0, feat, ext_f), (1, grad, ext_g)):
        for s in range(2):
            for row in range(2):
                stretch(ext.at[s * 2 + row], own[s, row], in_chip[field, s, row], next_chip[field, s, row], core)
    for i, (row, k) in enumerate(OWN):
        for s in range(2):
            ahead, behind = strides[s, lat * 2 + row, k], adjoint_stride(strides, s, row, k, lat)
            at, cells = s * 2 + row + k - 1, slice(s * width, (s + 1) * width)
            for col in range(3):
                taps_f[i * 3 + col, cells] = moved(ext_f, at, 0 if col == 1 else (col - 1) * ahead, width)
                taps_g[i * 3 + col, cells] = moved(ext_g, at, 0 if col == 1 else (1 - col) * behind, width)
    for row in range(2):
        pre, back = None, None
        for i, (at, k) in enumerate(OWN):
            if at != row:
                continue
            for col in range(3):
                term = dot(taps_f[i * 3 + col], first_kernel[k, col], NN)
                pre = term if pre is None else pre + term
                term = dot(taps_g[i * 3 + col], second_kernel[2 - k, col], NT)
                back = term if back is None else back + term
        pre_part[row * half : (row + 1) * half] = pre
        back_part[row * half : (row + 1) * half] = back


def main_kernel(where, strides, own_f, own_g, pre_part, back_part, pair, next_pair, in_chip, next_chip,
                first_kernel, second_kernel, pre_grad, act, edge_f, edge_g, ext_f, ext_g):
    lat, core = where[0], where[1]
    odd, second_core = where[2] == 1, core == 1
    mirror = lat == 0
    width = pair.shape[2]
    half = 2 * width
    for field, ext in ((0, ext_f), (1, ext_g)):
        for s in range(2):
            one, other = pair[field, s], next_pair[field, s]
            for row in range(2):
                middle = jnp.where(odd, one, other) if row == 0 else jnp.where(odd, other, one)
                stretch(ext.at[s * 2 + row], middle, in_chip[field, s, row], next_chip[field, s, row], second_core)
    for row in range(2):
        for s in range(2):
            ahead, behind = strides[s, lat * 2 + row, 2 * row], adjoint_stride(strides, s, row, 2 * row, lat)
            cells = slice(s * width, (s + 1) * width)
            for col in range(3):
                edge_f[row * 3 + col, cells] = moved(ext_f, s * 2 + row, 0 if col == 1 else (col - 1) * ahead, width)
                edge_g[row * 3 + col, cells] = moved(ext_g, s * 2 + row, 0 if col == 1 else (1 - col) * behind, width)

    for row in range(2):
        at = slice(row * half, (row + 1) * half)
        pre, back = pre_part[at], back_part[at]
        for col in range(3):
            pre += dot(edge_f[row * 3 + col], first_kernel[2 * row, col], NN)
            weight = second_kernel[2 - 2 * row, col]
            if row == 0:
                weight = jnp.where(mirror, second_kernel[0, col], weight)
            back += dot(edge_g[row * 3 + col], weight, NT)
        square = pre * pre
        bend = jnp.tanh(ROOT * (pre + CUBIC * (pre * square)))
        act[at] = (0.5 * pre * (1.0 + bend)).astype(jnp.bfloat16)
        slope = 0.5 * (1.0 + bend) + 0.5 * pre * (1.0 - bend * bend) * (ROOT * (1.0 + 3.0 * CUBIC * square))
        result = (back * slope).astype(jnp.bfloat16)
        for s in range(2):
            pre_grad[s, row] = result[s * width : (s + 1) * width]


def weight_kernel(owner, where, own_f, own_g, edge_f, edge_g, act, pre_grad, out):
    mirror = where[0] == 0
    half = act.shape[0] // 2

    def taps_of(own, edge, row, k, col):
        return own[OWN.index((row, k)) * 3 + col] if (row, k) in OWN else edge[row * 3 + col]

    def place(value, k, col):
        at = (k * 3 + col) * 256
        out[at : at + 256] = value.astype(out.dtype)

    def second():
        turned = act[...].T
        above, below = turned[:, :half], turned[:, half:]
        for col in range(3):
            edge, upper = (dot(a, taps_of(own_g, edge_g, r, 0, col), NN) for r, a in enumerate((above, below)))
            centre, lower = (
                sum(dot(a, taps_of(own_g, edge_g, r, slot, col), NN) for r, a in enumerate((above, below))) for slot in (1, 2)
            )
            place(centre, 1, col)
            place(lower + jnp.where(mirror, edge, 0.0), 0, col)
            place(upper + jnp.where(mirror, 0.0, edge), 2, col)

    def first():
        rows = [jnp.concatenate([pre_grad[s, row] for s in range(2)], axis=0) for row in range(2)]
        for k in range(3):
            for col in range(3):
                place(sum(dot(taps_of(own_f, edge_f, r, k, col), rows[r], TN) for r in range(2)), k, col)

    pl.when(where[1] == owner)(first)
    pl.when(where[1] != owner)(second)


def back_kernel(where, strides, grad, pre, pair, next_pair, in_chip, next_chip, first_kernel, out, ext, taps):
    lat = where[0]
    mirror = lat == 0
    width = grad.shape[2]
    fill(ext, 0, pre, (pair, next_pair, in_chip, next_chip), where)
    adjoint_taps(ext, taps, strides, lat, width)
    for row in range(2):
        total = adjoint_product(taps, first_kernel, mirror, row, 2 * width)
        for s in range(2):
            own = grad[s, row].astype(jnp.float32)
            out[s, row] = (own + total[s * width : (s + 1) * width]).astype(jnp.bfloat16)


def part_kernel(scale, owner, where, given, *refs):
    first, second, held, sems = refs[-4:]
    count = sems.shape[0]
    step = given.shape[0] // count
    rows = [pl.ds(i * step, step) for i in range(count)]
    to_first = where[1] == owner

    def every(act_on):
        for i, at in enumerate(rows):
            act_on(i, at)

    def write(out):
        def one(i, at):
            held[at] = given[at].astype(jnp.float32) * scale
            pltpu.make_async_copy(held.at[at], out.at[at], sems.at[i]).start()

        every(one)
        every(lambda i, at: pltpu.make_async_copy(held.at[at], out.at[at], sems.at[i]).wait())

    pl.when(to_first)(lambda: write(first))
    pl.when(jnp.logical_not(to_first))(lambda: write(second))


def copies_kernel(part, got, out):
    value = (part[...] + got[...]).astype(jnp.bfloat16)
    for i in range(out.shape[0]):
        out[i] = value


def both_ways(pairs):
    return pairs + [(b, a) for a, b in pairs]


def row_halos(fields, lon_count, lat_count):
    at = lambda lon, lat: (lon % lon_count) * lat_count + lat
    lons = range(lon_count)
    odd = lax.rem(lax.axis_index(("x", "yh")), 2)
    row = lambda i: lax.dynamic_index_in_dim(fields, i, 2, keepdims=False)
    pair = lax.ppermute(row(1 - odd), ALL, both_ways([(at(i, k), at(i, k + 1)) for i in lons for k in range(0, lat_count, 2)]))
    between = both_ways([(at(i, k), at(i, k + 1)) for i in lons for k in range(1, lat_count - 1, 2)])
    across = [(at(i, 0), at(i + lon_count // 2, 0)) for i in lons]
    return pair, lax.ppermute(row(odd), ALL, between + across)


def column_halos(parts, width, lon_count, lat_count):
    at = lambda lon, lat: (lon % lon_count) * lat_count + lat
    core = lax.axis_index("core")

    def edge(start):
        return jnp.concatenate([lax.dynamic_slice_in_dim(a, start, SPAN, 3) for a in parts], axis=2)

    reach = width - SPAN
    places = [(i, k) for i in range(0, lon_count, 2) for k in range(lat_count)]
    next_chip = lax.ppermute(edge(core * reach), ALL, both_ways([(at(i + 1, k), at(i + 2, k)) for i, k in places]))
    in_chip = lax.ppermute(edge((1 - core) * reach), "core", [(0, 1), (1, 0)])
    return in_chip, next_chip


def ordered(pair, next_pair):
    odd = lax.rem(lax.axis_index(("x", "yh")), 2) == 1
    return jnp.where(odd, pair, next_pair)[:, :, None], jnp.where(odd, next_pair, pair)[:, :, None]


def folded(count, cores, reach):
    pairs = []
    for i in range(count):
        for core in range(cores):
            turn = 2 * core
            base = (i + turn) % count
            partner = base ^ (reach - 1 if reach == count else reach // 2)
            pairs.append((i * cores + core, (partner - turn) % count * cores + core))
    return pairs


def local(features, out_grad, first_kernel, second_kernel, strides):
    slabs, rows, width, chans = features.shape
    lat_axes, lon_axes = ("x", "yh"), ("yl", "z", "core")
    lat_count, lon_count = lax.axis_size(lat_axes), lax.axis_size(lon_axes)
    lat, core = lax.axis_index(lat_axes), lax.axis_index("core")
    where = jnp.stack([lat, core, lax.rem(lat, 2)]).astype(jnp.int32)
    smem = pl.BlockSpec(memory_space=pltpu.SMEM)
    vmem = pl.BlockSpec(memory_space=pltpu.VMEM)
    anywhere = pl.BlockSpec(memory_space=pl.ANY)
    cells = slabs * rows * width
    ext = pltpu.VMEM((slabs * (rows + 2), width + 2 * SPAN + 8, chans), jnp.float32)
    taps = pltpu.VMEM((9, cells, chans), jnp.bfloat16)
    params = pltpu.CompilerParams(vmem_limit_bytes=24 * 1024 * 1024)
    grads = (9 * chans, chans)
    swap = [(0, 1), (1, 0)]

    fields = jnp.stack([features, out_grad])
    rows_around = row_halos(fields, lon_count, lat_count)
    own_columns = column_halos([fields], width, lon_count, lat_count)
    ext_rows = pltpu.VMEM((2 * slabs, width + 2 * SPAN + 8, chans), jnp.float32)
    half = slabs * width
    early = pl.pallas_call(
        early_kernel,
        out_shape=[jax.ShapeDtypeStruct((3 * len(OWN), half, chans), jnp.bfloat16)] * 2
        + [jax.ShapeDtypeStruct((cells, chans), jnp.float32)] * 2,
        in_specs=[smem, smem] + [vmem] * 6,
        out_specs=[vmem] * 4,
        scratch_shapes=[ext_rows, ext_rows],
        compiler_params=params,
        name="early",
    )(where, strides, features, out_grad, *own_columns, first_kernel, second_kernel)
    early, rows_around = lax.optimization_barrier((early, rows_around))
    corners = column_halos(ordered(*rows_around), width, lon_count, lat_count)
    edge = jax.ShapeDtypeStruct((6, half, chans), jnp.bfloat16)
    pre_grad, act, *edges = pl.pallas_call(
        main_kernel,
        out_shape=[
            jax.ShapeDtypeStruct(features.shape, jnp.bfloat16),
            jax.ShapeDtypeStruct((cells, chans), jnp.bfloat16),
            edge,
            edge,
        ],
        in_specs=[smem, smem] + [vmem] * 10,
        out_specs=[vmem] * 4,
        scratch_shapes=[ext_rows, ext_rows],
        compiler_params=params,
        name="main",
    )(where, strides, *early, *rows_around, *corners, first_kernel, second_kernel)

    def weights(owner, kind, name):
        return pl.pallas_call(
            lambda *refs: weight_kernel(owner, *refs),
            out_shape=jax.ShapeDtypeStruct(grads, kind),
            in_specs=[smem] + [vmem] * 6,
            out_specs=vmem,
            compiler_params=params,
            name=name,
        )(where, *early[:2], *edges, act, pre_grad)

    send, keep = weights(1, jnp.bfloat16, "sent"), weights(0, jnp.float32, "kept")

    total = keep + lax.ppermute(send, "core", swap).astype(jnp.float32)
    planes, height, cores = lax.axis_size(PLANE), lax.axis_size("z"), lax.axis_size("core")
    total = total.astype(jnp.bfloat16).reshape(planes, 9 * chans // planes, chans)
    spread = lax.all_to_all(total, PLANE, 0, 0, tiled=True)

    spread, pre_grad = lax.optimization_barrier((spread, pre_grad))
    pre_field = pre_grad[None]
    pair, next_pair = row_halos(pre_field, lon_count, lat_count)
    part = jnp.sum(spread.astype(jnp.float32), axis=0)
    reach = 2
    while reach <= height:
        got = lax.ppermute(part, ("z", "core"), folded(height, cores, reach))
        if reach < height:
            part = part + got
        reach *= 2
        if reach == height:
            part, pair = lax.optimization_barrier((part, pair))
    got, next_pair = lax.optimization_barrier((got, next_pair))
    above, below = ordered(pair, next_pair)
    around = (pair, next_pair) + column_halos([above, pre_field, below], width, lon_count, lat_count)
    input_grad = pl.pallas_call(
        back_kernel,
        out_shape=jax.ShapeDtypeStruct(features.shape, jnp.bfloat16),
        in_specs=[smem, smem] + [vmem] * 7,
        out_specs=vmem,
        scratch_shapes=[ext, taps],
        compiler_params=params,
        name="back",
    )(where, strides, out_grad, pre_grad, *around, first_kernel)

    copies = pl.pallas_call(
        copies_kernel,
        out_shape=jax.ShapeDtypeStruct((planes,) + part.shape, jnp.bfloat16),
        in_specs=[vmem] * 2,
        out_specs=vmem,
        compiler_params=params,
        name="copies",
    )(part, got)
    mine = lax.all_to_all(copies, PLANE, 0, 0, tiled=True).reshape(grads)
    mine, input_grad = lax.optimization_barrier((mine, input_grad))
    other = lax.ppermute(mine, "core", swap)
    scale = 1.0 / math.sqrt(cells * lat_count * lon_count)
    wide = [jax.ShapeDtypeStruct(grads, jnp.float32)] * 2
    scratch = [pltpu.VMEM(grads, jnp.float32), pltpu.SemaphoreType.DMA((6,))]
    sides = pl.pallas_call(
        lambda *refs: part_kernel(scale, 0, *refs),
        out_shape=wide,
        in_specs=[smem, vmem],
        out_specs=[anywhere] * 2,
        scratch_shapes=scratch,
        compiler_params=params,
        name="own_part",
    )(where, mine)
    first, second = pl.pallas_call(
        lambda *refs: part_kernel(scale, 1, *refs),
        out_shape=wide,
        in_specs=[smem, vmem, anywhere, anywhere],
        out_specs=[anywhere] * 2,
        scratch_shapes=scratch,
        input_output_aliases={2: 0, 3: 1},
        compiler_params=params,
        name="other_part",
    )(where, other, *sides)
    return input_grad, first.reshape(first_kernel.shape), second.reshape(first_kernel.shape)


def solution(mesh):
    wide = Mesh(mesh.devices.reshape(2, 8, 2, 4, 2), ALL)
    field = P(None, ("x", "yh"), ("yl", "z", "core"), None)
    return jax.shard_map(
        local,
        mesh=wide,
        in_specs=(field, field, P(), P(), P()),
        out_specs=(field, P(), P()),
        check_vma=False,
    )
```

```python
import math

import jax
import jax.numpy as jnp
from jax import lax
from jax.experimental import pallas as pl
from jax.experimental.pallas import tpu as pltpu
from jax.sharding import Mesh
from jax.sharding import PartitionSpec as P

POLE = 16
SPAN = 16
ALL = ("yl", "z", "core", "x", "yh")
PLANE = ("x", "yh", "yl")
NN = (((1,), (0,)), ((), ()))
NT = (((1,), (1,)), ((), ()))
TN = (((0,), (0,)), ((), ()))
ROOT = math.sqrt(2.0 / math.pi)
CUBIC = 0.044715


def dot(a, b, dims):
    return lax.dot_general(a, b, dims, preferred_element_type=jnp.float32)


def fill(ext, field, own, halo, where):
    pair, next_pair, in_chip, next_chip = halo
    width = own.shape[2]
    odd, core = where[2] == 1, where[1] == 1
    for s in range(2):
        for row in range(4):
            place = ext.at[s * 4 + row]
            if row in (0, 3):
                one, other = pair[field, s].astype(jnp.float32), next_pair[field, s].astype(jnp.float32)
                middle = jnp.where(odd, one, other) if row == 0 else jnp.where(odd, other, one)
            else:
                middle = own[s, row - 1].astype(jnp.float32)
            near, far = in_chip[field, s, row].astype(jnp.float32), next_chip[field, s, row].astype(jnp.float32)
            place[:SPAN] = jnp.where(core, near, far)
            place[SPAN : SPAN + width] = middle
            place[SPAN + width : 2 * SPAN + width] = jnp.where(core, far, near)


def tap(ext, s, row, shift, width):
    if isinstance(shift, int):
        return ext[s * 4 + row, SPAN + shift : SPAN + shift + width, :].astype(jnp.bfloat16)
    start = SPAN + shift
    rest = lax.rem(start, 8)
    span = ext[s * 4 + row, pl.ds(pl.multiple_of(start - rest, 8), width + 8), :]
    chans = span.shape[-1]
    turned = pltpu.roll(span.reshape(width // 8 + 1, 8, chans), lax.rem(8 - rest, 8), 1)
    lane = lax.broadcasted_iota(jnp.int32, (1, 8, chans), 1)
    moved = jnp.where(lane < 8 - rest, turned[:-1], turned[1:])
    return moved.reshape(width, chans).astype(jnp.bfloat16)


def adjoint_stride(strides, s, row, slot, lat):
    here = lat * 2 + row
    if slot == 0:
        if row == 1:
            return strides[s, lat * 2, 2]
        return jnp.where(lat == 0, strides[s, 0, 0], strides[s, jnp.maximum(here - 1, 0), 2])
    if slot == 1:
        return strides[s, here, 1]
    return strides[s, jnp.minimum(here + 1, POLE - 1), 0]


def adjoint_taps(ext, taps, strides, lat, width):
    for row in range(2):
        for s in range(2):
            at = (row * 2 + s) * width
            for slot in range(3):
                stride = adjoint_stride(strides, s, row, slot, lat)
                for col in range(3):
                    shift = 0 if col == 1 else -(col - 1) * stride
                    taps[slot * 3 + col, at : at + width] = tap(ext, s, row + slot, shift, width)


def adjoint_product(taps, kernel, mirror, row, half):
    total = None
    at = row * half
    for slot in range(3):
        for col in range(3):
            weight = kernel[2 - slot, col]
            if slot == 0 and row == 0:
                weight = jnp.where(mirror, kernel[0, col], weight)
            term = dot(taps[slot * 3 + col, at : at + half], weight, NT)
            total = term if total is None else total + term
    return total


OWN = ((0, 1), (0, 2), (1, 0), (1, 1))


def stretch(place, middle, near, far, core):
    width = middle.shape[0]
    near, far = near.astype(jnp.float32), far.astype(jnp.float32)
    place[:SPAN] = jnp.where(core, near, far)
    place[SPAN : SPAN + width] = middle.astype(jnp.float32)
    place[SPAN + width : 2 * SPAN + width] = jnp.where(core, far, near)


def moved(ext, at, shift, width):
    return tap(ext, at // 4, at % 4, shift, width)


def early_kernel(where, strides, feat, grad, in_chip, next_chip, first_kernel, second_kernel,
                 taps_f, taps_g, pre_part, back_part, ext_f, ext_g):
    lat, core = where[0], where[1] == 1
    width = feat.shape[2]
    half = 2 * width
    for field, own, ext in ((0, feat, ext_f), (1, grad, ext_g)):
        for s in range(2):
            for row in range(2):
                stretch(ext.at[s * 2 + row], own[s, row], in_chip[field, s, row], next_chip[field, s, row], core)
    for i, (row, k) in enumerate(OWN):
        for s in range(2):
            ahead, behind = strides[s, lat * 2 + row, k], adjoint_stride(strides, s, row, k, lat)
            at, cells = s * 2 + row + k - 1, slice(s * width, (s + 1) * width)
            for col in range(3):
                taps_f[i * 3 + col, cells] = moved(ext_f, at, 0 if col == 1 else (col - 1) * ahead, width)
                taps_g[i * 3 + col, cells] = moved(ext_g, at, 0 if col == 1 else (1 - col) * behind, width)
    for row in range(2):
        pre, back = None, None
        for i, (at, k) in enumerate(OWN):
            if at != row:
                continue
            for col in range(3):
                term = dot(taps_f[i * 3 + col], first_kernel[k, col], NN)
                pre = term if pre is None else pre + term
                term = dot(taps_g[i * 3 + col], second_kernel[2 - k, col], NT)
                back = term if back is None else back + term
        pre_part[row * half : (row + 1) * half] = pre
        back_part[row * half : (row + 1) * half] = back


def main_kernel(where, strides, own_f, own_g, pre_part, back_part, pair, next_pair, in_chip, next_chip,
                first_kernel, second_kernel, keep, send, pre_grad, ext_f, ext_g, edge_f, edge_g, act):
    lat, core = where[0], where[1]
    odd, second_core = where[2] == 1, core == 1
    mirror = lat == 0
    width = pair.shape[2]
    half = 2 * width
    for field, ext in ((0, ext_f), (1, ext_g)):
        for s in range(2):
            one, other = pair[field, s], next_pair[field, s]
            for row in range(2):
                middle = jnp.where(odd, one, other) if row == 0 else jnp.where(odd, other, one)
                stretch(ext.at[s * 2 + row], middle, in_chip[field, s, row], next_chip[field, s, row], second_core)
    for row in range(2):
        for s in range(2):
            ahead, behind = strides[s, lat * 2 + row, 2 * row], adjoint_stride(strides, s, row, 2 * row, lat)
            cells = slice(s * width, (s + 1) * width)
            for col in range(3):
                edge_f[row * 3 + col, cells] = moved(ext_f, s * 2 + row, 0 if col == 1 else (col - 1) * ahead, width)
                edge_g[row * 3 + col, cells] = moved(ext_g, s * 2 + row, 0 if col == 1 else (1 - col) * behind, width)

    for row in range(2):
        at = slice(row * half, (row + 1) * half)
        pre, back = pre_part[at], back_part[at]
        for col in range(3):
            pre += dot(edge_f[row * 3 + col], first_kernel[2 * row, col], NN)
            weight = second_kernel[2 - 2 * row, col]
            if row == 0:
                weight = jnp.where(mirror, second_kernel[0, col], weight)
            back += dot(edge_g[row * 3 + col], weight, NT)
        square = pre * pre
        bend = jnp.tanh(ROOT * (pre + CUBIC * (pre * square)))
        act[at] = (0.5 * pre * (1.0 + bend)).astype(jnp.bfloat16)
        slope = 0.5 * (1.0 + bend) + 0.5 * pre * (1.0 - bend * bend) * (ROOT * (1.0 + 3.0 * CUBIC * square))
        result = (back * slope).astype(jnp.bfloat16)
        for s in range(2):
            pre_grad[s, row] = result[s * width : (s + 1) * width]

    def taps_of(own, edge, row, k, col):
        return own[OWN.index((row, k)) * 3 + col] if (row, k) in OWN else edge[row * 3 + col]

    rows = [jnp.concatenate([pre_grad[s, row] for s in range(2)], axis=0) for row in range(2)]

    def products(first, second):
        def place(out, value, k, col):
            at = (k * 3 + col) * 256
            out[at : at + 256] = value.astype(out.dtype)

        turned = act[...].T
        above, below = turned[:, :half], turned[:, half:]
        for col in range(3):
            edge, upper = (dot(a, taps_of(own_g, edge_g, r, 0, col), NN) for r, a in enumerate((above, below)))
            centre, lower = (
                sum(dot(a, taps_of(own_g, edge_g, r, slot, col), NN) for r, a in enumerate((above, below))) for slot in (1, 2)
            )
            place(second, centre, 1, col)
            place(second, lower + jnp.where(mirror, edge, 0.0), 0, col)
            place(second, upper + jnp.where(mirror, 0.0, edge), 2, col)
        for k in range(3):
            for col in range(3):
                place(first, sum(dot(taps_of(own_f, edge_f, r, k, col), rows[r], TN) for r in range(2)), k, col)

    pl.when(core == 0)(lambda: products(keep, send))
    pl.when(core != 0)(lambda: products(send, keep))


def back_kernel(where, strides, grad, pre, pair, next_pair, in_chip, next_chip, first_kernel, out, ext, taps):
    lat = where[0]
    mirror = lat == 0
    width = grad.shape[2]
    fill(ext, 0, pre, (pair, next_pair, in_chip, next_chip), where)
    adjoint_taps(ext, taps, strides, lat, width)
    for row in range(2):
        total = adjoint_product(taps, first_kernel, mirror, row, 2 * width)
        for s in range(2):
            own = grad[s, row].astype(jnp.float32)
            out[s, row] = (own + total[s * width : (s + 1) * width]).astype(jnp.bfloat16)


def part_kernel(scale, owner, where, given, *refs):
    first, second, held, sems = refs[-4:]
    count = sems.shape[0]
    step = given.shape[0] // count
    rows = [pl.ds(i * step, step) for i in range(count)]
    to_first = where[1] == owner

    def every(act_on):
        for i, at in enumerate(rows):
            act_on(i, at)

    def write(out):
        def one(i, at):
            held[at] = given[at].astype(jnp.float32) * scale
            pltpu.make_async_copy(held.at[at], out.at[at], sems.at[i]).start()

        every(one)
        every(lambda i, at: pltpu.make_async_copy(held.at[at], out.at[at], sems.at[i]).wait())

    pl.when(to_first)(lambda: write(first))
    pl.when(jnp.logical_not(to_first))(lambda: write(second))


def copies_kernel(part, got, out):
    value = (part[...] + got[...]).astype(jnp.bfloat16)
    for i in range(out.shape[0]):
        out[i] = value


def both_ways(pairs):
    return pairs + [(b, a) for a, b in pairs]


def row_halos(fields, lon_count, lat_count):
    at = lambda lon, lat: (lon % lon_count) * lat_count + lat
    lons = range(lon_count)
    odd = lax.rem(lax.axis_index(("x", "yh")), 2)
    row = lambda i: lax.dynamic_index_in_dim(fields, i, 2, keepdims=False)
    pair = lax.ppermute(row(1 - odd), ALL, both_ways([(at(i, k), at(i, k + 1)) for i in lons for k in range(0, lat_count, 2)]))
    between = both_ways([(at(i, k), at(i, k + 1)) for i in lons for k in range(1, lat_count - 1, 2)])
    across = [(at(i, 0), at(i + lon_count // 2, 0)) for i in lons]
    return pair, lax.ppermute(row(odd), ALL, between + across)


def column_halos(parts, width, lon_count, lat_count):
    at = lambda lon, lat: (lon % lon_count) * lat_count + lat
    core = lax.axis_index("core")

    def edge(start):
        return jnp.concatenate([lax.dynamic_slice_in_dim(a, start, SPAN, 3) for a in parts], axis=2)

    reach = width - SPAN
    places = [(i, k) for i in range(0, lon_count, 2) for k in range(lat_count)]
    next_chip = lax.ppermute(edge(core * reach), ALL, both_ways([(at(i + 1, k), at(i + 2, k)) for i, k in places]))
    in_chip = lax.ppermute(edge((1 - core) * reach), "core", [(0, 1), (1, 0)])
    return in_chip, next_chip


def ordered(pair, next_pair):
    odd = lax.rem(lax.axis_index(("x", "yh")), 2) == 1
    return jnp.where(odd, pair, next_pair)[:, :, None], jnp.where(odd, next_pair, pair)[:, :, None]


def folded(count, cores, reach):
    pairs = []
    for i in range(count):
        for core in range(cores):
            turn = 2 * core
            base = (i + turn) % count
            partner = base ^ (reach - 1 if reach == count else reach // 2)
            pairs.append((i * cores + core, (partner - turn) % count * cores + core))
    return pairs


def local(features, out_grad, first_kernel, second_kernel, strides):
    slabs, rows, width, chans = features.shape
    lat_axes, lon_axes = ("x", "yh"), ("yl", "z", "core")
    lat_count, lon_count = lax.axis_size(lat_axes), lax.axis_size(lon_axes)
    lat, core = lax.axis_index(lat_axes), lax.axis_index("core")
    where = jnp.stack([lat, core, lax.rem(lat, 2)]).astype(jnp.int32)
    smem = pl.BlockSpec(memory_space=pltpu.SMEM)
    vmem = pl.BlockSpec(memory_space=pltpu.VMEM)
    anywhere = pl.BlockSpec(memory_space=pl.ANY)
    cells = slabs * rows * width
    ext = pltpu.VMEM((slabs * (rows + 2), width + 2 * SPAN + 8, chans), jnp.float32)
    taps = pltpu.VMEM((9, cells, chans), jnp.bfloat16)
    params = pltpu.CompilerParams(vmem_limit_bytes=24 * 1024 * 1024)
    grads = (9 * chans, chans)
    swap = [(0, 1), (1, 0)]

    fields = jnp.stack([features, out_grad])
    rows_around = row_halos(fields, lon_count, lat_count)
    own_columns = column_halos([fields], width, lon_count, lat_count)
    ext_rows = pltpu.VMEM((2 * slabs, width + 2 * SPAN + 8, chans), jnp.float32)
    half = slabs * width
    early = pl.pallas_call(
        early_kernel,
        out_shape=[jax.ShapeDtypeStruct((3 * len(OWN), half, chans), jnp.bfloat16)] * 2
        + [jax.ShapeDtypeStruct((cells, chans), jnp.float32)] * 2,
        in_specs=[smem, smem] + [vmem] * 6,
        out_specs=[vmem] * 4,
        scratch_shapes=[ext_rows, ext_rows],
        compiler_params=params,
        name="early",
    )(where, strides, features, out_grad, *own_columns, first_kernel, second_kernel)
    early, rows_around = lax.optimization_barrier((early, rows_around))
    corners = column_halos(ordered(*rows_around), width, lon_count, lat_count)
    edge = pltpu.VMEM((6, half, chans), jnp.bfloat16)
    keep, send, pre_grad = pl.pallas_call(
        main_kernel,
        out_shape=[
            jax.ShapeDtypeStruct(grads, jnp.float32),
            jax.ShapeDtypeStruct(grads, jnp.bfloat16),
            jax.ShapeDtypeStruct(features.shape, jnp.bfloat16),
        ],
        in_specs=[smem, smem] + [vmem] * 10,
        out_specs=[vmem] * 3,
        scratch_shapes=[
            ext_rows,
            ext_rows,
            edge,
            edge,
            pltpu.VMEM((cells, chans), jnp.bfloat16),
        ],
        compiler_params=params,
        name="main",
    )(where, strides, *early, *rows_around, *corners, first_kernel, second_kernel)

    total = keep + lax.ppermute(send, "core", swap).astype(jnp.float32)
    planes, height, cores = lax.axis_size(PLANE), lax.axis_size("z"), lax.axis_size("core")
    total = total.astype(jnp.bfloat16).reshape(planes, 9 * chans // planes, chans)
    spread = lax.all_to_all(total, PLANE, 0, 0, tiled=True)

    spread, pre_grad = lax.optimization_barrier((spread, pre_grad))
    pre_field = pre_grad[None]
    pair, next_pair = row_halos(pre_field, lon_count, lat_count)
    part = jnp.sum(spread.astype(jnp.float32), axis=0)
    reach = 2
    while reach <= height:
        got = lax.ppermute(part, ("z", "core"), folded(height, cores, reach))
        if reach < height:
            part = part + got
        reach *= 2
        if reach == height // 2:
            part, pair = lax.optimization_barrier((part, pair))
    got, next_pair = lax.optimization_barrier((got, next_pair))
    above, below = ordered(pair, next_pair)
    around = (pair, next_pair) + column_halos([above, pre_field, below], width, lon_count, lat_count)
    input_grad = pl.pallas_call(
        back_kernel,
        out_shape=jax.ShapeDtypeStruct(features.shape, jnp.bfloat16),
        in_specs=[smem, smem] + [vmem] * 7,
        out_specs=vmem,
        scratch_shapes=[ext, taps],
        compiler_params=params,
        name="back",
    )(where, strides, out_grad, pre_grad, *around, first_kernel)

    copies = pl.pallas_call(
        copies_kernel,
        out_shape=jax.ShapeDtypeStruct((planes,) + part.shape, jnp.bfloat16),
        in_specs=[vmem] * 2,
        out_specs=vmem,
        compiler_params=params,
        name="copies",
    )(part, got)
    mine = lax.all_to_all(copies, PLANE, 0, 0, tiled=True).reshape(grads)
    mine, input_grad = lax.optimization_barrier((mine, input_grad))
    other = lax.ppermute(mine, "core", swap)
    scale = 1.0 / math.sqrt(cells * lat_count * lon_count)
    wide = [jax.ShapeDtypeStruct(grads, jnp.float32)] * 2
    scratch = [pltpu.VMEM(grads, jnp.float32), pltpu.SemaphoreType.DMA((6,))]
    sides = pl.pallas_call(
        lambda *refs: part_kernel(scale, 0, *refs),
        out_shape=wide,
        in_specs=[smem, vmem],
        out_specs=[anywhere] * 2,
        scratch_shapes=scratch,
        compiler_params=params,
        name="own_part",
    )(where, mine)
    first, second = pl.pallas_call(
        lambda *refs: part_kernel(scale, 1, *refs),
        out_shape=wide,
        in_specs=[smem, vmem, anywhere, anywhere],
        out_specs=[anywhere] * 2,
        scratch_shapes=scratch,
        input_output_aliases={2: 0, 3: 1},
        compiler_params=params,
        name="other_part",
    )(where, other, *sides)
    return input_grad, first.reshape(first_kernel.shape), second.reshape(first_kernel.shape)


def solution(mesh):
    wide = Mesh(mesh.devices.reshape(2, 8, 2, 4, 2), ALL)
    field = P(None, ("x", "yh"), ("yl", "z", "core"), None)
    return jax.shard_map(
        local,
        mesh=wide,
        in_specs=(field, field, P(), P(), P()),
        out_specs=(field, P(), P()),
        check_vma=False,
    )
```
